32 devices in a mesh: group: 4 (over y, x), chan: 8 (over z, core).
Axes of the slice: x: 2, y: 2, z: 4, core: 2. Of those that a mesh axis runs over, the one named last changes fastest.
Arguments:
- hidden_in: bfloat16 [8192, 768], P(('group', 'chan')), may hold values from -6 to 6
- mix_gain: float32 [768], replicated, may hold values from 0.5 to 1.5
- mix_shift: float32 [768], replicated, may hold values from -4 to 4
- w_query: bfloat16 [768, 768], P(None, 'chan'), may hold values from -0.21875 to 0.21875
- bias_query: float32 [768], P('chan'), may hold values from -4 to 4
- w_key: bfloat16 [768, 768], P(None, 'chan'), may hold values from -0.21875 to 0.21875
- bias_key: float32 [768], P('chan'), may hold values from -4 to 4
- w_value: bfloat16 [768, 768], P(None, 'chan'), may hold values from -0.21875 to 0.21875
- bias_value: float32 [768], P('chan'), may hold values from -4 to 4
- shift_taps: float32 [768, 4], P('chan'), may hold values from -3 to 3
- log_step: float32 [768], P('chan'), may hold values from -6.9 to -2.3
- log_decay: float32 [768, 32], P('chan'), may hold values from -1.6 to 0
- frequency: float32 [768, 32], P('chan'), may hold values from 0 to 30
- out_real: float32 [768, 32], P('chan'), may hold values from -6 to 6
- out_imag: float32 [768, 32], P('chan'), may hold values from -6 to 6
- skip_gain: float32 [768], P('chan'), may hold values from -6 to 6
- w_out: bfloat16 [768, 768], P('chan'), may hold values from -0.21875 to 0.21875
- bias_out: float32 [768], replicated, may hold values from -4 to 4
- mlp_gain: float32 [768], replicated, may hold values from 0.5 to 1.5
- mlp_shift: float32 [768], replicated, may hold values from -4 to 4
- w_up: bfloat16 [768, 3072], P(None, 'chan'), may hold values from -0.21875 to 0.21875
- bias_up: float32 [3072], P('chan'), may hold values from -4 to 4
- w_down: bfloat16 [3072, 768], P('chan'), may hold values from -0.109375 to 0.109375
- bias_down: float32 [768], replicated, may hold values from -4 to 4
- cotangent: bfloat16 [8192, 768], P(('group', 'chan')), may hold values from -6 to 6
- seq_blocks: int32 [4, 3], P('group'), may hold values from 0 to 16, as said below
Outputs:
- output: bfloat16 [8192, 768], P(('group', 'chan'))
- grad_input: bfloat16 [8192, 768], P(('group', 'chan'))
- grad_mix_gain: float32 [768], P('chan')
- grad_mix_shift: float32 [768], P('chan')
- grad_w_query: float32 [768, 768], P(None, 'chan')
- grad_bias_query: float32 [768], P('chan')
- grad_w_key: float32 [768, 768], P(None, 'chan')
- grad_bias_key: float32 [768], P('chan')
- grad_w_value: float32 [768, 768], P(None, 'chan')
- grad_bias_value: float32 [768], P('chan')
- grad_shift_taps: float32 [768, 4], P('chan')
- grad_log_step: float32 [768], P('chan')
- grad_log_decay: float32 [768, 32], P('chan')
- grad_frequency: float32 [768, 32], P('chan')
- grad_out_real: float32 [768, 32], P('chan')
- grad_out_imag: float32 [768, 32], P('chan')
- grad_skip_gain: float32 [768], P('chan')
- grad_w_out: float32 [768, 768], P('chan')
- grad_bias_out: float32 [768], P('chan')
- grad_mlp_gain: float32 [768], P('chan')
- grad_mlp_shift: float32 [768], P('chan')
- grad_w_up: float32 [768, 3072], P(None, 'chan')
- grad_bias_up: float32 [3072], P('chan')
- grad_w_down: float32 [3072, 768], P('chan')
- grad_bias_down: float32 [768], P('chan')
The draws below stay inside these ranges and needn't reach their ends.
Inputs may be any that keep to these rules, and one draw needn't show every extreme that they name: `seq_blocks`: row g holds the lengths, in blocks of 128 rows and in order, of the three sequences that fill group g; they sum to 16, the first and the last are 0 or 1.
All inputs are finite; a program needn't handle non-finite values.
Results may differ from the reference program's by a relative error of at most 0.0087.
Values may be sent and summed in bfloat16 or wider, within the bound.
No kernel may reach another device: no remote copies, remote signals or barrier semaphores. Data moves between devices by JAX's collectives and lax.ppermute only.
A program may use at most 256 MiB of HBM per device.

```python
import jax
import jax.numpy as jnp
from jax import lax

D = 768
FF = 3072
MODES = 32
SHIFT = 4
STRETCH = 128
GROUPS = 4
GROUP_TOK = 2048
TOKENS = 8192


def draw_seq_blocks(key, part):
    key = jax.random.fold_in(key, 11)
    head_key, tail_key, pick_key = jax.random.split(key, 3)
    head = jax.random.randint(head_key, (GROUPS,), 0, 2, dtype=jnp.int32)
    tail = jax.random.randint(tail_key, (GROUPS,), 0, 2, dtype=jnp.int32)
    chosen = jax.random.randint(pick_key, (), 0, GROUPS, dtype=jnp.int32)
    whole = jnp.arange(GROUPS, dtype=jnp.int32) == chosen
    head = jnp.where(whole, 0, head)
    tail = jnp.where(whole, 0, tail)
    middle = GROUP_TOK // STRETCH - head - tail
    return jnp.stack([head, middle, tail], axis=1).astype(jnp.int32)


def shard_levels(stream_key, extent, cuts, low, high):
    loudness, own = 1.0, jax.random.fold_in(stream_key, 6)
    for position, blocks in cuts:
        heights = jnp.exp(jax.random.uniform(jax.random.fold_in(own, position), (blocks,), jnp.float32, low / len(cuts), high / len(cuts)))
        loudness = loudness * jnp.repeat(heights, extent[position] // blocks).reshape([-1 if axis == position else 1 for axis in range(len(extent))])
    return loudness


def noise(own_key, extent, scale, most, pieces=(), kind=jnp.bfloat16):
    array = jax.random.normal(own_key, extent, jnp.float32) * scale
    if len(pieces) > 0:
        array = shard_levels(own_key, extent, pieces, -0.22, 0.18) * array
    return jnp.clip(array, min=-most, max=most).astype(kind)


def setup_inputs(seed: int = 0) -> dict:
    key_list = jax.random.split(jax.random.key(seed), 27)
    hidden_in = noise(key_list[0], (TOKENS, D), 1.0, 6.0, ((0, 32),))
    mix_gain = jnp.clip(1.0 + 0.1 * jax.random.normal(key_list[1], (D,), jnp.float32), 0.5, 1.5)
    mix_shift = noise(key_list[2], (D,), 0.3, 4.0, (), jnp.float32)
    w_query = noise(key_list[3], (D, D), D ** -0.5, 0.21875, ((1, 8),))
    bias_query = noise(key_list[4], (D,), 0.3, 4.0, ((0, 8),), jnp.float32)
    w_key = noise(key_list[5], (D, D), D ** -0.5, 0.21875, ((1, 8),))
    bias_key = noise(key_list[6], (D,), 0.3, 4.0, ((0, 8),), jnp.float32)
    w_value = noise(key_list[7], (D, D), D ** -0.5, 0.21875, ((1, 8),))
    bias_value = noise(key_list[8], (D,), 0.3, 4.0, ((0, 8),), jnp.float32)
    shift_taps = noise(key_list[9], (D, SHIFT), SHIFT ** -0.5, 3.0, ((0, 8),), jnp.float32)
    log_step = jnp.clip(-6.9 + 4.6000001430511475 * jax.random.uniform(key_list[10], (D,), jnp.float32) ** shard_levels(key_list[10], (D,), ((0, 8),), -0.2, 0.2), -6.9, -2.3)
    log_decay = jnp.clip(-1.6 + 1.6 * jax.random.uniform(key_list[11], (D, MODES), jnp.float32) ** shard_levels(key_list[11], (D, MODES), ((0, 8),), -0.2, 0.2), -1.6, 0.0)
    frequency = jnp.clip(30.0 * jax.random.uniform(key_list[12], (D, MODES), jnp.float32) ** shard_levels(key_list[12], (D, MODES), ((0, 8),), -0.2, 0.2), 0.0, 30.0)
    out_real = noise(key_list[13], (D, MODES), 1.0, 6.0, ((0, 8),), jnp.float32)
    out_imag = noise(key_list[14], (D, MODES), 1.0, 6.0, ((0, 8),), jnp.float32)
    skip_gain = noise(key_list[15], (D,), 1.0, 6.0, ((0, 8),), jnp.float32)
    w_out = noise(key_list[16], (D, D), D ** -0.5, 0.21875, ((0, 8),))
    bias_out = noise(key_list[17], (D,), 0.3, 4.0, (), jnp.float32)
    mlp_gain = jnp.clip(1.0 + 0.1 * jax.random.normal(key_list[18], (D,), jnp.float32), 0.5, 1.5)
    mlp_shift = noise(key_list[19], (D,), 0.3, 4.0, (), jnp.float32)
    w_up = noise(key_list[20], (D, FF), D ** -0.5, 0.21875, ((1, 8),))
    bias_up = noise(key_list[21], (FF,), 0.3, 4.0, ((0, 8),), jnp.float32)
    w_down = noise(key_list[22], (FF, D), FF ** -0.5, 0.109375, ((0, 8),))
    bias_down = noise(key_list[23], (D,), 0.3, 4.0, (), jnp.float32)
    cotangent = noise(key_list[24], (TOKENS, D), 1.0, 6.0, ((0, 32),))
    seq_blocks = draw_seq_blocks(jax.random.fold_in(key_list[26], 71), 0)
    return {"hidden_in": hidden_in, "mix_gain": mix_gain, "mix_shift": mix_shift, "w_query": w_query, "bias_query": bias_query, "w_key": w_key, "bias_key": bias_key, "w_value": w_value, "bias_value": bias_value, "shift_taps": shift_taps, "log_step": log_step, "log_decay": log_decay, "frequency": frequency, "out_real": out_real, "out_imag": out_imag, "skip_gain": skip_gain, "w_out": w_out, "bias_out": bias_out, "mlp_gain": mlp_gain, "mlp_shift": mlp_shift, "w_up": w_up, "bias_up": bias_up, "w_down": w_down, "bias_down": bias_down, "cotangent": cotangent, "seq_blocks": seq_blocks}


@jax.custom_vjp
def low(v):
    return lax.optimization_barrier(v.astype(jnp.bfloat16)).astype(jnp.float32)

@jax.custom_vjp
def low_back(v):
    return v

def low_keep(v):
    return (low(v), None)

def low_pass(kept, grad):
    return (grad,)

def back_keep(v):
    return (v, None)

def back_low(kept, grad):
    return (low(grad),)
low.defvjp(low_keep, low_pass)
low_back.defvjp(back_keep, back_low)
epsilon = 1e-05
exact_precision = lax.Precision.HIGHEST

def matmul(left, right):
    return jnp.dot(left, right, precision=exact_precision, preferred_element_type=jnp.float32)

def layer_norm(values, gain, shift):
    center = values - lax.optimization_barrier(jnp.mean(values, axis=-1, keepdims=True))
    spread = lax.optimization_barrier(jnp.mean(center * center, axis=-1, keepdims=True))
    return center * lax.rsqrt(spread + epsilon) * gain + shift

def gelu_tanh(values):
    return jax.nn.gelu(values, approximate=True)

def ssm_tables(log_step, log_decay, frequency, out_real, out_imag):
    step_size = jnp.exp(log_step)[:, None]
    rate = -jnp.exp(log_decay)
    decay = rate * step_size
    turn = frequency * step_size
    growth = jnp.exp(decay)
    ratio_re = growth * jnp.cos(turn) - 1.0
    ratio_im = growth * jnp.sin(turn)
    denom = rate * rate + frequency * frequency
    scaled_re = (ratio_re * rate + ratio_im * frequency) / denom
    scaled_im = (ratio_im * rate - ratio_re * frequency) / denom
    weight_re = out_real * scaled_re - out_imag * scaled_im
    weight_im = out_real * scaled_im + out_imag * scaled_re
    return (decay, turn, weight_re, weight_im)

def ssm_kernel(log_step, log_decay, frequency, out_real, out_imag, span):
    decay, turn, weight_re, weight_im = ssm_tables(log_step, log_decay, frequency, out_real, out_imag)
    times = jnp.arange(span, dtype=jnp.float32)
    magnitude = jnp.exp(decay[:, :, None] * times)
    angle = turn[:, :, None] * times
    terms = weight_re[:, :, None] * jnp.cos(angle) - weight_im[:, :, None] * jnp.sin(angle)
    return 2.0 * lax.optimization_barrier(jnp.sum(magnitude * terms, axis=1))

def causal_conv(product, kernel):
    total = product.shape[0]
    padded = 2 * total
    spectrum = jnp.fft.rfft(product, n=padded, axis=0)
    response = jnp.fft.rfft(kernel.T, n=padded, axis=0)
    return jnp.fft.irfft(spectrum * response, n=padded, axis=0)[:total]

def segments_of(lengths):
    rows = jnp.arange(GROUP_TOK, dtype=jnp.int32)
    block_of = rows // STRETCH
    first = lengths[0]
    second = lengths[0] + lengths[1]
    segment = (block_of >= first).astype(jnp.int32) + (block_of >= second).astype(jnp.int32)
    start_block = jnp.where(segment == 2, second, jnp.where(segment == 1, first, 0))
    return (segment, rows - start_block * STRETCH)

def group_layer(params, block_rows, lengths):
    mix_gain, mix_shift, w_query, bias_query, w_key, bias_key, w_value, bias_value, shift_taps, log_step, log_decay, frequency, out_real, out_imag, skip_gain, w_out, bias_out, mlp_gain, mlp_shift, w_up, bias_up, w_down, bias_down = params
    normed = low(layer_norm(block_rows, mix_gain, mix_shift))
    query = low_back(matmul(normed, w_query) + bias_query)
    key_rows = low_back(matmul(normed, w_key) + bias_key)
    value_rows = low_back(matmul(normed, w_value) + bias_value)
    segment, place = segments_of(lengths)
    shifted = key_rows * shift_taps[:, 0]
    for offset in range(1, SHIFT):
        moved = jnp.pad(key_rows[:-offset], ((offset, 0), (0, 0)))
        shifted = shifted + jnp.where((place >= offset)[:, None], moved, 0.0) * shift_taps[:, offset]
    product = shifted * value_rows
    kernel = ssm_kernel(log_step, log_decay, frequency, out_real, out_imag, GROUP_TOK)
    conv = skip_gain * product
    for which in range(3):
        inside = (segment == which)[:, None]
        conv = conv + jnp.where(inside, causal_conv(jnp.where(inside, product, 0.0), kernel), 0.0)
    core = query * conv
    mixer = low_back(matmul(low(core), w_out))
    residual = block_rows + mixer + bias_out
    normed_two = low(layer_norm(residual, mlp_gain, mlp_shift))
    upward = low_back(matmul(normed_two, w_up) + bias_up)
    active = low(gelu_tanh(upward))
    branch = low_back(matmul(active, w_down))
    return residual + branch + bias_down

def reference(hidden_in, mix_gain, mix_shift, w_query, bias_query, w_key, bias_key, w_value, bias_value, shift_taps, log_step, log_decay, frequency, out_real, out_imag, skip_gain, w_out, bias_out, mlp_gain, mlp_shift, w_up, bias_up, w_down, bias_down, cotangent, seq_blocks):
    params = tuple((entry.astype(jnp.float32) for entry in (mix_gain, mix_shift, w_query, bias_query, w_key, bias_key, w_value, bias_value, shift_taps, log_step, log_decay, frequency, out_real, out_imag, skip_gain, w_out, bias_out, mlp_gain, mlp_shift, w_up, bias_up, w_down, bias_down)))
    group_rows = hidden_in.astype(jnp.float32).reshape(GROUPS, GROUP_TOK, D)
    group_cot = cotangent.astype(jnp.float32).reshape(GROUPS, GROUP_TOK, D)

    def forward(weights, inputs):
        layer = jax.checkpoint(group_layer)

        def one_group(element):
            return layer(weights, element[0], element[1])
        return lax.map(one_group, (inputs, seq_blocks))
    results, pullback = jax.vjp(forward, params, group_rows)
    gradients, grad_rows = pullback(group_cot)
    grad_mix_gain, grad_mix_shift, grad_w_query, grad_bias_query, grad_w_key, grad_bias_key, grad_w_value, grad_bias_value, grad_shift_taps, grad_log_step, grad_log_decay, grad_frequency, grad_out_real, grad_out_imag, grad_skip_gain, grad_w_out, grad_bias_out, grad_mlp_gain, grad_mlp_shift, grad_w_up, grad_bias_up, grad_w_down, grad_bias_down = gradients
    return (results.reshape(TOKENS, D).astype(jnp.bfloat16), grad_rows.reshape(TOKENS, D).astype(jnp.bfloat16), grad_mix_gain, grad_mix_shift, grad_w_query, grad_bias_query, grad_w_key, grad_bias_key, grad_w_value, grad_bias_value, grad_shift_taps, grad_log_step, grad_log_decay, grad_frequency, grad_out_real, grad_out_imag, grad_skip_gain, grad_w_out, grad_bias_out, grad_mlp_gain, grad_mlp_shift, grad_w_up, grad_bias_up, grad_w_down, grad_bias_down)
```

```python
import functools

import jax
import jax.numpy as jnp
from jax import lax
from jax.experimental import pallas as pl
from jax.experimental.pallas import tpu as pltpu
from jax.sharding import PartitionSpec as P

F32 = jnp.float32
BF16 = jnp.bfloat16
MODES = 32
LANES = 128
SEGS = 8
TAPS = 4
EPSILON = 1e-05
VMEM_LIMIT = 48 * 1024 * 1024
SMEM = pl.BlockSpec(memory_space=pltpu.SMEM)


def dot_nn(a, b):
    return lax.dot_general(a, b, (((1,), (0,)), ((), ())), preferred_element_type=F32)


def dot_nt(a, b):
    return lax.dot_general(a, b, (((1,), (1,)), ((), ())), preferred_element_type=F32)


def dot_tn(a, b):
    return lax.dot_general(a, b, (((0,), (0,)), ((), ())), preferred_element_type=F32)


def cmul(ar, ai, br, bi):
    return ar * br - ai * bi, ar * bi + ai * br


def fill_powers(zr, zi, pr, pi, steps):
    ar, ai = jnp.ones_like(zr), jnp.zeros_like(zi)
    pr[pl.ds(0, MODES), :] = ar
    pi[pl.ds(0, MODES), :] = ai
    for j in range(1, steps + 1):
        ar, ai = cmul(ar, ai, zr, zi)
        pr[pl.ds(j * MODES, MODES), :] = ar
        pi[pl.ds(j * MODES, MODES), :] = ai
    return ar, ai


def over_chunk(ar, ai):
    n = 1
    while n < SEGS:
        ar, ai = cmul(ar, ai, ar, ai)
        n *= 2
    return ar, ai


def fill_kern(wr, wi, pr, pi, kern, steps):
    for j in range(steps):
        v = wr * pr[pl.ds(j * MODES, MODES), :] - wi * pi[pl.ds(j * MODES, MODES), :]
        kern[pl.ds(j, 1), :] = 2.0 * jnp.sum(v, axis=0, keepdims=True)


def row(ref, i):
    return jnp.broadcast_to(ref[pl.ds(i, 1), :], (SEGS, LANES))


def group(ref, t):
    return ref[pl.ds(t * SEGS, SEGS), :]


def sublanes():
    return lax.broadcasted_iota(jnp.int32, (SEGS, LANES), 0)


def seg_mask(keep0, keep4):
    ids = sublanes()
    m = jnp.where(ids == 0, keep0, 1.0)
    return jnp.where(ids == SEGS // 2, keep4, m)


def at_seg(ref, k):
    return ref[pl.ds(k, MODES, stride=SEGS), :]


def store_pairs(ref, values, base=0):
    for t in range(0, len(values), 2):
        ref[pl.ds(base + t * SEGS, 2 * SEGS), :] = jnp.concatenate(values[t : t + 2]).astype(BF16)


def before_kernel(
    steps, keeps, key, halo, value, taps, zr, zi,
    prod, shifted, er, ei, dr, di, halos, own, chip, pr, pi, last,
):
    c = pl.program_id(1)
    k0, k4 = keeps[c, 0], keeps[c, 1]
    mask = seg_mask(k0, k4)
    ids = sublanes()
    ar, ai = fill_powers(zr[...], zi[...], pr, pi, steps)

    @pl.when(c == 0)
    def _():
        halos[...] = halo[...]

    @pl.when(c == 1)
    def _():
        halos[...] = last[...]

    window = []
    for back in (1, 2, 3):
        v = pltpu.roll(group(key, steps - back), 1, 0)
        window.append(jnp.where(ids == 0, row(halos, SEGS - back), v) * mask)
        last[pl.ds(SEGS - back, 1), :] = v[0:1, :]
    tap = [row(taps, j) for j in range(TAPS)]
    xs = []
    for t in range(steps):
        cur = group(key, t)
        s = tap[0] * cur + tap[1] * window[0] + tap[2] * window[1] + tap[3] * window[2]
        window = [cur] + window[:2]
        shifted[pl.ds(t * SEGS, SEGS), :] = s
        p = s * group(value, t)
        prod[pl.ds(t * SEGS, SEGS), :] = p
        xs.append(p)

    def per_mode(m, carry):
        sr = si = tr = ti = jnp.zeros((SEGS, LANES), F32)
        for t in range(steps):
            j = steps - 1 - t
            sr = sr + row(pr, j * MODES + m) * xs[t]
            si = si + row(pi, j * MODES + m) * xs[t]
            if t < steps - 1:
                tr = tr + sr
                ti = ti + si
        at = pl.multiple_of(m * SEGS, SEGS)
        er[pl.ds(at, SEGS), :] = sr
        ei[pl.ds(at, SEGS), :] = si
        dr[pl.ds(at, SEGS), :] = tr
        di[pl.ds(at, SEGS), :] = ti
        return carry

    lax.fori_loop(0, MODES, per_mode, 0)
    sr = si = jnp.zeros((MODES, LANES), F32)
    for k in range(SEGS):
        if k == SEGS // 2:
            sr, si = sr * k4, si * k4
        cr, ci = cmul(sr, si, ar, ai)
        sr = cr + at_seg(er, k)
        si = ci + at_seg(ei, k)

    @pl.when(c == 0)
    def _():
        own[pl.ds(0, MODES), :] = sr
        own[pl.ds(MODES, MODES), :] = si

    @pl.when(c == 1)
    def _():
        br, bi = over_chunk(ar, ai)
        cr, ci = cmul(own[pl.ds(0, MODES), :], own[pl.ds(MODES, MODES), :], br, bi)
        keep = k0 * k4
        chip[pl.ds(0, MODES), :] = (cr * keep + sr).astype(BF16)
        chip[pl.ds(MODES, MODES), :] = (ci * keep + si).astype(BF16)


def incoming(ref_list, masks, which, ar, ai):
    br, bi = cmul(ar, ai, ar, ai)
    read = lambda r: (r[pl.ds(0, MODES), :].astype(F32), r[pl.ds(MODES, MODES), :].astype(F32))
    sr, si = read(ref_list[-1])
    for by in range(len(ref_list) - 1, 0, -1):
        m = masks[which, by]
        cr, ci = cmul(sr, si, br * m, bi * m)
        rr, ri = read(ref_list[by - 1])
        sr, si = cr + rr, ci + ri
    return sr, si


def conv_kernel(steps, n_recv, keeps, masks, x, query, er, ei, own, *refs):
    recv, (zr, zi, wr, wi, skip, conv, core, state_r, state_i, pr, pi, kern) = refs[:n_recv], refs[n_recv:]
    c = pl.program_id(1)
    k4 = keeps[c, 1]
    ar, ai = fill_powers(zr[...], zi[...], pr, pi, steps)
    fill_kern(wr[...], wi[...], pr, pi, kern, steps)
    br, bi = over_chunk(ar, ai)
    sr, si = incoming(recv, masks, 0, br, bi)
    sr, si = sr * keeps[0, 0], si * keeps[0, 0]
    cr, ci = cmul(sr, si, br * keeps[0, 1], bi * keeps[0, 1])
    cr = (cr + own[pl.ds(0, MODES), :]) * keeps[1, 0]
    ci = (ci + own[pl.ds(MODES, MODES), :]) * keeps[1, 0]
    sr, si = jnp.where(c == 0, sr, cr), jnp.where(c == 0, si, ci)
    for k in range(SEGS):
        if k == SEGS // 2:
            sr, si = sr * k4, si * k4
        state_r[pl.ds(k, MODES, stride=SEGS), :] = sr
        state_i[pl.ds(k, MODES, stride=SEGS), :] = si
        if k < SEGS - 1:
            cr, ci = cmul(sr, si, ar, ai)
            sr = cr + at_seg(er, k)
            si = ci + at_seg(ei, k)
    sk = row(skip, 0)
    ys = [sk * group(x, t) for t in range(steps)]
    for j in range(steps):
        kj = row(kern, j)
        for t in range(j, steps):
            ys[t] = ys[t] + kj * group(x, t - j)

    def per_mode(m, ys):
        at = pl.multiple_of(m * SEGS, SEGS)
        a, b = state_r[pl.ds(at, SEGS), :], state_i[pl.ds(at, SEGS), :]
        u, v = cmul(2.0 * row(wr, m), 2.0 * row(wi, m), a, b)
        return tuple(
            y + (row(pr, (t + 1) * MODES + m) * u - row(pi, (t + 1) * MODES + m) * v) for t, y in enumerate(ys)
        )

    ys = lax.fori_loop(0, MODES, per_mode, tuple(ys))
    low = []
    for t in range(steps):
        conv[pl.ds(t * SEGS, SEGS), :] = ys[t]
        low.append(ys[t] * group(query, t))
    store_pairs(core, low)


def after_kernel(
    steps, keeps, grad_core, query, conv, zr, zi, wr, wi,
    g, grad_query, qr, qi, rr, ri, own, chip, pr, pi,
):
    c = 1 - pl.program_id(1)
    k0, k4 = keeps[c, 0], keeps[c, 1]
    ar, ai = fill_powers(zr[...], zi[...], pr, pi, steps)
    gs, low = [], []
    for t in range(steps):
        d = group(grad_core, t)
        v = d * group(query, t)
        g[pl.ds(t * SEGS, SEGS), :] = v
        gs.append(v)
        low.append(d * group(conv, t))
    store_pairs(grad_query, low)

    def per_mode(m, carry):
        sr = si = tr = ti = jnp.zeros((SEGS, LANES), F32)
        for t in reversed(range(steps)):
            sr = sr + row(pr, (t + 1) * MODES + m) * gs[t]
            si = si + row(pi, (t + 1) * MODES + m) * gs[t]
            tr = tr + sr
            ti = ti + si
        at = pl.multiple_of(m * SEGS, SEGS)
        qr[pl.ds(at, SEGS), :] = sr
        qi[pl.ds(at, SEGS), :] = si
        rr[pl.ds(at, SEGS), :] = tr
        ri[pl.ds(at, SEGS), :] = ti
        return carry

    lax.fori_loop(0, MODES, per_mode, 0)
    w2r, w2i = 2.0 * wr[...], 2.0 * wi[...]
    lr = jnp.where(c == 1, 0.0, own[pl.ds(0, MODES), :])
    li = jnp.where(c == 1, 0.0, own[pl.ds(MODES, MODES), :])
    for k in reversed(range(SEGS)):
        cr, ci = cmul(lr, li, ar, ai)
        ur, ui = cmul(w2r, w2i, at_seg(qr, k), at_seg(qi, k))
        lr, li = ur + cr, ui + ci
        if k == SEGS // 2:
            lr, li = lr * k4, li * k4
    lr, li = lr * k0, li * k0

    @pl.when(c == 1)
    def _():
        own[pl.ds(0, MODES), :] = lr
        own[pl.ds(MODES, MODES), :] = li

    @pl.when(c == 0)
    def _():
        chip[pl.ds(0, MODES), :] = lr.astype(BF16)
        chip[pl.ds(MODES, MODES), :] = li.astype(BF16)


def grads_kernel(steps, n_recv, keeps, masks, g, x, qr, qi, rr, ri, state_r, state_i, dr, di, own, *refs):
    recv = refs[:n_recv]
    zr, zi, wr, wi, skip, taps, key, halos, value, shifted = refs[n_recv : n_recv + 10]
    grad_kv, ghalo, dwr, dwi, dzr, dzi, dskip, dtaps, pr, pi, kern, mur, mui, nexts = refs[n_recv + 10 :]
    c = 1 - pl.program_id(1)
    lane = pl.program_id(0)
    k0, k4 = keeps[c, 0], keeps[c, 1]
    mask = seg_mask(k0, k4)
    ids = sublanes()
    ar, ai = fill_powers(zr[...], zi[...], pr, pi, steps)
    w2r, w2i = 2.0 * wr[...], 2.0 * wi[...]
    fill_kern(wr[...], wi[...], pr, pi, kern, steps)
    br, bi = over_chunk(ar, ai)
    mr, mi = incoming(recv, masks, 1, br, bi)
    keep = keeps[1, 0] * keeps[1, 1]
    cr, ci = cmul(mr, mi, br * keep, bi * keep)
    cr, ci = cr + own[pl.ds(0, MODES), :], ci + own[pl.ds(MODES, MODES), :]
    mr, mi = jnp.where(c == 1, mr, cr), jnp.where(c == 1, mi, ci)
    zero = jnp.zeros((MODES, LANES), F32)
    awr = awi = azr = azi = acr = aci = zero
    for k in reversed(range(SEGS)):
        mur[pl.ds(k, MODES, stride=SEGS), :] = mr
        mui[pl.ds(k, MODES, stride=SEGS), :] = mi
        s_r, s_i = at_seg(state_r, k), at_seg(state_i, k)
        q_r, q_i = at_seg(qr, k), at_seg(qi, k)
        u = cmul(s_r, s_i, q_r, q_i)
        awr, awi = awr + u[0], awi + u[1]
        u = cmul(s_r, s_i, at_seg(rr, k), at_seg(ri, k))
        azr, azi = azr + u[0], azi + u[1]
        u = cmul(mr, mi, at_seg(dr, k), at_seg(di, k))
        acr, aci = acr + u[0], aci + u[1]
        u = cmul(mr, mi, s_r, s_i)
        u = cmul(u[0], u[1], ar, ai)
        acr, aci = acr + float(steps) * u[0], aci + float(steps) * u[1]
        if k > 0:
            ur, ui = cmul(w2r, w2i, q_r, q_i)
            cr, ci = cmul(mr, mi, ar, ai)
            mr, mi = ur + cr, ui + ci
            if k == SEGS // 2:
                mr, mi = mr * k4, mi * k4
    for j in range(steps):
        acc = group(g, j) * group(x, 0)
        for t in range(j + 1, steps):
            acc = acc + group(g, t) * group(x, t - j)
        lag = jnp.sum(acc, axis=0, keepdims=True)
        u, v = pr[pl.ds(j * MODES, MODES), :] * lag, pi[pl.ds(j * MODES, MODES), :] * lag
        awr, awi = awr + u, awi + v
        azr, azi = azr + float(j) * u, azi + float(j) * v
    u = cmul(w2r, w2i, azr, azi)
    sk = row(skip, 0)
    gx = []
    dsk = jnp.zeros((SEGS, LANES), F32)
    for t in range(steps):
        gt = group(g, t)
        dsk = dsk + gt * group(x, t)
        gx.append(sk * gt)
    for j in range(steps):
        kj = row(kern, j)
        for t in range(0, steps - j):
            gx[t] = gx[t] + kj * group(g, t + j)

    def per_mode(m, gx):
        a = pl.multiple_of(m * SEGS, SEGS)
        u, v = mur[pl.ds(a, SEGS), :], mui[pl.ds(a, SEGS), :]
        return tuple(
            y + (row(pr, (steps - 1 - t) * MODES + m) * u - row(pi, (steps - 1 - t) * MODES + m) * v)
            for t, y in enumerate(gx)
        )

    gx = list(lax.fori_loop(0, MODES, per_mode, tuple(gx)))
    gv = [gx[t] * group(shifted, t) for t in range(steps)]
    gs = [gx[t] * group(value, t) for t in range(steps)]
    tap = [row(taps, j) for j in range(TAPS)]
    window = []
    for back in (1, 2, 3):
        v = pltpu.roll(group(key, steps - back), 1, 0)
        window.append(jnp.where(ids == 0, row(halos, SEGS - back), v) * mask)
    acc = [jnp.zeros((SEGS, LANES), F32)] * TAPS
    for t in range(steps):
        cur = group(key, t)
        for j, v in enumerate([cur] + window):
            acc[j] = acc[j] + gs[t] * v
        window = [cur] + window[:2]
    new = [2.0 * awr, -2.0 * awi, u[0] + acr, -(u[1] + aci), jnp.sum(dsk, axis=0, keepdims=True)]
    new.append(jnp.concatenate([jnp.sum(a, axis=0, keepdims=True) for a in acc], axis=0))
    outs = [dwr, dwi, dzr, dzi, dskip, dtaps]

    @pl.when(c == 1)
    def _():
        nexts[...] = jnp.zeros_like(nexts)
        for ref, v in zip(outs, new):
            ref[...] = v

    @pl.when(c == 0)
    def _():
        for ref, v in zip(outs, new):
            ref[...] += v

    begin = [gs[t] * mask for t in range(TAPS - 1)]
    later = [
        pltpu.roll(jnp.where(ids == 0, group(nexts, t), v), SEGS - 1, 0) for t, v in enumerate(begin)
    ]
    for t, v in enumerate(begin):
        nexts[pl.ds(t * SEGS, SEGS), :] = v
    ext = gs + later
    gk = [tap[0] * ext[t] + tap[1] * ext[t + 1] + tap[2] * ext[t + 2] + tap[3] * ext[t + 3] for t in range(steps)]
    size = steps * SEGS
    for part, values in enumerate((gk, gv)):
        at = pl.multiple_of((part * pl.num_programs(0) + lane) * LANES, LANES)
        for t in range(0, steps, 2):
            r = pl.multiple_of(c * size + t * SEGS, 2 * SEGS)
            grad_kv[pl.ds(r, 2 * SEGS), pl.ds(at, LANES)] = jnp.concatenate(values[t : t + 2]).astype(BF16)
    rows = [jnp.zeros((SEGS - TAPS + 1, LANES), F32)]
    for back in (3, 2, 1):
        v = jnp.zeros((1, LANES), F32)
        for j in range(back, TAPS):
            v = v + taps[pl.ds(j, 1), :] * begin[j - back][0:1, :]
        rows.append(v)
    ghalo[...] = jnp.concatenate(rows, axis=0)


class Mixer:
    def __init__(self, rows, channels):
        self.rows, self.channels, self.steps = rows, channels, rows // SEGS
        self.lanes = channels // LANES

    def chunk(self, rows, shift=0, flip=False):
        if flip:
            return pl.BlockSpec((rows, LANES), lambda l, c: (1 - c, l + shift))
        return pl.BlockSpec((rows, LANES), lambda l, c: (c, l + shift))

    def fixed(self, rows, at=0):
        return pl.BlockSpec((rows, LANES), lambda l, c: (at, l))

    def shape(self, rows, kind=F32):
        return jax.ShapeDtypeStruct((rows, self.channels), kind)

    def call(self, name, kernel, in_specs, out_specs, out_shape, scratch, work):
        table = pltpu.VMEM(((self.steps + 1) * MODES, LANES), F32)
        return pl.pallas_call(
            kernel,
            grid=(self.lanes, 2),
            in_specs=in_specs,
            out_specs=out_specs,
            out_shape=out_shape,
            scratch_shapes=[table, table] + scratch,
            compiler_params=pltpu.CompilerParams(vmem_limit_bytes=VMEM_LIMIT),
            cost_estimate=pl.CostEstimate(flops=work, bytes_accessed=work // 400, transcendentals=0),
            name=name,
        )

    def before(self, keeps, key_value, taps, zr, zi):
        n, ms = self.rows, MODES * SEGS
        big, states = self.chunk(n), self.chunk(ms)
        return self.call(
            "ssm_before",
            functools.partial(before_kernel, self.steps),
            [SMEM, big, self.fixed(SEGS, 2 * n // SEGS), self.chunk(n, self.lanes), self.fixed(TAPS)]
            + [self.fixed(MODES)] * 2,
            [big, big] + [states] * 4 + [self.chunk(SEGS), self.fixed(2 * MODES), self.fixed(2 * MODES)],
            [self.shape(2 * n)] * 2 + [self.shape(2 * ms)] * 4
            + [self.shape(2 * SEGS), self.shape(2 * MODES), self.shape(2 * MODES, BF16)],
            [pltpu.VMEM((SEGS, LANES), F32)],
            10**10,
        )(keeps, key_value, key_value, key_value, taps, zr, zi)

    def conv(self, keeps, masks, prod, query, er, ei, own, recv, zr, zi, wr, wi, skip):
        n, ms = self.rows, MODES * SEGS
        big, states, ends, modes = self.chunk(n), self.chunk(ms), self.fixed(2 * MODES), self.fixed(MODES)
        return self.call(
            "ssm_conv",
            functools.partial(conv_kernel, self.steps, len(recv)),
            [SMEM, SMEM, big, big, states, states] + [ends] * (1 + len(recv)) + [modes] * 4 + [self.fixed(1)],
            [big, big, states, states],
            [self.shape(2 * n), self.shape(2 * n, BF16)] + [self.shape(2 * ms)] * 2,
            [pltpu.VMEM((self.steps, LANES), F32)],
            10**10,
        )(keeps, masks, prod, query, er, ei, own, *recv, zr, zi, wr, wi, skip)

    def after(self, keeps, grad_core, query, conv, zr, zi, wr, wi):
        n, ms = self.rows, MODES * SEGS
        big, states, modes = self.chunk(n, 0, True), self.chunk(ms, 0, True), self.fixed(MODES)
        ends = self.fixed(2 * MODES)
        return self.call(
            "ssm_after",
            functools.partial(after_kernel, self.steps),
            [SMEM, big, big, big] + [modes] * 4,
            [big, big] + [states] * 4 + [ends, ends],
            [self.shape(2 * n), self.shape(2 * n, BF16)] + [self.shape(2 * ms)] * 4
            + [self.shape(2 * MODES), self.shape(2 * MODES, BF16)],
            [],
            10**10,
        )(keeps, grad_core, query, conv, zr, zi, wr, wi)

    def grads(self, keeps, masks, g, prod, q, state, d, own, recv, zr, zi, wr, wi, skip, taps, key_value, halos, shifted):
        n, ms = self.rows, MODES * SEGS
        big, states, modes = self.chunk(n, 0, True), self.chunk(ms, 0, True), self.fixed(MODES)
        ends, one, four = self.fixed(2 * MODES), self.fixed(1), self.fixed(TAPS)
        return self.call(
            "ssm_grads",
            functools.partial(grads_kernel, self.steps, len(recv)),
            [SMEM, SMEM, big, big] + [states] * 8 + [ends] * (1 + len(recv)) + [modes] * 4
            + [one, four, big, self.chunk(SEGS, 0, True), self.chunk(n, self.lanes, True), big],
            [pl.BlockSpec((2 * n, 2 * self.channels), lambda l, c: (0, 0)), self.fixed(SEGS)] + [modes] * 4 + [one, four],
            [jax.ShapeDtypeStruct((2 * n, 2 * self.channels), BF16), self.shape(SEGS)]
            + [self.shape(MODES)] * 4 + [self.shape(1), self.shape(TAPS)],
            [pltpu.VMEM((self.steps, LANES), F32)] + [pltpu.VMEM((ms, LANES), F32)] * 2
            + [pltpu.VMEM(((TAPS - 1) * SEGS, LANES), F32)],
            15 * 10**9,
        )(keeps, masks, g, prod, *q, *state, *d, own, *recv, zr, zi, wr, wi, skip, taps, key_value, halos, key_value, shifted)


TILE = 128


def feed_forward_kernel(n_sets, up_at, down_at, *refs):
    x_own, x_sib, c_own, c_sib = refs[:4]
    ups, downs = refs[4 : 4 + n_sets], refs[4 + n_sets : 4 + 2 * n_sets]
    bias = refs[4 + 2 * n_sets]
    outs = refs[5 + 2 * n_sets :]
    branch, grad_x, grad_bias = outs[0:2], outs[2:4], outs[4]
    n_up = 1 + max(a for a, _ in up_at)
    up_refs = outs[5 : 5 + n_up]
    down_refs = outs[5 + n_up : -4]
    xs, cs, acts, backs = outs[-4:]
    half = x_own.shape[0]
    xs[pl.ds(0, half), :] = x_own[...]
    xs[pl.ds(half, half), :] = x_sib[...]
    cs[pl.ds(0, half), :] = c_own[...]
    cs[pl.ds(half, half), :] = c_sib[...]
    for s in range(n_sets):
        up, down = ups[s], downs[s]
        total = None
        for r in range(2 * half // TILE):
            at = pl.ds(r * TILE, TILE)
            side, place = r * TILE // half, pl.ds(r * TILE % half, TILE)
            v = dot_nt(xs[at, :], up[...]) + bias[pl.ds(s, 1), :]
            square = v * v
            th = jnp.tanh(v * (0.79788456 + 0.79788456 * 0.044715 * square))
            half_up = 0.5 + 0.5 * th
            slope = half_up + v * (0.5 - 0.5 * th * th) * (0.79788456 + 0.79788456 * 3.0 * 0.044715 * square)
            active = (v * half_up).astype(BF16)
            back = (dot_nt(cs[at, :], down[...]) * slope).astype(BF16)
            acts[at, :] = active
            backs[at, :] = back
            part = jnp.sum(back.astype(F32), axis=0, keepdims=True)
            total = part if total is None else total + part
            out, grad = dot_nn(active, down[...]), dot_nn(back, up[...])
            if s == 0:
                branch[side][place, :] = out
                grad_x[side][place, :] = grad
            else:
                branch[side][place, :] += out
                grad_x[side][place, :] += grad
        grad_bias[pl.ds(s, 1), :] = total
        array, slot = up_at[s]
        up_refs[array][slot] = dot_tn(backs[...], xs[...]).astype(BF16)
        array, slot = down_at[s]
        down_refs[array][slot] = dot_tn(acts[...], cs[...]).astype(BF16)


def feed_forward(x_own, x_sib, c_own, c_sib, ups, downs, bias, up_at, down_at):
    rows, width = x_own.shape
    units = bias.shape[1]

    def arrays(where):
        return [
            jax.ShapeDtypeStruct((sum(a == i for a, _ in where), units, width), BF16)
            for i in range(1 + max(a for a, _ in where))
        ]

    full = jax.ShapeDtypeStruct((rows, width), F32)
    n_up = 1 + max(a for a, _ in up_at)
    out = pl.pallas_call(
        functools.partial(feed_forward_kernel, len(ups), up_at, down_at),
        out_shape=[full] * 4 + [jax.ShapeDtypeStruct(bias.shape, F32)] + arrays(up_at) + arrays(down_at),
        scratch_shapes=[pltpu.VMEM((2 * rows, width), BF16)] * 2 + [pltpu.VMEM((2 * rows, units), BF16)] * 2,
        compiler_params=pltpu.CompilerParams(vmem_limit_bytes=VMEM_LIMIT),
        cost_estimate=pl.CostEstimate(
            flops=24 * rows * width * units * len(ups), bytes_accessed=12 * units * width * len(ups), transcendentals=0
        ),
        name="feed_forward",
    )(x_own, x_sib, c_own, c_sib, *ups, *downs, bias)
    return out[0:2], out[2:4], out[4], out[5 : 5 + n_up], out[5 + n_up :]


def normalize(values):
    center = values - jnp.mean(values, axis=-1, keepdims=True)
    scale = lax.rsqrt(jnp.mean(center * center, axis=-1, keepdims=True) + EPSILON)
    return center * scale, scale


def normalize_back(grad, gain, xhat, scale):
    gy = grad * gain
    mean_gy = jnp.mean(gy, axis=-1, keepdims=True)
    mean_gx = jnp.mean(gy * xhat, axis=-1, keepdims=True)
    return scale * (gy - mean_gy - xhat * mean_gx)


def ssm_tables(log_step, log_decay, frequency, out_real, out_imag):
    step_size = jnp.exp(log_step)
    rate = -jnp.exp(log_decay)
    decay = rate * step_size
    turn = frequency * step_size
    growth = jnp.exp(decay)
    ratio_re = growth * jnp.cos(turn) - 1.0
    ratio_im = growth * jnp.sin(turn)
    denom = rate * rate + frequency * frequency
    scaled_re = (ratio_re * rate + ratio_im * frequency) / denom
    scaled_im = (ratio_im * rate - ratio_re * frequency) / denom
    weight_re = out_real * scaled_re - out_imag * scaled_im
    weight_im = out_real * scaled_im + out_imag * scaled_re
    return decay, turn, weight_re, weight_im


def local(
    groups, chips,
    hidden_in, mix_gain, mix_shift, w_query, bias_query, w_key, bias_key, w_value, bias_value, shift_taps,
    log_step, log_decay, frequency, out_real, out_imag, skip_gain, w_out, bias_out, mlp_gain, mlp_shift,
    w_up, bias_up, w_down, bias_down, cotangent, seq_blocks,
):
    rows, width = hidden_in.shape
    shard, shard_units = w_query.shape[1], w_up.shape[1]
    chans, channels = 2 * chips, chips * shard
    cut, unit_cut = shard // groups, shard_units // groups
    steps = rows // SEGS
    me_group, me_chan = lax.axis_index("group"), lax.axis_index("chan")
    me_chip, me_core = me_chan // 2, me_chan % 2
    same_core = [[2 * z + k for z in range(chips)] for k in range(2)]
    square = groups == 4

    def swap(x, axis, members=None):
        return lax.all_to_all(x, axis, 0, 0, axis_index_groups=members, tiled=True)

    def spread(x, axis, count, members=None):
        return swap(jnp.broadcast_to(x[None], (count,) + x.shape), axis, members)

    def along_z(x):
        return spread(x, "chan", chips, same_core)

    def fold_z(x):
        return jnp.sum(swap(x, "chan", same_core).astype(F32), axis=0)

    def group_swap(x, bit):
        return lax.ppermute(x, "group", [(i, i ^ bit) for i in range(groups)])

    def sibling(x):
        return lax.ppermute(x, "chan", [(i, i ^ 1) for i in range(chans)])

    def chip_shift(x, by):
        pairs = [(i, i + 2 * by) for i in range(chans) if 0 <= i + 2 * by < chans]
        return lax.ppermute(x, "chan", pairs)

    def gather_groups(a, b):
        if not square:
            return [list(spread(x, "group", groups)) for x in (a, b)]
        ax, bx, ay, by = group_swap(a, 1), group_swap(b, 1), group_swap(a, 2), group_swap(b, 2)
        return [a, ax, ay, group_swap(ay, 1)], [b, bx, by, group_swap(bx, 2)]

    def by_group(x, axis):
        if not square:
            return x
        pick = lambda order: jnp.concatenate([lax.slice_in_dim(x, i, i + 1, axis=axis) for i in order], axis=axis)
        for bit, order in ((1, (1, 0, 3, 2)), (2, (2, 3, 0, 1))):
            x = jnp.where((me_group & bit) > 0, pick(order), x)
        return x

    def add(*xs):
        return sum(x.astype(F32) for x in xs).astype(BF16)

    def fold_pair(send_a, a0, ay, send_b, b0, bx):
        ra, rb = group_swap(send_a, 1), group_swap(send_b, 2)
        ra2, rb2 = group_swap(add(ay, ra[1]), 2), group_swap(add(bx, rb[1]), 1)
        return add(a0, ra[0], ra2), add(b0, rb[0], rb2)

    def fold_groups(a, b):
        if not square:
            return [jnp.sum(swap(x, "group").astype(F32), axis=0).astype(BF16) for x in (a, b)]
        pair = lambda x, i, j: jnp.stack([x[i], x[j]])
        return fold_pair(pair(a, 1, 3), a[0], a[2], pair(b, 2, 3), b[0], b[1])

    def share(x):
        return lax.dynamic_index_in_dim(x.reshape(groups, -1, width), me_group, 0, keepdims=False)

    def to_steps(x):
        return x.reshape(SEGS, steps, width).transpose(1, 0, 2).reshape(rows, width)

    def to_rows(x):
        return x.reshape(steps, SEGS, width).transpose(1, 0, 2).reshape(rows, width)

    def in_chunks(own, other):
        return jnp.where(me_core == 0, own, other), jnp.where(me_core == 0, other, own)

    kv_piece = jnp.stack([share(w_key.T), share(w_value.T)])
    qo_piece = jnp.stack([share(w_query.T), share(w_out)])
    kv_z = along_z(kv_piece)
    small = jnp.concatenate(
        [
            log_decay.T, frequency.T, out_real.T, out_imag.T, shift_taps.T,
            jnp.stack([log_step, skip_gain, bias_query, bias_key, bias_value]),
            bias_up.reshape(shard_units // shard, shard),
        ]
    )
    small = along_z(small)
    qo_z = along_z(qo_piece)
    up_z = along_z(share(w_up.T))
    down_z = along_z(share(w_down))
    n_small = 4 * MODES + TAPS + 5
    units_bias = by_group(small[:, n_small:].reshape(chips, groups, unit_cut), 1)
    units_bias = jnp.moveaxis(units_bias, 1, 0).reshape(groups, chips * unit_cut)
    small = by_group(small[:, :n_small].reshape(chips, n_small, groups, cut), 2)
    small = jnp.transpose(small, (1, 2, 0, 3)).reshape(n_small, channels)
    all_decay, all_freq, all_real, all_imag = (small[i * MODES : (i + 1) * MODES] for i in range(4))
    rest = small[4 * MODES :]
    all_taps, all_step, all_skip = rest[:TAPS], rest[TAPS : TAPS + 1], rest[TAPS + 1 : TAPS + 2]
    all_bias = rest[TAPS + 2 :]

    def whole(parts):
        return jnp.concatenate([p.reshape(-1, width) for p in parts])

    ks, vs = gather_groups(kv_z[:, 0], kv_z[:, 1])
    wkv = whole(ks + vs)
    qs, os_ = gather_groups(qo_z[:, 0], qo_z[:, 1])
    wq, wo = whole(qs), whole(os_)
    ups, downs = gather_groups(up_z, down_z)
    ups, downs = ([p.reshape(-1, width) for p in x] for x in (ups, downs))

    first = seq_blocks[0, 0]
    second = first + seq_blocks[0, 1]

    def keep(block):
        starts = (block == 0) | (block == first) | (block == second)
        return jnp.where(starts, 0.0, 1.0).astype(F32)

    blocks = 4 * me_chip + jnp.arange(4)
    keeps = keep(blocks).reshape(2, 2)
    near = me_chip + jnp.stack([-jnp.arange(chips), jnp.arange(chips)])
    masks = jnp.prod(keep(4 * near[..., None] + jnp.arange(4)), axis=-1)

    halo_in = lax.ppermute(hidden_in[rows - SEGS :], "chan", [(2 * z + 1, 2 * z + 3) for z in range(chips - 1)])
    inputs = jnp.concatenate([to_steps(hidden_in), halo_in]).astype(F32)
    xhat, scale = normalize(inputs)
    normed = (xhat * mix_gain + mix_shift).astype(BF16)
    normed_sib = sibling(normed)
    chunk_0, chunk_1 = in_chunks(normed[:rows], normed_sib[:rows])
    halo = jnp.where(me_core == 0, normed_sib[rows:], normed[rows:])
    normed_all = jnp.concatenate([chunk_0, chunk_1, halo])
    key_value = dot_nt(normed_all, wkv) + all_bias[1:3].reshape(-1)
    query = dot_nt(normed_all[: 2 * rows], wq) + all_bias[0]

    (decay, turn, wr, wi), tables_back = jax.vjp(ssm_tables, all_step, all_decay, all_freq, all_real, all_imag)
    mag = jnp.exp(decay)
    zr, zi = mag * jnp.cos(turn), mag * jnp.sin(turn)
    mixer = Mixer(rows, channels)
    prod, shifted, er, ei, dr, di, halos, end_0, end = mixer.before(keeps, key_value, all_taps, zr, zi)
    recv = [chip_shift(end, by) for by in range(1, chips)]
    conv, core_low, state_r, state_i = mixer.conv(
        keeps, masks, prod, query, er, ei, end_0, recv, zr, zi, wr, wi, all_skip
    )
    core_own, core_other = in_chunks(core_low[:rows], core_low[rows:])
    from_sib = sibling(dot_nn(core_other, wo))
    residual = inputs[:rows] + dot_nn(core_own, wo) + from_sib + bias_out
    xhat_two, scale_two = normalize(residual)
    normed_two = (xhat_two * mlp_gain + mlp_shift).astype(BF16)
    cot = to_steps(cotangent)
    outgoing = cot.astype(F32)
    if square:
        up_at, down_at = ((0, 0), (2, 0), (1, 0), (2, 1)), ((0, 0), (1, 0), (2, 0), (2, 1))
    else:
        up_at = down_at = tuple((0, s) for s in range(groups))
    branch, grad_two, grad_units_bias, grad_ups, grad_downs = feed_forward(
        normed_two, sibling(normed_two), cot, sibling(cot), ups, downs, units_bias, up_at, down_at
    )
    output = to_rows((residual + branch[0] + sibling(branch[1]) + bias_down).astype(BF16))
    if square:
        ff = fold_pair(
            grad_ups[2], grad_ups[0][0], grad_ups[1][0], grad_downs[2], grad_downs[0][0], grad_downs[1][0]
        )
    else:
        ff = fold_groups(grad_ups[0], grad_downs[0])
    ff = jnp.stack([x.reshape(chips, unit_cut, width) for x in ff], axis=1)
    ff = fold_z(ff).astype(BF16)
    ff = spread(ff, "group", groups).astype(F32)
    ff = jnp.moveaxis(ff, 1, 0).reshape(2, shard_units, width)

    grad_two = grad_two[0] + sibling(grad_two[1])
    grad_residual = outgoing + normalize_back(grad_two, mlp_gain, xhat_two, scale_two)
    grad_res_low = grad_residual.astype(BF16)
    grad_res_all = jnp.concatenate(in_chunks(grad_res_low, sibling(grad_res_low)))
    grad_core = dot_nt(grad_res_all, wo)
    grad_wo = dot_tn(core_low, grad_res_all)
    g, grad_query, *qsums, back_1, back = mixer.after(keeps, grad_core, query, conv, zr, zi, wr, wi)
    recv = [chip_shift(back, -by) for by in range(1, chips)]
    grad_wq = dot_tn(grad_query, normed_all[: 2 * rows])
    grad_kv, grad_halo, dwr, dwi, dzr, dzi, dskip, dtaps = mixer.grads(
        keeps, masks, g, prod, qsums, (state_r, state_i), (dr, di), back_1, recv, zr, zi, wr, wi, all_skip, all_taps,
        key_value, halos, shifted,
    )
    dstep, ddecay, dfreq, dreal, dimag = tables_back((dzr, dzi, dwr, dwi))
    grad_halo = grad_halo.astype(BF16)
    grad_wkv = dot_tn(grad_kv, normed_all[: 2 * rows])
    grad_wk = grad_wkv[:channels] + dot_tn(grad_halo, normed_all[2 * rows :])
    grad_wv = grad_wkv[channels:]
    kv_own, kv_other = in_chunks(grad_kv[:rows], grad_kv[rows:])
    q_own, q_other = in_chunks(grad_query[:rows], grad_query[rows:])
    halo_back = dot_nn(grad_halo, wkv[:channels])
    to_sib = jnp.concatenate([dot_nn(kv_other, wkv) + dot_nn(q_other, wq), halo_back])
    from_sib = sibling(to_sib)
    halo_back = lax.ppermute(
        halo_back + from_sib[rows:], "chan", [(2 * z + 3, 2 * z + 1) for z in range(chips - 1)]
    )
    grad_normed = dot_nn(kv_own, wkv) + dot_nn(q_own, wq) + from_sib[:rows]
    grad_normed = grad_normed.reshape(steps, SEGS, width)
    grad_normed = grad_normed.at[steps - SEGS :, SEGS - 1].add(halo_back).reshape(rows, width)
    grad_inputs = grad_residual + normalize_back(grad_normed, mix_gain, xhat[:rows], scale[:rows])
    grad_input = to_rows(grad_inputs.astype(BF16))

    col = lambda x: jnp.sum(x.astype(F32), axis=0)
    features = jnp.stack(
        [
            col(grad_normed * xhat[:rows]), col(grad_normed), col(grad_residual),
            col(grad_two * xhat_two), col(grad_two), col(outgoing),
        ]
    )
    features = features.reshape(6, chips, 2, shard)
    mine = lambda x: lax.dynamic_index_in_dim(x, me_core, 2, keepdims=False)
    theirs = lambda x: lax.dynamic_index_in_dim(x, 1 - me_core, 2, keepdims=False)
    features = mine(features) + sibling(theirs(features))
    features = by_group(features.reshape(6, chips, groups, cut), 2)
    grad_bias_kv = col(grad_kv).reshape(2, channels) + jnp.stack([col(grad_halo), jnp.zeros((channels,), F32)])
    per_channel = jnp.concatenate(
        [ddecay, dfreq, dreal, dimag, dtaps, dstep, dskip, col(grad_query)[None], grad_bias_kv]
    )
    n_chan = per_channel.shape[0]
    tail = jnp.concatenate(
        [
            per_channel.reshape(n_chan, groups, chips, cut).transpose(1, 2, 0, 3).reshape(groups, chips, -1),
            features.transpose(2, 1, 0, 3).reshape(groups, chips, -1),
            grad_units_bias.reshape(groups, chips, -1),
        ],
        axis=-1,
    )
    used = tail.shape[-1]
    tail_rows = -(-used // (8 * width)) * 8
    tail = jnp.pad(tail, [(0, 0), (0, 0), (0, tail_rows * width - used)])
    tail = tail.reshape(groups, chips, tail_rows, width).astype(BF16)
    in_shares = lambda x: x.astype(BF16).reshape(groups, chips, cut, width)
    qo = fold_groups(in_shares(grad_wq), in_shares(grad_wo))
    kv = fold_groups(jnp.concatenate([in_shares(grad_wk), tail], axis=2), in_shares(grad_wv))
    mats = [*qo, *kv]
    sums = fold_z(jnp.concatenate(mats, axis=1)).astype(BF16)
    sums = spread(sums, "group", groups).astype(F32)
    wide = cut + tail_rows
    mat = lambda i, r=0: sums[:, i * cut + r : (i + 1) * cut + r].reshape(shard, width)
    tail = sums[:, 3 * cut : 2 * cut + wide].reshape(groups, -1)[:, :used]
    chan_part = tail[:, : n_chan * cut].reshape(groups, n_chan, cut).transpose(0, 2, 1).reshape(shard, n_chan)
    feat_part = tail[:, n_chan * cut : (n_chan + 6) * cut].reshape(groups, 6, cut).transpose(1, 0, 2).reshape(6, shard)
    sum_bias_up = tail[:, (n_chan + 6) * cut :].reshape(shard_units)
    modes = [chan_part[:, i * MODES : (i + 1) * MODES] for i in range(4)]
    sum_taps = chan_part[:, 4 * MODES : 4 * MODES + TAPS]
    singles = chan_part[:, 4 * MODES + TAPS :]
    return (
        output,
        grad_input,
        feat_part[0],
        feat_part[1],
        mat(0).T,
        singles[:, 2],
        mat(2).T,
        singles[:, 3],
        mat(3, tail_rows).T,
        singles[:, 4],
        sum_taps,
        singles[:, 0],
        modes[0],
        modes[1],
        modes[2],
        modes[3],
        singles[:, 1],
        mat(1),
        feat_part[2],
        feat_part[3],
        feat_part[4],
        ff[0].T,
        sum_bias_up,
        ff[1],
        feat_part[5],
    )


def solution(mesh):
    rows = P(("group", "chan"), None)
    columns, channels, vector, copied = P(None, "chan"), P("chan", None), P("chan"), P()
    return jax.shard_map(
        functools.partial(local, mesh.shape["group"], mesh.shape["chan"] // 2),
        mesh=mesh,
        in_specs=(
            rows, copied, copied, columns, vector, columns, vector, columns, vector, channels,
            vector, channels, channels, channels, channels, vector, channels, copied, copied, copied,
            columns, vector, channels, copied, rows, P("group", None),
        ),
        out_specs=(
            rows, rows, vector, vector, columns, vector, columns, vector, columns, vector,
            channels, vector, channels, channels, channels, channels, vector, channels, vector, vector,
            vector, columns, vector, channels, vector,
        ),
        check_vma=False,
    )
```

```python
import functools

import jax
import jax.numpy as jnp
import numpy as np
from jax import lax
from jax.experimental import pallas as pl
from jax.experimental.pallas import tpu as pltpu
from jax.sharding import PartitionSpec as P

F32 = jnp.float32
BF16 = jnp.bfloat16
MODES = 32
LANES = 128
SEGS = 8
TAPS = 4
BLOCK = 8
HALO = 16
TILE = 128
LN_TILE = 64
EPSILON = 1e-05
VMEM_LIMIT = 60 * 1024 * 1024
SMEM = pl.BlockSpec(memory_space=pltpu.SMEM)

TAP_ROW = 4 * MODES
STEP_ROW = TAP_ROW + TAPS
SKIP_ROW = STEP_ROW + 1
BIAS_ROW = SKIP_ROW + 1
PARAM_ROWS = BIAS_ROW + 3


def ssm_tables(log_step, log_decay, frequency, out_real, out_imag):
    step_size = jnp.exp(log_step)
    rate = -jnp.exp(log_decay)
    decay = rate * step_size
    turn = frequency * step_size
    growth = jnp.exp(decay)
    ratio_re = growth * jnp.cos(turn) - 1.0
    ratio_im = growth * jnp.sin(turn)
    denom = rate * rate + frequency * frequency
    scaled_re = (ratio_re * rate + ratio_im * frequency) / denom
    scaled_im = (ratio_im * rate - ratio_re * frequency) / denom
    weight_re = out_real * scaled_re - out_imag * scaled_im
    weight_im = out_real * scaled_im + out_imag * scaled_re
    return decay, turn, weight_re, weight_im


def table_inputs(params):
    parts = [params[pl.ds(i * MODES, MODES), :] for i in range(4)]
    return [params[pl.ds(STEP_ROW, 1), :], *parts]


def read_tables(tables):
    return [tables[pl.ds(i * MODES, MODES), :] for i in range(4)]


def dot_nn(a, b):
    return lax.dot_general(a, b, (((1,), (0,)), ((), ())), preferred_element_type=F32)


def dot_nt(a, b):
    return lax.dot_general(a, b, (((1,), (1,)), ((), ())), preferred_element_type=F32)


def dot_tn(a, b):
    return lax.dot_general(a, b, (((0,), (0,)), ((), ())), preferred_element_type=F32)


def cmul(ar, ai, br, bi):
    return ar * br - ai * bi, ar * bi + ai * br


def normalize(values):
    center = values - jnp.mean(values, axis=-1, keepdims=True)
    scale = lax.rsqrt(jnp.mean(center * center, axis=-1, keepdims=True) + EPSILON)
    return center * scale, scale


def normalize_back(grad, gain, xhat, scale):
    gy = grad * gain
    mean_gy = jnp.mean(gy, axis=-1, keepdims=True)
    mean_gx = jnp.mean(gy * xhat, axis=-1, keepdims=True)
    return scale * (gy - mean_gy - xhat * mean_gx)


def fill_powers(zr, zi, pr, pi, steps):
    ar, ai = jnp.ones_like(zr), jnp.zeros_like(zi)
    pr[pl.ds(0, MODES), :] = ar
    pi[pl.ds(0, MODES), :] = ai
    for j in range(1, steps + 1):
        ar, ai = cmul(ar, ai, zr, zi)
        pr[pl.ds(j * MODES, MODES), :] = ar
        pi[pl.ds(j * MODES, MODES), :] = ai
    return ar, ai


def over_chunk(ar, ai):
    n = 1
    while n < SEGS:
        ar, ai = cmul(ar, ai, ar, ai)
        n *= 2
    return ar, ai


def fill_kern(wr, wi, pr, pi, kern, steps):
    for j in range(steps):
        v = wr * pr[pl.ds(j * MODES, MODES), :] - wi * pi[pl.ds(j * MODES, MODES), :]
        kern[pl.ds(j, 1), :] = 2.0 * jnp.sum(v, axis=0, keepdims=True)


def row(ref, i):
    return jnp.broadcast_to(ref[pl.ds(i, 1), :], (SEGS, LANES))


def group(ref, steps, c, t):
    return ref[pl.ds((c * steps + t) * SEGS, SEGS), :]


def put(ref, steps, c, t, value):
    ref[pl.ds((c * steps + t) * SEGS, SEGS), :] = value


def put_low(ref, steps, c, t, pair):
    ref[pl.ds((c * steps + t) * SEGS, 2 * SEGS), :] = jnp.concatenate(pair).astype(BF16)


def sublanes():
    return lax.broadcasted_iota(jnp.int32, (SEGS, LANES), 0)


def seg_mask(keep0, keep4):
    ids = sublanes()
    m = jnp.where(ids == 0, keep0, 1.0)
    return jnp.where(ids == SEGS // 2, keep4, m)


def seg_rows(c, k):
    return pl.ds(c * MODES * SEGS + k, MODES, stride=SEGS)


def mode_rows(c, m):
    return pl.ds(pl.multiple_of(c * MODES * SEGS + m * SEGS, SEGS), SEGS)


def weigh(pr, pi, steps, order, power, last, data, outs):
    outs_r, outs_i, runs_r, runs_i = outs
    half = steps // 2
    for part in range(2):
        ts = order[part * half : (part + 1) * half]
        values = [[data(c, t) for t in ts] for c in range(2)]

        def per_mode(m, carry):
            acc = []
            for c in range(2):
                if part == 0:
                    acc.append([jnp.zeros((SEGS, LANES), F32)] * 4)
                else:
                    acc.append([r[mode_rows(c, m), :] for r in (outs_r, outs_i, runs_r, runs_i)])
            for i, t in enumerate(ts):
                a, b = row(pr, power(t) * MODES + m), row(pi, power(t) * MODES + m)
                for c in range(2):
                    sr, si, tr, ti = acc[c]
                    sr, si = sr + a * values[c][i], si + b * values[c][i]
                    if last or t != order[-1]:
                        tr, ti = tr + sr, ti + si
                    acc[c] = [sr, si, tr, ti]
            for c in range(2):
                for r, v in zip((outs_r, outs_i, runs_r, runs_i), acc[c]):
                    r[mode_rows(c, m), :] = v
            return carry

        lax.fori_loop(0, MODES, per_mode, 0, unroll=2)


def unfold(pr, pi, steps, power, states, ys):
    half = steps // 2
    out = [[], []]
    for part in range(2):
        ts = range(part * half, (part + 1) * half)
        init = tuple(ys[c][t] for c in range(2) for t in ts)

        def per_mode(m, acc):
            acc = list(acc)
            u = [states[0][mode_rows(c, m), :] for c in range(2)]
            v = [states[1][mode_rows(c, m), :] for c in range(2)]
            for i, t in enumerate(ts):
                a, b = row(pr, power(t) * MODES + m), row(pi, power(t) * MODES + m)
                for c in range(2):
                    at = c * half + i
                    acc[at] = acc[at] + (a * u[c] - b * v[c])
            return tuple(acc)

        acc = lax.fori_loop(0, MODES, per_mode, init, unroll=2)
        for c in range(2):
            out[c].extend(acc[c * half : (c + 1) * half])
    return out


def lags_apply(kern, steps, ys, source, adjoint):
    n = steps // BLOCK
    for tb in range(n):
        ts = range(tb * BLOCK, (tb + 1) * BLOCK)
        for sb in range(tb, n) if adjoint else range(tb + 1):
            ss = range(sb * BLOCK, (sb + 1) * BLOCK)
            xs = {(c, s): source(c, s) for c in range(2) for s in ss}
            for lag in range(steps):
                pairs = [(t, s) for t in ts for s in ss if (s - t if adjoint else t - s) == lag]
                if pairs:
                    k = row(kern, lag)
                    for t, s in pairs:
                        for c in range(2):
                            ys[c][t] = ys[c][t] + k * xs[c, s]
    return ys


def lag_sums(steps, left, right):
    n = steps // BLOCK
    sums = []
    for jb in range(n):
        acc = [jnp.zeros((SEGS, LANES), F32)] * BLOCK
        for c in range(2):
            for tb in range(jb, n):
                ts = range(tb * BLOCK, (tb + 1) * BLOCK)
                base = (tb - jb) * BLOCK
                xs = {s: right(c, s) for s in range(max(base - BLOCK + 1, 0), base + BLOCK)}
                for t in ts:
                    g = left(c, t)
                    for j in range(BLOCK):
                        s = t - jb * BLOCK - j
                        if s >= 0:
                            acc[j] = acc[j] + g * xs[s]
        sums.extend(jnp.sum(a, axis=0, keepdims=True) for a in acc)
    return sums


def earlier_keys(key, steps, keeps):
    ids = sublanes()
    out = []
    rolled = None
    for c in range(2):
        mask = seg_mask(keeps[c, 0], keeps[c, 1])
        new, windows = [], []
        for back in (1, 2, 3):
            v = pltpu.roll(group(key, steps, c, steps - back), 1, 0)
            new.append(v)
            before = row(key, 2 * steps * SEGS + HALO - back) if c == 0 else rolled[back - 1]
            windows.append(jnp.where(ids == 0, before, v) * mask)
        rolled = new
        out.append(windows)
    return out


def chunk_of(own, sib, core, c, at):
    return jnp.where(core == c, own[at, :].astype(F32), sib[at, :].astype(F32))


def join(parts, out):
    at = 0
    for p in parts:
        n = p.shape[0]
        out[pl.ds(at, n), :] = p[...]
        at += n


def part_to(outs, value):
    at = 0
    for o in outs:
        n = o.shape[0]
        o[...] = value[at : at + n].astype(BF16)
        at += n


def before_kernel(steps, n_parts, core, keeps, own, sib, gain, shift, order, *refs):
    mixed_kv, params = refs[:n_parts], refs[n_parts]
    normed, wkv, tables, key, value, prod, shifted, er, ei, dr, di, ends, chip, pr, pi, joined = refs[n_parts + 1 :]
    lane = pl.program_id(0)
    rows = steps * SEGS
    channels = wkv.shape[0] // 2

    @pl.when(lane == 0)
    def _():
        me = core[0]
        join(mixed_kv, joined)
        wkv[...] = dot_nn(order[...], joined[...]).astype(BF16)

        def rows_of(x):
            xhat, _ = normalize(x)
            return (xhat * gain[...] + shift[...]).astype(BF16)

        for c in range(2):
            for r in range(0, rows, LN_TILE):
                normed[pl.ds(c * rows + r, LN_TILE), :] = rows_of(chunk_of(own, sib, me, c, pl.ds(r, LN_TILE)))
        normed[pl.ds(2 * rows, HALO), :] = rows_of(chunk_of(own, sib, me, 1, pl.ds(rows, HALO)))

    decay, turn, wr, wi = ssm_tables(*table_inputs(params))
    mag = jnp.exp(decay)
    zr, zi = mag * jnp.cos(turn), mag * jnp.sin(turn)
    for i, v in enumerate((zr, zi, wr, wi)):
        tables[pl.ds(i * MODES, MODES), :] = v
    ar, ai = fill_powers(zr, zi, pr, pi, steps)
    at = pl.ds(pl.multiple_of(lane * LANES, LANES), LANES)
    also = pl.ds(pl.multiple_of(channels + lane * LANES, LANES), LANES)
    key[...] = dot_nt(normed[...], wkv[at, :]) + params[pl.ds(BIAS_ROW + 1, 1), :]
    value[...] = dot_nt(normed[pl.ds(0, 2 * rows), :], wkv[also, :]) + params[pl.ds(BIAS_ROW + 2, 1), :]
    tap = [row(params, TAP_ROW + j) for j in range(TAPS)]
    windows = earlier_keys(key, steps, keeps)
    for c in range(2):
        window = windows[c]
        for t in range(steps):
            cur = group(key, steps, c, t)
            s = tap[0] * cur + tap[1] * window[0] + tap[2] * window[1] + tap[3] * window[2]
            window = [cur] + window[:2]
            put(shifted, steps, c, t, s)
            put(prod, steps, c, t, s * group(value, steps, c, t))
    weigh(
        pr, pi, steps, list(range(steps)), lambda t: steps - 1 - t, False,
        lambda c, t: group(prod, steps, c, t), (er, ei, dr, di),
    )
    states = []
    for c in range(2):
        k4 = keeps[c, 1]
        sr = si = jnp.zeros((MODES, LANES), F32)
        for k in range(SEGS):
            if k == SEGS // 2:
                sr, si = sr * k4, si * k4
            cr, ci = cmul(sr, si, ar, ai)
            sr = cr + er[seg_rows(c, k), :]
            si = ci + ei[seg_rows(c, k), :]
        states.append((sr, si))
    ends[pl.ds(0, MODES), :], ends[pl.ds(MODES, MODES), :] = states[0]
    br, bi = over_chunk(ar, ai)
    cr, ci = cmul(*states[0], br, bi)
    keep = keeps[1, 0] * keeps[1, 1]
    chip[pl.ds(0, MODES), :] = (cr * keep + states[1][0]).astype(BF16)
    chip[pl.ds(MODES, MODES), :] = (ci * keep + states[1][1]).astype(BF16)


def incoming(ref_list, masks, which, ar, ai):
    br, bi = cmul(ar, ai, ar, ai)
    read = lambda r: (r[pl.ds(0, MODES), :].astype(F32), r[pl.ds(MODES, MODES), :].astype(F32))
    sr, si = read(ref_list[-1])
    for by in range(len(ref_list) - 1, 0, -1):
        m = masks[which, by]
        cr, ci = cmul(sr, si, br * m, bi * m)
        rr, ri = read(ref_list[by - 1])
        sr, si = cr + rr, ci + ri
    return sr, si


def conv_kernel(steps, n_parts, n_recv, keeps, masks, normed, prod, er, ei, ends, *refs):
    recv, mixed_qo, refs = refs[:n_recv], refs[n_recv : n_recv + n_parts], refs[n_recv + n_parts :]
    order, params, tables, wqo, query, conv, core_low, state_r, state_i, mixed = refs[:10]
    pr, pi, kern, twice_r, twice_i, joined = refs[10:]
    lane = pl.program_id(0)
    rows = steps * SEGS
    channels = wqo.shape[0] // 2

    @pl.when(lane == 0)
    def _():
        join(mixed_qo, joined)
        wqo[...] = dot_nn(order[...], joined[...]).astype(BF16)

    at = pl.ds(pl.multiple_of(lane * LANES, LANES), LANES)
    also = pl.ds(pl.multiple_of(channels + lane * LANES, LANES), LANES)
    query[...] = dot_nt(normed[pl.ds(0, 2 * rows), :], wqo[at, :]) + params[pl.ds(BIAS_ROW, 1), :]
    zr, zi, wr, wi = read_tables(tables)
    ar, ai = fill_powers(zr, zi, pr, pi, steps)
    w2r, w2i = 2.0 * wr, 2.0 * wi
    fill_kern(wr, wi, pr, pi, kern, steps)
    br, bi = over_chunk(ar, ai)
    sr, si = incoming(recv, masks, 0, br, bi)
    for c in range(2):
        if c == 1:
            sr, si = cmul(first_r, first_i, br * keeps[0, 1], bi * keeps[0, 1])
            sr, si = sr + ends[pl.ds(0, MODES), :], si + ends[pl.ds(MODES, MODES), :]
        sr, si = sr * keeps[c, 0], si * keeps[c, 0]
        first_r, first_i = sr, si
        for k in range(SEGS):
            if k == SEGS // 2:
                sr, si = sr * keeps[c, 1], si * keeps[c, 1]
            state_r[seg_rows(c, k), :] = sr
            state_i[seg_rows(c, k), :] = si
            twice_r[seg_rows(c, k), :], twice_i[seg_rows(c, k), :] = cmul(w2r, w2i, sr, si)
            if k < SEGS - 1:
                cr, ci = cmul(sr, si, ar, ai)
                sr = cr + er[seg_rows(c, k), :]
                si = ci + ei[seg_rows(c, k), :]
    source = lambda c, t: group(prod, steps, c, t)
    sk = row(params, SKIP_ROW)
    ys = [[sk * source(c, t) for t in range(steps)] for c in range(2)]
    for c in range(2):
        for t in range(steps):
            put(conv, steps, c, t, ys[c][t])
    base = lags_apply(kern, steps, [[group(conv, steps, c, t) for t in range(steps)] for c in range(2)], source, False)
    for c in range(2):
        for t in range(steps):
            put(conv, steps, c, t, base[c][t])
    ys = unfold(
        pr, pi, steps, lambda t: t + 1, (twice_r, twice_i),
        [[group(conv, steps, c, t) for t in range(steps)] for c in range(2)],
    )
    for c in range(2):
        for t in range(0, steps, 2):
            low = []
            for i in (t, t + 1):
                put(conv, steps, c, i, ys[c][i])
                low.append(ys[c][i] * group(query, steps, c, i))
            put_low(core_low, steps, c, t, low)
    out = dot_nn(core_low[...], wqo[also, :])

    @pl.when(lane == 0)
    def _():
        mixed[...] = out

    @pl.when(lane > 0)
    def _():
        mixed[...] += out


def after_kernel(
    steps, core, keeps, residual, grad_own, grad_sib, cot_own, cot_sib, gain, order, wo, normed, query, conv, core_low,
    tables, grad_residual, g, grad_query, qr, qi, rr, ri, ends, chip, sums, *refs,
):
    grad_qo, (pr, pi, low, grad_core, grad_w) = refs[:-5], refs[-5:]
    lane = pl.program_id(0)
    rows = steps * SEGS
    channels = grad_w.shape[0] // 2

    @pl.when(lane == 0)
    def _():
        me = core[0]
        total = [jnp.zeros((1, low.shape[1]), F32)] * 4
        for c in range(2):
            for r in range(0, rows, LN_TILE):
                at = pl.ds(c * rows + r, LN_TILE)
                xhat, scale = normalize(residual[at, :])
                grad = grad_own[at, :] + grad_sib[at, :]
                cot = chunk_of(cot_own, cot_sib, me, c, pl.ds(r, LN_TILE))
                out = cot + normalize_back(grad, gain[...], xhat, scale)
                grad_residual[at, :] = out
                low[at, :] = out.astype(BF16)
                for i, v in enumerate((out, grad * xhat, grad, cot)):
                    total[i] = total[i] + jnp.sum(v, axis=0, keepdims=True)
        sums[...] = jnp.concatenate(total, axis=0)

    zr, zi, wr, wi = read_tables(tables)
    ar, ai = fill_powers(zr, zi, pr, pi, steps)
    grad_core[...] = dot_nt(low[...], wo[...])
    for c in range(2):
        for t in range(0, steps, 2):
            pair = []
            for i in (t, t + 1):
                d = group(grad_core, steps, c, i)
                put(g, steps, c, i, d * group(query, steps, c, i))
                pair.append(d * group(conv, steps, c, i))
            put_low(grad_query, steps, c, t, pair)
    at = pl.ds(pl.multiple_of(lane * LANES, LANES), LANES)
    also = pl.ds(pl.multiple_of(channels + lane * LANES, LANES), LANES)
    grad_w[at, :] = dot_tn(grad_query[...], normed[pl.ds(0, 2 * rows), :]).astype(BF16)
    grad_w[also, :] = dot_tn(core_low[...], low[...]).astype(BF16)

    @pl.when(lane == pl.num_programs(0) - 1)
    def _():
        part_to(grad_qo, dot_tn(order[...], grad_w[...]))

    weigh(
        pr, pi, steps, list(reversed(range(steps))), lambda t: t + 1, True,
        lambda c, t: group(g, steps, c, t), (qr, qi, rr, ri),
    )
    w2r, w2i = 2.0 * wr, 2.0 * wi
    lr = li = jnp.zeros((MODES, LANES), F32)
    for c in (1, 0):
        for k in reversed(range(SEGS)):
            cr, ci = cmul(lr, li, ar, ai)
            ur, ui = cmul(w2r, w2i, qr[seg_rows(c, k), :], qi[seg_rows(c, k), :])
            lr, li = ur + cr, ui + ci
            if k == SEGS // 2:
                lr, li = lr * keeps[c, 1], li * keeps[c, 1]
        lr, li = lr * keeps[c, 0], li * keeps[c, 0]
        if c == 1:
            ends[pl.ds(0, MODES), :] = lr
            ends[pl.ds(MODES, MODES), :] = li
    chip[pl.ds(0, MODES), :] = lr.astype(BF16)
    chip[pl.ds(MODES, MODES), :] = li.astype(BF16)


def grads_kernel(
    steps, n_recv, core, keeps, masks, g, prod, qr, qi, rr, ri, state_r, state_i, dr, di, ends, *refs
):
    recv = refs[:n_recv]
    params, tables, key, value, shifted, grad_query, normed, order, wk, wv, wq = refs[n_recv : n_recv + 11]
    grad_normed, grad_params = refs[n_recv + 11 : n_recv + 13]
    grad_kv, (pr, pi, kern, mur, mui, back, cat, cat_w, grad_w) = refs[n_recv + 13 : -9], refs[-9:]
    lane = pl.program_id(0)
    rows = steps * SEGS
    channels = grad_w.shape[0] // 2
    ids = sublanes()
    zr, zi, wr, wi = read_tables(tables)
    ar, ai = fill_powers(zr, zi, pr, pi, steps)
    w2r, w2i = 2.0 * wr, 2.0 * wi
    fill_kern(wr, wi, pr, pi, kern, steps)
    br, bi = over_chunk(ar, ai)
    mr, mi = incoming(recv, masks, 1, br, bi)
    zero = jnp.zeros((MODES, LANES), F32)
    awr = awi = azr = azi = acr = aci = zero
    for c in (1, 0):
        if c == 0:
            keep = keeps[1, 0] * keeps[1, 1]
            mr, mi = cmul(last_r, last_i, br * keep, bi * keep)
            mr, mi = mr + ends[pl.ds(0, MODES), :], mi + ends[pl.ds(MODES, MODES), :]
        last_r, last_i = mr, mi
        for k in reversed(range(SEGS)):
            at = seg_rows(c, k)
            mur[at, :] = mr
            mui[at, :] = mi
            s_r, s_i = state_r[at, :], state_i[at, :]
            q_r, q_i = qr[at, :], qi[at, :]
            u = cmul(s_r, s_i, q_r, q_i)
            awr, awi = awr + u[0], awi + u[1]
            u = cmul(s_r, s_i, rr[at, :], ri[at, :])
            azr, azi = azr + u[0], azi + u[1]
            u = cmul(mr, mi, dr[at, :], di[at, :])
            acr, aci = acr + u[0], aci + u[1]
            u = cmul(mr, mi, s_r, s_i)
            u = cmul(u[0], u[1], ar, ai)
            acr, aci = acr + float(steps) * u[0], aci + float(steps) * u[1]
            if k > 0:
                ur, ui = cmul(w2r, w2i, q_r, q_i)
                cr, ci = cmul(mr, mi, ar, ai)
                mr, mi = ur + cr, ui + ci
                if k == SEGS // 2:
                    mr, mi = mr * keeps[c, 1], mi * keeps[c, 1]
    source = lambda c, t: group(g, steps, c, t)
    for j, lag in enumerate(lag_sums(steps, source, lambda c, t: group(prod, steps, c, t))):
        u, v = pr[pl.ds(j * MODES, MODES), :] * lag, pi[pl.ds(j * MODES, MODES), :] * lag
        awr, awi = awr + u, awi + v
        azr, azi = azr + float(j) * u, azi + float(j) * v
    u = cmul(w2r, w2i, azr, azi)
    _, tables_back = jax.vjp(ssm_tables, *table_inputs(params))
    dstep, *dmodes = tables_back((u[0] + acr, -(u[1] + aci), 2.0 * awr, -2.0 * awi))
    for i, v in enumerate(dmodes):
        grad_params[pl.ds(i * MODES, MODES), :] = v
    grad_params[pl.ds(STEP_ROW, 1), :] = dstep
    sk = row(params, SKIP_ROW)
    dsk = jnp.zeros((SEGS, LANES), F32)
    for c in range(2):
        for t in range(steps):
            gt = source(c, t)
            dsk = dsk + gt * group(prod, steps, c, t)
            put(back, steps, c, t, sk * gt)
    grad_params[pl.ds(SKIP_ROW, 1), :] = jnp.sum(dsk, axis=0, keepdims=True)
    read = lambda: [[group(back, steps, c, t) for t in range(steps)] for c in range(2)]
    gx = lags_apply(kern, steps, read(), source, True)
    for c in range(2):
        for t in range(steps):
            put(back, steps, c, t, gx[c][t])
    gx = unfold(pr, pi, steps, lambda t: steps - 1 - t, (mur, mui), read())
    for c in range(2):
        for t in range(0, steps, 2):
            low = [gx[c][i] * group(shifted, steps, c, i) for i in (t, t + 1)]
            cat[pl.ds((c * steps + t) * SEGS, 2 * SEGS), pl.ds(LANES, LANES)] = jnp.concatenate(low).astype(BF16)
            for i in (t, t + 1):
                put(back, steps, c, i, gx[c][i] * group(value, steps, c, i))
    tap = [row(params, TAP_ROW + j) for j in range(TAPS)]
    windows = earlier_keys(key, steps, keeps)
    acc = [jnp.zeros((SEGS, LANES), F32)] * TAPS
    for c in range(2):
        window = windows[c]
        for t in range(steps):
            cur = group(key, steps, c, t)
            v = group(back, steps, c, t)
            for j, w in enumerate([cur] + window):
                acc[j] = acc[j] + v * w
            window = [cur] + window[:2]
    for j, a in enumerate(acc):
        grad_params[pl.ds(TAP_ROW + j, 1), :] = jnp.sum(a, axis=0, keepdims=True)
    following = [jnp.zeros((SEGS, LANES), F32)] * (TAPS - 1)
    for c in (1, 0):
        mask = seg_mask(keeps[c, 0], keeps[c, 1])
        begin = [group(back, steps, c, t) * mask for t in range(TAPS - 1)]
        later = [pltpu.roll(jnp.where(ids == 0, f, v), SEGS - 1, 0) for f, v in zip(following, begin)]
        following = begin
        ext = lambda t: group(back, steps, c, t) if t < steps else later[t - steps]
        for t in range(0, steps, 2):
            low = [
                tap[0] * ext(i) + tap[1] * ext(i + 1) + tap[2] * ext(i + 2) + tap[3] * ext(i + 3) for i in (t, t + 1)
            ]
            cat[pl.ds((c * steps + t) * SEGS, 2 * SEGS), pl.ds(0, LANES)] = jnp.concatenate(low).astype(BF16)
    edge = [jnp.zeros((HALO - TAPS + 1, LANES), F32)]
    for b in (3, 2, 1):
        v = jnp.zeros((1, LANES), F32)
        for j in range(b, TAPS):
            v = v + params[pl.ds(TAP_ROW + j, 1), :] * following[j - b][0:1, :]
        edge.append(v)
    halo_at = pl.ds(2 * rows, HALO)
    cat[halo_at, pl.ds(0, LANES)] = jnp.concatenate(edge, axis=0).astype(BF16)
    cat[halo_at, pl.ds(LANES, 2 * LANES)] = jnp.zeros((HALO, 2 * LANES), BF16)
    cat[pl.ds(0, 2 * rows), pl.ds(2 * LANES, LANES)] = grad_query[...]
    for i, w in enumerate((wk, wv, wq)):
        cat_w[pl.ds(i * LANES, LANES), :] = w[...]
    both = dot_tn(cat[:, pl.ds(0, 2 * LANES)], normed[...])
    grad_w[pl.ds(pl.multiple_of(lane * LANES, LANES), LANES), :] = both[:LANES].astype(BF16)
    grad_w[pl.ds(pl.multiple_of(channels + lane * LANES, LANES), LANES), :] = both[LANES:].astype(BF16)

    @pl.when(lane == pl.num_programs(0) - 1)
    def _():
        part_to(grad_kv, dot_tn(order[...], grad_w[...]))

    for i, part in enumerate((2, 0, 1)):
        grad_params[pl.ds(BIAS_ROW + i, 1), :] = jnp.sum(cat[:, pl.ds(part * LANES, LANES)].astype(F32), axis=0, keepdims=True)
    me = core[0]
    for c in range(2):
        out = dot_nn(cat[pl.ds(c * rows, rows), :], cat_w[...])
        at = pl.ds(pl.multiple_of(lax.rem(c + me, 2) * rows, rows), rows)
        add_to(grad_normed, at, out, lane)
    add_to(grad_normed, halo_at, dot_nn(cat[halo_at, :], cat_w[...]), lane)


def add_to(ref, at, value, step):
    @pl.when(step == 0)
    def _():
        ref[at, :] = value

    @pl.when(step > 0)
    def _():
        ref[at, :] += value


class Mixer:
    def __init__(self, rows, channels, width, groups):
        self.rows, self.channels, self.width, self.groups = rows, channels, width, groups
        self.steps = rows // SEGS

    def lanes(self, rows):
        return pl.BlockSpec((rows, LANES), lambda l: (0, l))

    def whole(self, *shape):
        return pl.BlockSpec(shape, lambda l: (0,) * len(shape))

    def shape(self, rows, kind=F32):
        return jax.ShapeDtypeStruct((rows, self.channels), kind)

    def wide(self, rows, kind):
        return jax.ShapeDtypeStruct((rows, self.width), kind)

    def call(self, name, kernel, in_specs, outs, scratch, work):
        table = pltpu.VMEM(((self.steps + 1) * MODES, LANES), F32)
        return pl.pallas_call(
            kernel,
            grid=(self.channels // LANES,),
            in_specs=in_specs,
            out_specs=[s for s, _ in outs],
            out_shape=[s for _, s in outs],
            scratch_shapes=[table, table] + scratch,
            compiler_params=pltpu.CompilerParams(vmem_limit_bytes=VMEM_LIMIT),
            cost_estimate=pl.CostEstimate(flops=work, bytes_accessed=work // 400, transcendentals=0),
            name=name,
        )

    def units(self, part=0):
        return pl.BlockSpec((LANES, self.width), lambda l: (l + part * self.channels // LANES, 0))

    def pair(self):
        n = 2 * self.channels
        return self.whole(n, self.width), self.wide(n, BF16)

    def parts(self):
        n = 2 * self.channels // self.groups
        return [(self.whole(n, self.width), self.wide(n, BF16))] * self.groups

    def order(self):
        return self.whole(2 * self.channels, 2 * self.channels)

    def before(self, core, keeps, own, sib, gain, shift, order, mixed_kv, params):
        n, ms, w = 2 * self.rows, 2 * MODES * SEGS, self.width
        line, states, ends = self.whole(1, w), (self.lanes(ms), self.shape(ms)), self.lanes(2 * MODES)
        return self.call(
            "ssm_before",
            functools.partial(before_kernel, self.steps, len(mixed_kv)),
            [SMEM, SMEM, self.whole(*own.shape), self.whole(*own.shape), line, line, self.order()]
            + [self.whole(*p.shape) for p in mixed_kv] + [self.lanes(PARAM_ROWS)],
            [(self.whole(n + HALO, w), self.wide(n + HALO, BF16)), self.pair(), (self.lanes(4 * MODES), self.shape(4 * MODES))]
            + [(self.lanes(n + HALO), self.shape(n + HALO))] + [(self.lanes(n), self.shape(n))] * 3 + [states] * 4
            + [(ends, self.shape(2 * MODES)), (ends, self.shape(2 * MODES, BF16))],
            [pltpu.VMEM((2 * self.channels, w), BF16)],
            10**10,
        )(core, keeps, own, sib, gain, shift, order, *mixed_kv, params)

    def conv(self, keeps, masks, normed, prod, er, ei, ends, recv, order, mixed_qo, params, tables):
        n, ms, w = 2 * self.rows, 2 * MODES * SEGS, self.width
        big, states, last = self.lanes(n), self.lanes(ms), self.lanes(2 * MODES)
        return self.call(
            "ssm_conv",
            functools.partial(conv_kernel, self.steps, len(mixed_qo), len(recv)),
            [SMEM, SMEM, self.whole(*normed.shape), big, states, states] + [last] * (1 + len(recv))
            + [self.whole(*p.shape) for p in mixed_qo] + [self.order(), self.lanes(PARAM_ROWS), self.lanes(4 * MODES)],
            [self.pair(), (big, self.shape(n)), (big, self.shape(n)), (big, self.shape(n, BF16))]
            + [(states, self.shape(ms))] * 2 + [(self.whole(n, w), self.wide(n, F32))],
            [pltpu.VMEM((self.steps, LANES), F32)] + [pltpu.VMEM((ms, LANES), F32)] * 2
            + [pltpu.VMEM((2 * self.channels, w), BF16)],
            10**10,
        )(keeps, masks, normed, prod, er, ei, ends, *recv, *mixed_qo, order, params, tables)

    def after(
        self, core, keeps, residual, grad_own, grad_sib, cot_own, cot_sib, gain, order, wqo, normed, query, conv, core_low,
        tables,
    ):
        n, ms, w = 2 * self.rows, 2 * MODES * SEGS, self.width
        big, states, last = self.lanes(n), self.lanes(ms), self.lanes(2 * MODES)
        full, half = self.whole(n, w), self.whole(n // 2, w)
        return self.call(
            "ssm_after",
            functools.partial(after_kernel, self.steps),
            [SMEM, SMEM, full, full, full, half, half, self.whole(1, w), self.order(), self.units(1), self.whole(*normed.shape)]
            + [big] * 3 + [self.lanes(4 * MODES)],
            [(full, self.wide(n, F32)), (big, self.shape(n)), (big, self.shape(n, BF16))]
            + [(states, self.shape(ms))] * 4 + [(last, self.shape(2 * MODES)), (last, self.shape(2 * MODES, BF16))]
            + [(self.whole(4, w), self.wide(4, F32))] + self.parts(),
            [pltpu.VMEM((n, w), BF16), pltpu.VMEM((n, LANES), F32), pltpu.VMEM((2 * self.channels, w), BF16)],
            10**10,
        )(
            core, keeps, residual, grad_own, grad_sib, cot_own, cot_sib, gain, order, wqo, normed, query, conv, core_low,
            tables,
        )

    def grads(
        self, core, keeps, masks, g, prod, q, state, d, ends, recv, params, tables, key, value, shifted, grad_query, normed,
        order, wkv, wqo,
    ):
        n, ms, w = 2 * self.rows, 2 * MODES * SEGS, self.width
        big, states, last = self.lanes(n), self.lanes(ms), self.lanes(2 * MODES)
        return self.call(
            "ssm_grads",
            functools.partial(grads_kernel, self.steps, len(recv)),
            [SMEM, SMEM, SMEM, big, big] + [states] * 8 + [last] * (1 + len(recv))
            + [self.lanes(PARAM_ROWS), self.lanes(4 * MODES), self.lanes(n + HALO), big, big, big, self.whole(*normed.shape)]
            + [self.order(), self.units(), self.units(1), self.units()],
            [(self.whole(n + HALO, w), self.wide(n + HALO, F32)), (self.lanes(PARAM_ROWS), self.shape(PARAM_ROWS))]
            + self.parts(),
            [pltpu.VMEM((self.steps, LANES), F32)] + [pltpu.VMEM((ms, LANES), F32)] * 2
            + [pltpu.VMEM((n, LANES), F32), pltpu.VMEM((n + HALO, 3 * LANES), BF16), pltpu.VMEM((3 * LANES, w), BF16)]
            + [pltpu.VMEM((2 * self.channels, w), BF16)],
            15 * 10**9,
        )(
            core, keeps, masks, g, prod, *q, *state, *d, ends, *recv, params, tables, key, value, shifted, grad_query, normed,
            order, wkv, wkv, wqo,
        )


def finish_kernel(steps, grad, from_sib, edge, own, grad_residual, core, gain, out, sums, total):
    rows = steps * SEGS
    total[...] = grad[pl.ds(0, rows), :] + from_sib[pl.ds(0, rows), :]
    for b in range(1, TAPS):
        total[pl.ds((steps - b) * SEGS + SEGS - 1, 1), :] += edge[pl.ds(HALO - b, 1), :]
    first = pl.multiple_of(core[0] * rows, rows)
    acc = [jnp.zeros((1, total.shape[1]), F32)] * 2
    for r in range(0, rows, LN_TILE):
        at = pl.ds(r, LN_TILE)
        xhat, scale = normalize(own[at, :].astype(F32))
        v = total[at, :]
        res = grad_residual[pl.ds(first + r, LN_TILE), :]
        out[at, :] = (res + normalize_back(v, gain[...], xhat, scale)).astype(BF16)
        for i, w in enumerate((v * xhat, v)):
            acc[i] = acc[i] + jnp.sum(w, axis=0, keepdims=True)
    sums[...] = jnp.concatenate(acc, axis=0)


def finish(grad, from_sib, edge, own, grad_residual, core, gain):
    rows, width = from_sib.shape[0] - HALO, grad.shape[1]
    vmem = pl.BlockSpec(memory_space=pltpu.VMEM)
    return pl.pallas_call(
        functools.partial(finish_kernel, rows // SEGS),
        in_specs=[vmem] * 5 + [SMEM, vmem],
        out_shape=[jax.ShapeDtypeStruct((rows, width), BF16), jax.ShapeDtypeStruct((2, width), F32)],
        scratch_shapes=[pltpu.VMEM((rows, width), F32)],
        compiler_params=pltpu.CompilerParams(vmem_limit_bytes=VMEM_LIMIT),
        cost_estimate=pl.CostEstimate(flops=2 * 10**9, bytes_accessed=10**6, transcendentals=0),
        name="finish",
    )(grad, from_sib, edge, own, grad_residual, core, gain)


def feed_forward_kernel(n_sets, up_at, down_at, core, own, sib, mixed_own, mixed_sib, c_own, c_sib, lines, *refs):
    ups, downs = refs[:n_sets], refs[n_sets : 2 * n_sets]
    bias = refs[2 * n_sets]
    outs = refs[1 + 2 * n_sets :]
    residual, branch, grad_x, grad_bias = outs[:4]
    n_up = 1 + max(a for a, _ in up_at)
    up_refs = outs[4 : 4 + n_up]
    down_refs = outs[4 + n_up : -4]
    xs, cs, acts, backs = outs[-4:]
    me = core[0]
    half = c_own.shape[0]
    for c in range(2):
        for r in range(0, half, LN_TILE):
            at, part = pl.ds(c * half + r, LN_TILE), pl.ds(r, LN_TILE)
            v = chunk_of(own, sib, me, c, part) + mixed_own[at, :] + mixed_sib[at, :] + lines[pl.ds(0, 1), :]
            residual[at, :] = v
            xhat, _ = normalize(v)
            xs[at, :] = (xhat * lines[pl.ds(1, 1), :] + lines[pl.ds(2, 1), :]).astype(BF16)
            cs[at, :] = chunk_of(c_own, c_sib, me, c, part).astype(BF16)
    for s in range(n_sets):
        up, down = ups[s], downs[s]
        total = None
        for r in range(0, 2 * half, TILE):
            at = pl.ds(r, TILE)
            side = pl.ds(pl.multiple_of(lax.rem(r // half + me, 2) * half + r % half, TILE), TILE)
            v = dot_nt(xs[at, :], up[...]) + bias[pl.ds(s, 1), :]
            square = v * v
            th = jnp.tanh(v * (0.79788456 + 0.79788456 * 0.044715 * square))
            half_up = 0.5 + 0.5 * th
            slope = half_up + v * (0.5 - 0.5 * th * th) * (0.79788456 + 0.79788456 * 3.0 * 0.044715 * square)
            active = (v * half_up).astype(BF16)
            back = (dot_nt(cs[at, :], down[...]) * slope).astype(BF16)
            acts[at, :] = active
            backs[at, :] = back
            part = jnp.sum(back.astype(F32), axis=0, keepdims=True)
            total = part if total is None else total + part
            out, grad = dot_nn(active, down[...]), dot_nn(back, up[...])
            if s == 0:
                branch[side, :] = out
                grad_x[at, :] = grad
            else:
                branch[side, :] += out
                grad_x[at, :] += grad
        grad_bias[pl.ds(s, 1), :] = total
        array, slot = up_at[s]
        up_refs[array][slot] = dot_tn(backs[...], xs[...]).astype(BF16)
        array, slot = down_at[s]
        down_refs[array][slot] = dot_tn(acts[...], cs[...]).astype(BF16)


def feed_forward(core, own, sib, mixed_own, mixed_sib, c_own, c_sib, lines, ups, downs, bias, up_at, down_at):
    rows, width = c_own.shape
    units = bias.shape[1]

    def arrays(where):
        return [
            jax.ShapeDtypeStruct((sum(a == i for a, _ in where), units, width), BF16)
            for i in range(1 + max(a for a, _ in where))
        ]

    full = jax.ShapeDtypeStruct((2 * rows, width), F32)
    n_up = 1 + max(a for a, _ in up_at)
    vmem = pl.BlockSpec(memory_space=pltpu.VMEM)
    out = pl.pallas_call(
        functools.partial(feed_forward_kernel, len(ups), up_at, down_at),
        in_specs=[SMEM] + [vmem] * (8 + 2 * len(ups)),
        out_shape=[full] * 3 + [jax.ShapeDtypeStruct(bias.shape, F32)] + arrays(up_at) + arrays(down_at),
        scratch_shapes=[pltpu.VMEM((2 * rows, width), BF16)] * 2 + [pltpu.VMEM((2 * rows, units), BF16)] * 2,
        compiler_params=pltpu.CompilerParams(vmem_limit_bytes=VMEM_LIMIT),
        cost_estimate=pl.CostEstimate(
            flops=24 * rows * width * units * len(ups), bytes_accessed=12 * units * width * len(ups), transcendentals=0
        ),
        name="feed_forward",
    )(core, own, sib, mixed_own, mixed_sib, c_own, c_sib, lines, *ups, *downs, bias)
    return *out[:4], out[4 : 4 + n_up], out[4 + n_up :]


def local(
    groups, chips,
    hidden_in, mix_gain, mix_shift, w_query, bias_query, w_key, bias_key, w_value, bias_value, shift_taps,
    log_step, log_decay, frequency, out_real, out_imag, skip_gain, w_out, bias_out, mlp_gain, mlp_shift,
    w_up, bias_up, w_down, bias_down, cotangent, seq_blocks,
):
    rows, width = hidden_in.shape
    shard, shard_units = w_query.shape[1], w_up.shape[1]
    chans, channels = 2 * chips, chips * shard
    cut, unit_cut = shard // groups, shard_units // groups
    steps = rows // SEGS
    me_group, me_chan = lax.axis_index("group"), lax.axis_index("chan")
    me_chip, me_core = me_chan // 2, me_chan % 2
    same_core = [[2 * z + k for z in range(chips)] for k in range(2)]
    square = groups == 4

    def swap_z(x):
        return lax.all_to_all(x, "chan", 0, 0, axis_index_groups=same_core, tiled=True)

    def group_swap(x, bits):
        return lax.ppermute(x, "group", [(i, i ^ bits) for i in range(groups)])

    def sibling(x):
        return lax.ppermute(x, "chan", [(i, i ^ 1) for i in range(chans)])

    def chip_shift(x, by):
        pairs = [(i, i + 2 * by) for i in range(chans) if 0 <= i + 2 * by < chans]
        return lax.ppermute(x, "chan", pairs)

    def chip_turn(x, by):
        return lax.ppermute(x, "chan", [(i, (i + 2 * by) % chans) for i in range(chans)])

    def gather_z(x):
        return jnp.concatenate([x] + [chip_turn(x, by) for by in range(1, chips)])

    def gather_group(x):
        return [x] + [group_swap(x, r) for r in range(1, groups)]

    def add(*xs):
        return sum(x.astype(F32) for x in xs).astype(BF16)

    def fold_z(parts):
        return add(parts[0], *(chip_turn(p, -by) for by, p in enumerate(parts) if by))

    def fold_group(parts):
        return add(parts[0], *(group_swap(p, r) for r, p in enumerate(parts) if r))

    def pieces(x, count):
        n = x.shape[0] // count
        return [x[i * n : (i + 1) * n] for i in range(count)]

    def by_index(parts):
        out = []
        for g in range(groups):
            x = parts[0]
            for r in range(1, groups):
                x = jnp.where(me_group == g ^ r, parts[r], x)
            out.append(x)
        return jnp.stack(out)

    def first_round(a):
        return (group_swap(a, 1), group_swap(a, 2)) if square else tuple(gather_group(a)[1:])

    def second_round(a, one, which):
        return [a, one[0], one[1], group_swap(one[1 - which], 1 + which)] if square else [a, *one]

    def fold_first(send_a, send_b):
        return group_swap(send_a, 1), group_swap(send_b, 2)

    def fold_second(one, ay, bx):
        return group_swap(add(ay, one[0][1]), 2), group_swap(add(bx, one[1][1]), 1)

    def fold_end(one, two, a0, b0):
        return add(a0, one[0][0], two[0]), add(b0, one[1][0], two[1])

    def fence(*xs):
        return lax.optimization_barrier(xs)

    def share(x):
        return lax.dynamic_index_in_dim(x.reshape(groups, -1, width), me_group, 0, keepdims=False)

    def to_steps(x):
        return x.reshape(SEGS, steps, width).transpose(1, 0, 2).reshape(rows, width)

    def to_rows(x):
        return x.reshape(steps, SEGS, width).transpose(1, 0, 2).reshape(rows, width)

    first = seq_blocks[0, 0]
    second = first + seq_blocks[0, 1]

    def keep(block):
        starts = (block == 0) | (block == first) | (block == second)
        return jnp.where(starts, 0.0, 1.0).astype(F32)

    blocks = 4 * me_chip + jnp.arange(4)
    keeps = keep(blocks).reshape(2, 2)
    near = me_chip + jnp.stack([-jnp.arange(chips), jnp.arange(chips)])
    masks = jnp.prod(keep(4 * near[..., None] + jnp.arange(4)), axis=-1)

    def two_shares(a, b):
        return jnp.concatenate([share(a), share(b)])

    turns = (me_chip - jnp.arange(chips)) % chips
    flips = me_group ^ jnp.arange(groups)
    place = flips[None, None, :, None] * chips + turns[None, :, None, None]
    place = (place * 2 + jnp.arange(2)[:, None, None, None]) * cut + jnp.arange(cut)
    order = (place.reshape(-1, 1) == jnp.arange(2 * channels)).astype(BF16)
    z_turn = (turns[:, None] == jnp.arange(chips)).astype(F32)
    g_flip = (flips[:, None] == jnp.arange(groups)).astype(F32)
    exact = lax.Precision.HIGHEST

    core = me_core.reshape(1)
    line = lambda x: x.reshape(1, width)
    kv_z = gather_z(two_shares(w_key.T, w_value.T))
    edge = lax.ppermute(hidden_in[rows - HALO :], "chan", [(2 * z + 1, 2 * z + 3) for z in range(chips - 1)])
    own = jnp.concatenate([to_steps(hidden_in), edge])
    kv_z, own, w_query, w_out, w_up, cotangent, log_decay, frequency, out_real, out_imag = fence(
        kv_z, own, w_query, w_out, w_up, cotangent, log_decay, frequency, out_real, out_imag
    )

    mixed_kv = gather_group(kv_z)
    small = jnp.concatenate(
        [
            log_decay.T, frequency.T, out_real.T, out_imag.T, shift_taps.T,
            jnp.stack([log_step, skip_gain, bias_query, bias_key, bias_value]),
            bias_up.reshape(shard_units // shard, shard),
        ]
    )
    small = swap_z(jnp.broadcast_to(small, (chips,) + small.shape))
    sib = sibling(own)
    qo_z = gather_z(two_shares(w_query.T, w_out))
    params = jnp.moveaxis(small[:, :PARAM_ROWS], 0, 1).reshape(PARAM_ROWS, channels)
    mixed_kv, sib, qo_z, params, w_up, w_down, cotangent = fence(mixed_kv, sib, qo_z, params, w_up, w_down, cotangent)

    mixed_qo = gather_group(qo_z)
    up_z = gather_z(share(w_up.T))
    mixer = Mixer(rows, channels, width, groups)
    normed, wkv, tables, key, value, prod, shifted, er, ei, dr, di, ends, chip = mixer.before(
        core, keeps, own, sib, line(mix_gain), line(mix_shift), order, mixed_kv, params
    )
    mixed_qo, chip, ends, up_z, w_down = fence(mixed_qo, chip, ends, up_z, w_down)

    recv = [chip_shift(chip, by) for by in range(1, chips)]
    up_one = first_round(up_z)
    cot = to_steps(cotangent)
    recv, w_down, mixed_qo, cot = fence(recv, w_down, mixed_qo, cot)

    down_z = gather_z(share(w_down))
    cot_sib = sibling(cot)
    wqo, query, conv, core_low, state_r, state_i, mixed = mixer.conv(
        keeps, masks, normed, prod, er, ei, ends, recv, order, mixed_qo, params, tables
    )
    mixed, up_one, down_z, cot_sib = fence(mixed, up_one, down_z, cot_sib)

    down_one = first_round(down_z)
    mixed_sib = sibling(mixed)
    ups = second_round(up_z, up_one, 0)
    units_bias = small[:, PARAM_ROWS:].reshape(chips, groups, unit_cut)
    units_bias = jnp.einsum("kz,rg,zgu->rku", z_turn, g_flip, units_bias, precision=exact).reshape(groups, -1)
    ups, down_one, mixed_sib, units_bias = fence(ups, down_one, mixed_sib, units_bias)

    downs = second_round(down_z, down_one, 1)
    if square:
        up_at, down_at = ((0, 0), (2, 0), (1, 0), (2, 1)), ((0, 0), (1, 0), (2, 0), (2, 1))
    else:
        up_at = down_at = tuple((0, s) for s in range(groups))
    residual, branch, grad_two, grad_units_bias, grad_ups, grad_downs = feed_forward(
        core, own, sib, mixed, mixed_sib, cot, cot_sib, jnp.stack([bias_out, mlp_gain, mlp_shift]), ups, downs, units_bias,
        up_at, down_at,
    )

    grad_two_sib = sibling(grad_two)
    ff_one = fold_first(grad_ups[2], grad_downs[2]) if square else ()
    after = mixer.after(
        core, keeps, residual, grad_two, grad_two_sib, cot, cot_sib, line(mlp_gain), order, wqo, normed, query, conv,
        core_low, tables,
    )
    grad_residual, g, grad_query, *qsums, ends, chip, sums = after[:10]
    grad_qo = after[10:]
    chip, ff_one, grad_qo, branch, ends = fence(chip, ff_one, grad_qo, branch, ends)

    recv = [chip_shift(chip, -by) for by in range(1, chips)]
    ff_two = fold_second(ff_one, grad_ups[1][0], grad_downs[1][0]) if square else ()
    branch_sib = sibling(branch[rows:])
    recv, branch_sib, ff_two, grad_qo = fence(recv, branch_sib, ff_two, grad_qo)

    if square:
        ff = fold_end(ff_one, ff_two, grad_ups[0][0], grad_downs[0][0])
    else:
        ff = [fold_group(list(x[0])) for x in (grad_ups, grad_downs)]
    ff = fold_z([jnp.stack(p) for p in zip(*(pieces(x, chips) for x in ff))])
    qo = fold_group(grad_qo)
    mine = lax.dynamic_slice_in_dim(residual, me_core * rows, rows, axis=0)
    output = to_rows((mine + branch[:rows] + branch_sib + bias_down).astype(BF16))
    grad_normed, grad_params, *grad_kv = mixer.grads(
        core, keeps, masks, g, prod, qsums, (state_r, state_i), (dr, di), ends, recv, params, tables, key, value, shifted,
        grad_query, normed, order, wkv, wqo,
    )
    ff, qo, grad_kv, grad_normed, grad_params, output = fence(ff, qo, grad_kv, grad_normed, grad_params, output)

    kv = fold_group(grad_kv)
    ff = gather_group(ff)
    qo = fold_z(pieces(qo, chips))
    from_sib = sibling(grad_normed[rows:])
    edge = grad_normed[2 * rows :] + from_sib[rows:]
    edge = lax.ppermute(edge, "chan", [(2 * z + 3, 2 * z + 1) for z in range(chips - 1)])
    grad_input, sums_one = finish(grad_normed, from_sib, edge, own, grad_residual, core, line(mix_gain))
    grad_input = to_rows(grad_input)
    kv, sums_one, qo, grad_input, ff = fence(kv, sums_one, qo, grad_input, ff)

    kv = fold_z(pieces(kv, chips))
    qo = gather_group(qo)
    features = jnp.concatenate([sums_one, 0.5 * sums]).reshape(6, chips, 2, shard)
    pick = lambda core: lax.dynamic_index_in_dim(features, core, 2, keepdims=False)
    features = pick(me_core) + sibling(pick(1 - me_core))
    units_bias = grad_units_bias.reshape(groups, chips, unit_cut)
    units_bias = jnp.einsum("kz,rg,rku->zgu", z_turn, g_flip, units_bias, precision=exact)
    tail = jnp.concatenate(
        [
            grad_params.reshape(PARAM_ROWS, chips, shard),
            features,
            jnp.moveaxis(units_bias.reshape(chips, shard_units // shard, shard), 0, 1),
        ]
    )
    tail = jnp.sum(swap_z(jnp.moveaxis(tail, 1, 0)), axis=0)
    grad_wf = jnp.moveaxis(by_index(ff), 1, 0).reshape(2, shard_units, width).astype(F32)
    kv, qo, tail, grad_wf = fence(kv, qo, tail, grad_wf)

    kv = gather_group(kv)
    tail = sum(gather_group(tail))

    def halves(parts):
        x = by_index(parts).reshape(groups, 2, cut, width)
        return jnp.moveaxis(x, 1, 0).reshape(2, shard, width).astype(F32)

    (grad_wk, grad_wv), (grad_wq, grad_wo) = halves(kv), halves(qo)
    modes = [tail[i * MODES : (i + 1) * MODES].T for i in range(4)]
    biases = tail[BIAS_ROW:PARAM_ROWS]
    feat_part = tail[PARAM_ROWS : PARAM_ROWS + 6]
    sum_bias_up = tail[PARAM_ROWS + 6 :].reshape(shard_units)
    return (
        output,
        grad_input,
        feat_part[0],
        feat_part[1],
        grad_wq.T,
        biases[0],
        grad_wk.T,
        biases[1],
        grad_wv.T,
        biases[2],
        tail[TAP_ROW : TAP_ROW + TAPS].T,
        tail[STEP_ROW],
        modes[0],
        modes[1],
        modes[2],
        modes[3],
        tail[SKIP_ROW],
        grad_wo,
        feat_part[2],
        feat_part[3],
        feat_part[4],
        grad_wf[0].T,
        sum_bias_up,
        grad_wf[1],
        feat_part[5],
    )


def solution(mesh):
    rows = P(("group", "chan"), None)
    columns, channels, vector, copied = P(None, "chan"), P("chan", None), P("chan"), P()
    return jax.shard_map(
        functools.partial(local, mesh.shape["group"], mesh.shape["chan"] // 2),
        mesh=mesh,
        in_specs=(
            rows, copied, copied, columns, vector, columns, vector, columns, vector, channels,
            vector, channels, channels, channels, channels, vector, channels, copied, copied, copied,
            columns, vector, channels, copied, rows, P("group", None),
        ),
        out_specs=(
            rows, rows, vector, vector, columns, vector, columns, vector, columns, vector,
            channels, vector, channels, channels, channels, channels, vector, channels, vector, vector,
            vector, columns, vector, channels, vector,
        ),
        check_vma=False,
    )
```

```python
import functools

import jax
import jax.numpy as jnp
import numpy as np
from jax import lax
from jax.experimental import pallas as pl
from jax.experimental.pallas import tpu as pltpu
from jax.sharding import PartitionSpec as P

F32 = jnp.float32
BF16 = jnp.bfloat16
MODES = 32
LANES = 128
SEGS = 8
TAPS = 4
BLOCK = 8
HALO = 16
TILE = 128
LN_TILE = 64
EPSILON = 1e-05
VMEM_LIMIT = 60 * 1024 * 1024
SMEM = pl.BlockSpec(memory_space=pltpu.SMEM)

TAP_ROW = 4 * MODES
STEP_ROW = TAP_ROW + TAPS
SKIP_ROW = STEP_ROW + 1
BIAS_ROW = SKIP_ROW + 1
PARAM_ROWS = BIAS_ROW + 3


def ssm_tables(log_step, log_decay, frequency, out_real, out_imag):
    step_size = jnp.exp(log_step)
    rate = -jnp.exp(log_decay)
    decay = rate * step_size
    turn = frequency * step_size
    growth = jnp.exp(decay)
    ratio_re = growth * jnp.cos(turn) - 1.0
    ratio_im = growth * jnp.sin(turn)
    denom = rate * rate + frequency * frequency
    scaled_re = (ratio_re * rate + ratio_im * frequency) / denom
    scaled_im = (ratio_im * rate - ratio_re * frequency) / denom
    weight_re = out_real * scaled_re - out_imag * scaled_im
    weight_im = out_real * scaled_im + out_imag * scaled_re
    return decay, turn, weight_re, weight_im


def table_inputs(params):
    parts = [params[pl.ds(i * MODES, MODES), :] for i in range(4)]
    return [params[pl.ds(STEP_ROW, 1), :], *parts]


def read_tables(tables):
    return [tables[pl.ds(i * MODES, MODES), :] for i in range(4)]


def dot_nn(a, b):
    return lax.dot_general(a, b, (((1,), (0,)), ((), ())), preferred_element_type=F32)


def dot_nt(a, b):
    return lax.dot_general(a, b, (((1,), (1,)), ((), ())), preferred_element_type=F32)


def dot_tn(a, b):
    return lax.dot_general(a, b, (((0,), (0,)), ((), ())), preferred_element_type=F32)


def cmul(ar, ai, br, bi):
    return ar * br - ai * bi, ar * bi + ai * br


def normalize(values):
    center = values - jnp.mean(values, axis=-1, keepdims=True)
    scale = lax.rsqrt(jnp.mean(center * center, axis=-1, keepdims=True) + EPSILON)
    return center * scale, scale


def normalize_back(grad, gain, xhat, scale):
    gy = grad * gain
    mean_gy = jnp.mean(gy, axis=-1, keepdims=True)
    mean_gx = jnp.mean(gy * xhat, axis=-1, keepdims=True)
    return scale * (gy - mean_gy - xhat * mean_gx)


def fill_powers(zr, zi, pr, pi, steps):
    ar, ai = jnp.ones_like(zr), jnp.zeros_like(zi)
    pr[pl.ds(0, MODES), :] = ar
    pi[pl.ds(0, MODES), :] = ai
    for j in range(1, steps + 1):
        ar, ai = cmul(ar, ai, zr, zi)
        pr[pl.ds(j * MODES, MODES), :] = ar
        pi[pl.ds(j * MODES, MODES), :] = ai
    return ar, ai


def over_chunk(ar, ai):
    n = 1
    while n < SEGS:
        ar, ai = cmul(ar, ai, ar, ai)
        n *= 2
    return ar, ai


def fill_kern(wr, wi, pr, pi, kern, steps):
    for j in range(steps):
        v = wr * pr[pl.ds(j * MODES, MODES), :] - wi * pi[pl.ds(j * MODES, MODES), :]
        kern[pl.ds(j, 1), :] = 2.0 * jnp.sum(v, axis=0, keepdims=True)


def row(ref, i):
    return jnp.broadcast_to(ref[pl.ds(i, 1), :], (SEGS, LANES))


def group(ref, steps, c, t):
    return ref[pl.ds((c * steps + t) * SEGS, SEGS), :]


def put(ref, steps, c, t, value):
    ref[pl.ds((c * steps + t) * SEGS, SEGS), :] = value


def put_low(ref, steps, c, t, pair):
    ref[pl.ds((c * steps + t) * SEGS, 2 * SEGS), :] = jnp.concatenate(pair).astype(BF16)


def sublanes():
    return lax.broadcasted_iota(jnp.int32, (SEGS, LANES), 0)


def seg_mask(keep0, keep4):
    ids = sublanes()
    m = jnp.where(ids == 0, keep0, 1.0)
    return jnp.where(ids == SEGS // 2, keep4, m)


def seg_rows(c, k):
    return pl.ds(c * MODES * SEGS + k, MODES, stride=SEGS)


def mode_rows(c, m):
    return pl.ds(pl.multiple_of(c * MODES * SEGS + m * SEGS, SEGS), SEGS)


def weigh(pr, pi, steps, order, power, last, data, outs):
    outs_r, outs_i, runs_r, runs_i = outs
    half = steps // 2
    for part in range(2):
        ts = order[part * half : (part + 1) * half]
        values = [[data(c, t) for t in ts] for c in range(2)]

        def per_mode(m, carry):
            acc = []
            for c in range(2):
                if part == 0:
                    acc.append([jnp.zeros((SEGS, LANES), F32)] * 4)
                else:
                    acc.append([r[mode_rows(c, m), :] for r in (outs_r, outs_i, runs_r, runs_i)])
            for i, t in enumerate(ts):
                a, b = row(pr, power(t) * MODES + m), row(pi, power(t) * MODES + m)
                for c in range(2):
                    sr, si, tr, ti = acc[c]
                    sr, si = sr + a * values[c][i], si + b * values[c][i]
                    if last or t != order[-1]:
                        tr, ti = tr + sr, ti + si
                    acc[c] = [sr, si, tr, ti]
            for c in range(2):
                for r, v in zip((outs_r, outs_i, runs_r, runs_i), acc[c]):
                    r[mode_rows(c, m), :] = v
            return carry

        lax.fori_loop(0, MODES, per_mode, 0, unroll=2)


def unfold(pr, pi, steps, power, states, base, done):
    half = steps // 2
    for part in range(2):
        ts = range(part * half, (part + 1) * half)
        init = tuple(base(c, t) for c in range(2) for t in ts)

        def per_mode(m, acc):
            acc = list(acc)
            u = [states[0][mode_rows(c, m), :] for c in range(2)]
            v = [states[1][mode_rows(c, m), :] for c in range(2)]
            for i, t in enumerate(ts):
                a, b = row(pr, power(t) * MODES + m), row(pi, power(t) * MODES + m)
                for c in range(2):
                    at = c * half + i
                    acc[at] = acc[at] + (a * u[c] - b * v[c])
            return tuple(acc)

        acc = lax.fori_loop(0, MODES, per_mode, init, unroll=2)
        for c in range(2):
            for i in range(0, half, 2):
                done(c, ts[i], acc[c * half + i : c * half + i + 2])


def lags_apply(kern, steps, base, source, out, adjoint):
    n = steps // BLOCK
    for tb in range(n):
        ts = range(tb * BLOCK, (tb + 1) * BLOCK)
        ys = {(c, t): base(c, t) for c in range(2) for t in ts}
        for sb in range(tb, n) if adjoint else range(tb + 1):
            ss = range(sb * BLOCK, (sb + 1) * BLOCK)
            xs = {(c, s): source(c, s) for c in range(2) for s in ss}
            for lag in range(steps):
                pairs = [(t, s) for t in ts for s in ss if (s - t if adjoint else t - s) == lag]
                if pairs:
                    k = row(kern, lag)
                    for t, s in pairs:
                        for c in range(2):
                            ys[c, t] = ys[c, t] + k * xs[c, s]
        for (c, t), y in ys.items():
            put(out, steps, c, t, y)


def lag_sums(steps, left, right):
    n = steps // BLOCK
    sums = []
    for jb in range(n):
        acc = [jnp.zeros((SEGS, LANES), F32)] * BLOCK
        for c in range(2):
            for tb in range(jb, n):
                ts = range(tb * BLOCK, (tb + 1) * BLOCK)
                base = (tb - jb) * BLOCK
                xs = {s: right(c, s) for s in range(max(base - BLOCK + 1, 0), base + BLOCK)}
                for t in ts:
                    g = left(c, t)
                    for j in range(BLOCK):
                        s = t - jb * BLOCK - j
                        if s >= 0:
                            acc[j] = acc[j] + g * xs[s]
        sums.extend(jnp.sum(a, axis=0, keepdims=True) for a in acc)
    return sums


def earlier_keys(key, steps, keeps):
    ids = sublanes()
    out = []
    rolled = None
    for c in range(2):
        mask = seg_mask(keeps[c, 0], keeps[c, 1])
        new, windows = [], []
        for back in (1, 2, 3):
            v = pltpu.roll(group(key, steps, c, steps - back), 1, 0)
            new.append(v)
            before = row(key, 2 * steps * SEGS + HALO - back) if c == 0 else rolled[back - 1]
            windows.append(jnp.where(ids == 0, before, v) * mask)
        rolled = new
        out.append(windows)
    return out


def chunk_of(own, sib, core, c, at):
    return jnp.where(core == c, own[at, :].astype(F32), sib[at, :].astype(F32))


def join(parts, out):
    at = 0
    for p in parts:
        n = p.shape[0]
        out[pl.ds(at, n), :] = p[...]
        at += n


def part_to(outs, value):
    at = 0
    for o in outs:
        n = o.shape[0]
        o[...] = value[at : at + n].astype(BF16)
        at += n


def before_kernel(steps, n_parts, core, keeps, own, sib, gain, shift, order, *refs):
    mixed_kv, params = refs[:n_parts], refs[n_parts]
    normed, wkv, tables, kern, key, value, prod, shifted, er, ei, dr, di, ends, chip, pr, pi, joined = refs[n_parts + 1 :]
    lane = pl.program_id(0)
    rows = steps * SEGS
    channels = wkv.shape[0] // 2

    @pl.when(lane == 0)
    def _():
        me = core[0]
        join(mixed_kv, joined)
        wkv[...] = dot_nn(order[...], joined[...]).astype(BF16)

        def rows_of(x):
            xhat, _ = normalize(x)
            return (xhat * gain[...] + shift[...]).astype(BF16)

        for c in range(2):
            for r in range(0, rows, LN_TILE):
                normed[pl.ds(c * rows + r, LN_TILE), :] = rows_of(chunk_of(own, sib, me, c, pl.ds(r, LN_TILE)))
        normed[pl.ds(2 * rows, HALO), :] = rows_of(chunk_of(own, sib, me, 1, pl.ds(rows, HALO)))

    decay, turn, wr, wi = ssm_tables(*table_inputs(params))
    mag = jnp.exp(decay)
    zr, zi = mag * jnp.cos(turn), mag * jnp.sin(turn)
    for i, v in enumerate((zr, zi, wr, wi)):
        tables[pl.ds(i * MODES, MODES), :] = v
    ar, ai = fill_powers(zr, zi, pr, pi, steps)
    fill_kern(wr, wi, pr, pi, kern, steps)
    at = pl.ds(pl.multiple_of(lane * LANES, LANES), LANES)
    also = pl.ds(pl.multiple_of(channels + lane * LANES, LANES), LANES)
    key[...] = dot_nt(normed[...], wkv[at, :]) + params[pl.ds(BIAS_ROW + 1, 1), :]
    value[...] = dot_nt(normed[pl.ds(0, 2 * rows), :], wkv[also, :]) + params[pl.ds(BIAS_ROW + 2, 1), :]
    tap = [row(params, TAP_ROW + j) for j in range(TAPS)]
    windows = earlier_keys(key, steps, keeps)
    for c in range(2):
        window = windows[c]
        for t in range(steps):
            cur = group(key, steps, c, t)
            s = tap[0] * cur + tap[1] * window[0] + tap[2] * window[1] + tap[3] * window[2]
            window = [cur] + window[:2]
            put(shifted, steps, c, t, s)
            put(prod, steps, c, t, s * group(value, steps, c, t))
    weigh(
        pr, pi, steps, list(range(steps)), lambda t: steps - 1 - t, False,
        lambda c, t: group(prod, steps, c, t), (er, ei, dr, di),
    )
    states = []
    for c in range(2):
        k4 = keeps[c, 1]
        sr = si = jnp.zeros((MODES, LANES), F32)
        for k in range(SEGS):
            if k == SEGS // 2:
                sr, si = sr * k4, si * k4
            cr, ci = cmul(sr, si, ar, ai)
            sr = cr + er[seg_rows(c, k), :]
            si = ci + ei[seg_rows(c, k), :]
        states.append((sr, si))
    ends[pl.ds(0, MODES), :], ends[pl.ds(MODES, MODES), :] = states[0]
    br, bi = over_chunk(ar, ai)
    cr, ci = cmul(*states[0], br, bi)
    keep = keeps[1, 0] * keeps[1, 1]
    chip[pl.ds(0, MODES), :] = (cr * keep + states[1][0]).astype(BF16)
    chip[pl.ds(MODES, MODES), :] = (ci * keep + states[1][1]).astype(BF16)


def incoming(ref_list, masks, which, ar, ai):
    br, bi = cmul(ar, ai, ar, ai)
    read = lambda r: (r[pl.ds(0, MODES), :].astype(F32), r[pl.ds(MODES, MODES), :].astype(F32))
    sr, si = read(ref_list[-1])
    for by in range(len(ref_list) - 1, 0, -1):
        m = masks[which, by]
        cr, ci = cmul(sr, si, br * m, bi * m)
        rr, ri = read(ref_list[by - 1])
        sr, si = cr + rr, ci + ri
    return sr, si


def near_kernel(steps, n_parts, normed, prod, *refs):
    mixed_qo = refs[:n_parts]
    order, params, kern, wqo, query, near, joined = refs[n_parts:]
    lane = pl.program_id(0)
    rows = steps * SEGS

    @pl.when(lane == 0)
    def _():
        join(mixed_qo, joined)
        wqo[...] = dot_nn(order[...], joined[...]).astype(BF16)

    at = pl.ds(pl.multiple_of(lane * LANES, LANES), LANES)
    query[...] = dot_nt(normed[pl.ds(0, 2 * rows), :], wqo[at, :]) + params[pl.ds(BIAS_ROW, 1), :]
    source = lambda c, t: group(prod, steps, c, t)
    sk = row(params, SKIP_ROW)
    lags_apply(kern, steps, lambda c, t: sk * source(c, t), source, near, False)


def conv_kernel(steps, n_recv, keeps, masks, near, query, er, ei, ends, *refs):
    recv = refs[:n_recv]
    wo, tables, conv, core_low, state_r, state_i, mixed_low, pr, pi, twice_r, twice_i, mixed = refs[n_recv:]
    lane = pl.program_id(0)
    zr, zi, wr, wi = read_tables(tables)
    ar, ai = fill_powers(zr, zi, pr, pi, steps)
    w2r, w2i = 2.0 * wr, 2.0 * wi
    br, bi = over_chunk(ar, ai)
    sr, si = incoming(recv, masks, 0, br, bi)
    for c in range(2):
        if c == 1:
            sr, si = cmul(first_r, first_i, br * keeps[0, 1], bi * keeps[0, 1])
            sr, si = sr + ends[pl.ds(0, MODES), :], si + ends[pl.ds(MODES, MODES), :]
        sr, si = sr * keeps[c, 0], si * keeps[c, 0]
        first_r, first_i = sr, si
        for k in range(SEGS):
            if k == SEGS // 2:
                sr, si = sr * keeps[c, 1], si * keeps[c, 1]
            state_r[seg_rows(c, k), :] = sr
            state_i[seg_rows(c, k), :] = si
            twice_r[seg_rows(c, k), :], twice_i[seg_rows(c, k), :] = cmul(w2r, w2i, sr, si)
            if k < SEGS - 1:
                cr, ci = cmul(sr, si, ar, ai)
                sr = cr + er[seg_rows(c, k), :]
                si = ci + ei[seg_rows(c, k), :]

    def done(c, t, values):
        low = []
        for i, v in zip((t, t + 1), values):
            put(conv, steps, c, i, v)
            low.append(v * group(query, steps, c, i))
        put_low(core_low, steps, c, t, low)

    unfold(pr, pi, steps, lambda t: t + 1, (twice_r, twice_i), lambda c, t: group(near, steps, c, t), done)
    out = dot_nn(core_low[...], wo[...])

    @pl.when(lane == 0)
    def _():
        mixed[...] = out

    @pl.when(jnp.logical_and(lane > 0, lane < pl.num_programs(0) - 1))
    def _():
        mixed[...] += out

    @pl.when(lane == pl.num_programs(0) - 1)
    def _():
        mixed_low[...] = (mixed[...] + out).astype(BF16)


def after_kernel(
    steps, core, keeps, residual, grad_own, grad_sib, cot_own, cot_sib, gain, order, wo, normed, query, conv, core_low,
    tables, grad_residual, g, grad_query, qr, qi, rr, ri, ends, chip, sums, *refs,
):
    grad_qo, (pr, pi, low, grad_core, grad_w) = refs[:-5], refs[-5:]
    lane = pl.program_id(0)
    rows = steps * SEGS
    channels = grad_w.shape[0] // 2

    @pl.when(lane == 0)
    def _():
        me = core[0]
        total = [jnp.zeros((1, low.shape[1]), F32)] * 4
        for c in range(2):
            for r in range(0, rows, LN_TILE):
                at = pl.ds(c * rows + r, LN_TILE)
                xhat, scale = normalize(residual[at, :])
                grad = grad_own[at, :].astype(F32) + grad_sib[at, :].astype(F32)
                cot = chunk_of(cot_own, cot_sib, me, c, pl.ds(r, LN_TILE))
                out = cot + normalize_back(grad, gain[...], xhat, scale)
                grad_residual[at, :] = out
                low[at, :] = out.astype(BF16)
                for i, v in enumerate((out, grad * xhat, grad, cot)):
                    total[i] = total[i] + jnp.sum(v, axis=0, keepdims=True)
        sums[...] = jnp.concatenate(total, axis=0)

    zr, zi, wr, wi = read_tables(tables)
    ar, ai = fill_powers(zr, zi, pr, pi, steps)
    grad_core[...] = dot_nt(low[...], wo[...])
    for c in range(2):
        for t in range(0, steps, 2):
            pair = []
            for i in (t, t + 1):
                d = group(grad_core, steps, c, i)
                put(g, steps, c, i, d * group(query, steps, c, i))
                pair.append(d * group(conv, steps, c, i))
            put_low(grad_query, steps, c, t, pair)
    at = pl.ds(pl.multiple_of(lane * LANES, LANES), LANES)
    also = pl.ds(pl.multiple_of(channels + lane * LANES, LANES), LANES)
    grad_w[at, :] = dot_tn(grad_query[...], normed[pl.ds(0, 2 * rows), :]).astype(BF16)
    grad_w[also, :] = dot_tn(core_low[...], low[...]).astype(BF16)

    @pl.when(lane == pl.num_programs(0) - 1)
    def _():
        part_to(grad_qo, dot_tn(order[...], grad_w[...]))

    weigh(
        pr, pi, steps, list(reversed(range(steps))), lambda t: t + 1, True,
        lambda c, t: group(g, steps, c, t), (qr, qi, rr, ri),
    )
    w2r, w2i = 2.0 * wr, 2.0 * wi
    lr = li = jnp.zeros((MODES, LANES), F32)
    for c in (1, 0):
        for k in reversed(range(SEGS)):
            cr, ci = cmul(lr, li, ar, ai)
            ur, ui = cmul(w2r, w2i, qr[seg_rows(c, k), :], qi[seg_rows(c, k), :])
            lr, li = ur + cr, ui + ci
            if k == SEGS // 2:
                lr, li = lr * keeps[c, 1], li * keeps[c, 1]
        lr, li = lr * keeps[c, 0], li * keeps[c, 0]
        if c == 1:
            ends[pl.ds(0, MODES), :] = lr
            ends[pl.ds(MODES, MODES), :] = li
    chip[pl.ds(0, MODES), :] = lr.astype(BF16)
    chip[pl.ds(MODES, MODES), :] = li.astype(BF16)


def near_back_kernel(steps, g, prod, params, kern, near, lags):
    source = lambda c, t: group(g, steps, c, t)
    other = lambda c, t: group(prod, steps, c, t)
    sk = row(params, SKIP_ROW)
    for j, lag in enumerate(lag_sums(steps, source, other)):
        lags[pl.ds(j, 1), :] = lag
    dsk = jnp.zeros((SEGS, LANES), F32)
    for c in range(2):
        for t in range(steps):
            dsk = dsk + source(c, t) * other(c, t)
    lags[pl.ds(steps, 1), :] = jnp.sum(dsk, axis=0, keepdims=True)
    lags_apply(kern, steps, lambda c, t: sk * source(c, t), source, near, True)


def grads_kernel(steps, n_recv, base, last, core, keeps, masks, near, lags, qr, qi, rr, ri, state_r, state_i, dr, di, ends, *refs):
    recv = refs[:n_recv]
    params, tables, key, value, shifted, grad_query, normed, wk, wv, wq = refs[n_recv : n_recv + 10]
    refs = refs[n_recv + 10 :]
    if last:
        order, before_keep, before_send, before_w, *refs = refs
        grad_keep, grad_send, grad_params, *grad_kv = refs[:-8]
        pr, pi, mur, mui, back, cat, cat_w, grad_w = refs[-8:]
    else:
        before_keep = before_send = None
        grad_keep, grad_send, grad_params, grad_w, pr, pi, mur, mui, back, cat, cat_w = refs
    lane = pl.program_id(0)
    rows = steps * SEGS
    channels = grad_w.shape[0] // 2
    ids = sublanes()
    zr, zi, wr, wi = read_tables(tables)
    ar, ai = fill_powers(zr, zi, pr, pi, steps)
    w2r, w2i = 2.0 * wr, 2.0 * wi
    br, bi = over_chunk(ar, ai)
    mr, mi = incoming(recv, masks, 1, br, bi)
    zero = jnp.zeros((MODES, LANES), F32)
    awr = awi = azr = azi = acr = aci = zero
    for c in (1, 0):
        if c == 0:
            keep = keeps[1, 0] * keeps[1, 1]
            mr, mi = cmul(last_r, last_i, br * keep, bi * keep)
            mr, mi = mr + ends[pl.ds(0, MODES), :], mi + ends[pl.ds(MODES, MODES), :]
        last_r, last_i = mr, mi
        for k in reversed(range(SEGS)):
            at = seg_rows(c, k)
            mur[at, :] = mr
            mui[at, :] = mi
            s_r, s_i = state_r[at, :], state_i[at, :]
            q_r, q_i = qr[at, :], qi[at, :]
            u = cmul(s_r, s_i, q_r, q_i)
            awr, awi = awr + u[0], awi + u[1]
            u = cmul(s_r, s_i, rr[at, :], ri[at, :])
            azr, azi = azr + u[0], azi + u[1]
            u = cmul(mr, mi, dr[at, :], di[at, :])
            acr, aci = acr + u[0], aci + u[1]
            u = cmul(mr, mi, s_r, s_i)
            u = cmul(u[0], u[1], ar, ai)
            acr, aci = acr + float(steps) * u[0], aci + float(steps) * u[1]
            if k > 0:
                ur, ui = cmul(w2r, w2i, q_r, q_i)
                cr, ci = cmul(mr, mi, ar, ai)
                mr, mi = ur + cr, ui + ci
                if k == SEGS // 2:
                    mr, mi = mr * keeps[c, 1], mi * keeps[c, 1]
    for j in range(steps):
        lag = lags[pl.ds(j, 1), :]
        u, v = pr[pl.ds(j * MODES, MODES), :] * lag, pi[pl.ds(j * MODES, MODES), :] * lag
        awr, awi = awr + u, awi + v
        azr, azi = azr + float(j) * u, azi + float(j) * v
    u = cmul(w2r, w2i, azr, azi)
    _, tables_back = jax.vjp(ssm_tables, *table_inputs(params))
    dstep, *dmodes = tables_back((u[0] + acr, -(u[1] + aci), 2.0 * awr, -2.0 * awi))
    for i, v in enumerate(dmodes):
        grad_params[pl.ds(i * MODES, MODES), :] = v
    grad_params[pl.ds(STEP_ROW, 1), :] = dstep
    grad_params[pl.ds(SKIP_ROW, 1), :] = lags[pl.ds(steps, 1), :]

    def done(c, t, values):
        low = []
        for i, v in zip((t, t + 1), values):
            low.append(v * group(shifted, steps, c, i))
            put(back, steps, c, i, v * group(value, steps, c, i))
        cat[pl.ds((c * steps + t) * SEGS, 2 * SEGS), pl.ds(LANES, LANES)] = jnp.concatenate(low).astype(BF16)

    unfold(pr, pi, steps, lambda t: steps - 1 - t, (mur, mui), lambda c, t: group(near, steps, c, t), done)
    tap = [row(params, TAP_ROW + j) for j in range(TAPS)]
    windows = earlier_keys(key, steps, keeps)
    acc = [jnp.zeros((SEGS, LANES), F32)] * TAPS
    for c in range(2):
        window = windows[c]
        for t in range(steps):
            cur = group(key, steps, c, t)
            v = group(back, steps, c, t)
            for j, w in enumerate([cur] + window):
                acc[j] = acc[j] + v * w
            window = [cur] + window[:2]
    for j, a in enumerate(acc):
        grad_params[pl.ds(TAP_ROW + j, 1), :] = jnp.sum(a, axis=0, keepdims=True)
    following = [jnp.zeros((SEGS, LANES), F32)] * (TAPS - 1)
    for c in (1, 0):
        mask = seg_mask(keeps[c, 0], keeps[c, 1])
        begin = [group(back, steps, c, t) * mask for t in range(TAPS - 1)]
        later = [pltpu.roll(jnp.where(ids == 0, f, v), SEGS - 1, 0) for f, v in zip(following, begin)]
        following = begin
        ext = lambda t: group(back, steps, c, t) if t < steps else later[t - steps]
        for t in range(0, steps, 2):
            low = [
                tap[0] * ext(i) + tap[1] * ext(i + 1) + tap[2] * ext(i + 2) + tap[3] * ext(i + 3) for i in (t, t + 1)
            ]
            cat[pl.ds((c * steps + t) * SEGS, 2 * SEGS), pl.ds(0, LANES)] = jnp.concatenate(low).astype(BF16)
    edge = [jnp.zeros((HALO - TAPS + 1, LANES), F32)]
    for b in (3, 2, 1):
        v = jnp.zeros((1, LANES), F32)
        for j in range(b, TAPS):
            v = v + params[pl.ds(TAP_ROW + j, 1), :] * following[j - b][0:1, :]
        edge.append(v)
    halo_at = pl.ds(2 * rows, HALO)
    cat[halo_at, pl.ds(0, LANES)] = jnp.concatenate(edge, axis=0).astype(BF16)
    cat[halo_at, pl.ds(LANES, 2 * LANES)] = jnp.zeros((HALO, 2 * LANES), BF16)
    cat[pl.ds(0, 2 * rows), pl.ds(2 * LANES, LANES)] = grad_query[...]
    for i, w in enumerate((wk, wv, wq)):
        cat_w[pl.ds(i * LANES, LANES), :] = w[...]
    both = dot_tn(cat[:, pl.ds(0, 2 * LANES)], normed[...])
    if last:

        @pl.when(lane == 0)
        def _():
            grad_w[...] = before_w[...]

    at = (base + lane) * LANES
    grad_w[pl.ds(pl.multiple_of(at, LANES), LANES), :] = both[:LANES].astype(BF16)
    grad_w[pl.ds(pl.multiple_of(channels + at, LANES), LANES), :] = both[LANES:].astype(BF16)
    if last:

        @pl.when(lane == pl.num_programs(0) - 1)
        def _():
            part_to(grad_kv, dot_tn(order[...], grad_w[...]))

    for i, part in enumerate((2, 0, 1)):
        grad_params[pl.ds(BIAS_ROW + i, 1), :] = jnp.sum(cat[:, pl.ds(part * LANES, LANES)].astype(F32), axis=0, keepdims=True)
    me = core[0]
    for c in range(2):
        out = dot_nn(cat[pl.ds(c * rows, rows), :], cat_w[...])

        @pl.when(me == c)
        def _():
            add_to(grad_keep, pl.ds(0, rows), out, lane, before_keep)

        @pl.when(me != c)
        def _():
            add_to(grad_send, pl.ds(0, rows), out, lane, before_send)

    add_to(grad_send, pl.ds(rows, HALO), dot_nn(cat[halo_at, :], cat_w[...]), lane, before_send)


def add_to(ref, at, value, step, before):
    @pl.when(step == 0)
    def _():
        ref[at, :] = value if before is None else before[at, :] + value

    @pl.when(step > 0)
    def _():
        ref[at, :] += value


class Mixer:
    def __init__(self, rows, channels, width, groups):
        self.rows, self.channels, self.width, self.groups = rows, channels, width, groups
        self.steps = rows // SEGS

    def lanes(self, rows):
        return pl.BlockSpec((rows, LANES), lambda l: (0, l))

    def whole(self, *shape):
        return pl.BlockSpec(shape, lambda l: (0,) * len(shape))

    def shape(self, rows, kind=F32):
        return jax.ShapeDtypeStruct((rows, self.channels), kind)

    def wide(self, rows, kind):
        return jax.ShapeDtypeStruct((rows, self.width), kind)

    def call(self, name, kernel, in_specs, outs, scratch, work, powers=True, count=None):
        table = pltpu.VMEM(((self.steps + 1) * MODES, LANES), F32)
        return pl.pallas_call(
            kernel,
            grid=(count or self.channels // LANES,),
            in_specs=in_specs,
            out_specs=[s for s, _ in outs],
            out_shape=[s for _, s in outs],
            scratch_shapes=[table, table] * powers + scratch,
            compiler_params=pltpu.CompilerParams(vmem_limit_bytes=VMEM_LIMIT),
            cost_estimate=pl.CostEstimate(flops=work // 10000, bytes_accessed=work // 4000000, transcendentals=0),
            name=name,
        )

    def units(self, part=0):
        return pl.BlockSpec((LANES, self.width), lambda l: (l + part * self.channels // LANES, 0))

    def pair(self):
        n = 2 * self.channels
        return self.whole(n, self.width), self.wide(n, BF16)

    def parts(self):
        n = 2 * self.channels // self.groups
        return [(self.whole(n, self.width), self.wide(n, BF16))] * self.groups

    def order(self):
        return self.whole(2 * self.channels, 2 * self.channels)

    def before(self, core, keeps, own, sib, gain, shift, order, mixed_kv, params):
        n, ms, w = 2 * self.rows, 2 * MODES * SEGS, self.width
        line, states, ends = self.whole(1, w), (self.lanes(ms), self.shape(ms)), self.lanes(2 * MODES)
        return self.call(
            "ssm_before",
            functools.partial(before_kernel, self.steps, len(mixed_kv)),
            [SMEM, SMEM, self.whole(*own.shape), self.whole(*own.shape), line, line, self.order()]
            + [self.whole(*p.shape) for p in mixed_kv] + [self.lanes(PARAM_ROWS)],
            [(self.whole(n + HALO, w), self.wide(n + HALO, BF16)), self.pair(), (self.lanes(4 * MODES), self.shape(4 * MODES))]
            + [(self.lanes(self.steps), self.shape(self.steps))]
            + [(self.lanes(n + HALO), self.shape(n + HALO))] + [(self.lanes(n), self.shape(n))] * 3 + [states] * 4
            + [(ends, self.shape(2 * MODES)), (ends, self.shape(2 * MODES, BF16))],
            [pltpu.VMEM((2 * self.channels, w), BF16)],
            10**10,
        )(core, keeps, own, sib, gain, shift, order, *mixed_kv, params)

    def near(self, normed, prod, mixed_qo, order, params, kern):
        n, w = 2 * self.rows, self.width
        big = self.lanes(n)
        return self.call(
            "ssm_near",
            functools.partial(near_kernel, self.steps, len(mixed_qo)),
            [self.whole(*normed.shape), big] + [self.whole(*p.shape) for p in mixed_qo]
            + [self.order(), self.lanes(PARAM_ROWS), self.lanes(self.steps)],
            [self.pair(), (big, self.shape(n)), (big, self.shape(n))],
            [pltpu.VMEM((2 * self.channels, w), BF16)],
            6 * 10**9,
            False,
        )(normed, prod, *mixed_qo, order, params, kern)

    def conv(self, keeps, masks, near, query, er, ei, ends, recv, wqo, tables):
        n, ms, w = 2 * self.rows, 2 * MODES * SEGS, self.width
        big, states, last = self.lanes(n), self.lanes(ms), self.lanes(2 * MODES)
        return self.call(
            "ssm_conv",
            functools.partial(conv_kernel, self.steps, len(recv)),
            [SMEM, SMEM, big, big, states, states] + [last] * (1 + len(recv)) + [self.units(1), self.lanes(4 * MODES)],
            [(big, self.shape(n)), (big, self.shape(n, BF16))] + [(states, self.shape(ms))] * 2
            + [(self.whole(n, w), self.wide(n, BF16))],
            [pltpu.VMEM((ms, LANES), F32)] * 2 + [pltpu.VMEM((n, w), F32)],
            10**10,
        )(keeps, masks, near, query, er, ei, ends, *recv, wqo, tables)

    def after(
        self, core, keeps, residual, grad_own, grad_sib, cot_own, cot_sib, gain, order, wqo, normed, query, conv, core_low,
        tables,
    ):
        n, ms, w = 2 * self.rows, 2 * MODES * SEGS, self.width
        big, states, last = self.lanes(n), self.lanes(ms), self.lanes(2 * MODES)
        full, half = self.whole(n, w), self.whole(n // 2, w)
        return self.call(
            "ssm_after",
            functools.partial(after_kernel, self.steps),
            [SMEM, SMEM, full, full, full, half, half, self.whole(1, w), self.order(), self.units(1), self.whole(*normed.shape)]
            + [big] * 3 + [self.lanes(4 * MODES)],
            [(full, self.wide(n, F32)), (big, self.shape(n)), (big, self.shape(n, BF16))]
            + [(states, self.shape(ms))] * 4 + [(last, self.shape(2 * MODES)), (last, self.shape(2 * MODES, BF16))]
            + [(self.whole(4, w), self.wide(4, F32))] + self.parts(),
            [pltpu.VMEM((n, w), BF16), pltpu.VMEM((n, LANES), F32), pltpu.VMEM((2 * self.channels, w), BF16)],
            10**10,
        )(
            core, keeps, residual, grad_own, grad_sib, cot_own, cot_sib, gain, order, wqo, normed, query, conv, core_low,
            tables,
        )

    def near_back(self, g, prod, params, kern):
        big = self.lanes(2 * self.rows)
        tall = self.steps + SEGS
        return self.call(
            "ssm_near_back",
            functools.partial(near_back_kernel, self.steps),
            [big, big, self.lanes(PARAM_ROWS), self.lanes(self.steps)],
            [(big, self.shape(2 * self.rows)), (self.lanes(tall), self.shape(tall))],
            [],
            8 * 10**9,
            False,
        )(g, prod, params, kern)

    def grads(
        self, base, count, core, keeps, masks, near, lags, q, state, d, ends, recv, params, tables, key, value, shifted,
        grad_query, normed, wkv, wqo, order, before,
    ):
        n, ms, w = 2 * self.rows, 2 * MODES * SEGS, self.width
        lanes = lambda rows: pl.BlockSpec((rows, LANES), lambda l: (0, l + base))
        units = lambda part: pl.BlockSpec((LANES, w), lambda l: (l + base + part * self.channels // LANES, 0))
        big, states, ends_at = lanes(n), lanes(ms), lanes(2 * MODES)
        normed_at = [(self.whole(r, w), self.wide(r, F32)) for r in (self.rows, self.rows + HALO)]
        params_at = (lanes_from(PARAM_ROWS), jax.ShapeDtypeStruct((PARAM_ROWS, count * LANES), F32))
        last = before is not None
        return self.call(
            "ssm_grads_last" if last else "ssm_grads",
            functools.partial(grads_kernel, self.steps, len(recv), base, last),
            [SMEM, SMEM, SMEM, big, lanes(lags.shape[0])] + [states] * 8 + [ends_at] * (1 + len(recv))
            + [lanes(PARAM_ROWS), lanes(4 * MODES), lanes(n + HALO), big, big, big, self.whole(*normed.shape)]
            + [units(0), units(1), units(0)] + [self.order(), normed_at[0][0], normed_at[1][0], self.pair()[0]] * last,
            [*normed_at, params_at] + (self.parts() if last else [self.pair()]),
            [pltpu.VMEM((ms, LANES), F32)] * 2
            + [pltpu.VMEM((n, LANES), F32), pltpu.VMEM((n + HALO, 3 * LANES), BF16), pltpu.VMEM((3 * LANES, w), BF16)]
            + [pltpu.VMEM((2 * self.channels, w), BF16)] * last,
            10**9,
            True,
            count,
        )(
            core, keeps, masks, near, lags, *q, *state, *d, ends, *recv, params, tables, key, value, shifted, grad_query,
            normed, wkv, wkv, wqo, *([order, *before] if last else []),
        )


def lanes_from(rows):
    return pl.BlockSpec((rows, LANES), lambda l: (0, l))


def tail_kernel(steps, shard, core, keep, send, own, sib, sums, params_most, params_rest, bias, tail, rows_of):
    rows = steps * SEGS
    me, me_chip = core[0], core[1]
    total = [jnp.zeros((1, keep.shape[1]), F32)] * 2

    def more(total, grad, x):
        xhat, _ = normalize(x)
        return [t + jnp.sum(v, axis=0, keepdims=True) for t, v in zip(total, (grad * xhat, grad))]

    for r in range(0, rows, LN_TILE):
        at = pl.ds(r, LN_TILE)
        total = more(total, keep[at, :], own[at, :].astype(F32))
        total = more(total, send[at, :], sib[at, :].astype(F32))
    edge = pl.ds(rows, HALO)
    total = more(total, send[edge, :], chunk_of(own, sib, me, 1, edge))
    features = jnp.concatenate([*total, sums[...]], axis=0).astype(BF16)
    params = jnp.concatenate([params_most[...], params_rest[...]], axis=1).astype(BF16)
    chips, deep = tail.shape[0], tail.shape[1]
    rows_of[...] = jnp.zeros_like(rows_of)

    def columns(x, first):
        width = x.shape[1]
        i = lax.broadcasted_iota(jnp.int32, (width, LANES), 0)
        j = lax.broadcasted_iota(jnp.int32, (width, LANES), 1)
        pick = jnp.where(jnp.logical_and(i == first + j, j < shard), 1.0, 0.0).astype(BF16)
        return dot_nn(x, pick)

    for k in range(chips):
        z = lax.rem(me_chip - k + chips, chips)
        rows_of[pl.ds(0, PARAM_ROWS), :] = columns(params, z * shard)
        rows_of[pl.ds(PARAM_ROWS, 6), :] = columns(features, (2 * z + me) * shard)
        rows_of[pl.ds(PARAM_ROWS + 6, 2), :] = columns(features, (2 * z + 1 - me) * shard)[0:2]
        rows_of[pl.ds(PARAM_ROWS + 8, bias.shape[1]), :] = bias[k]
        for i in range(tail.shape[2] // LANES):
            tail[k, :, pl.ds(i * LANES, LANES)] = rows_of[pl.ds(i * deep, deep), :].astype(BF16)


def tail_of(core, keep, send, own, sib, sums, params_most, params_rest, bias, shard):
    width = keep.shape[1]
    across = width // LANES
    used = PARAM_ROWS + 8 + bias.shape[1]
    deep = -(-used // (across * 16)) * 16
    vmem = pl.BlockSpec(memory_space=pltpu.VMEM)
    return pl.pallas_call(
        functools.partial(tail_kernel, keep.shape[0] // SEGS, shard),
        in_specs=[SMEM] + [vmem] * 8,
        out_shape=jax.ShapeDtypeStruct((bias.shape[0], deep, width), BF16),
        scratch_shapes=[pltpu.VMEM((across * deep, LANES), F32)],
        compiler_params=pltpu.CompilerParams(vmem_limit_bytes=VMEM_LIMIT),
        cost_estimate=pl.CostEstimate(flops=10**6, bytes_accessed=10**4, transcendentals=0),
        name="tail_of",
    )(core, keep, send, own, sib, sums, params_most, params_rest, bias)


def finish_kernel(steps, core, keep, from_sib, edge, own, grad_residual, gain, out, total):
    rows = steps * SEGS
    total[...] = keep[...] + from_sib[pl.ds(0, rows), :]
    for b in range(1, TAPS):
        total[pl.ds((steps - b) * SEGS + SEGS - 1, 1), :] += edge[pl.ds(HALO - b, 1), :]
    first = pl.multiple_of(core[0] * rows, rows)
    for r in range(0, rows, LN_TILE):
        at = pl.ds(r, LN_TILE)
        xhat, scale = normalize(own[at, :].astype(F32))
        res = grad_residual[pl.ds(first + r, LN_TILE), :]
        out[at, :] = (res + normalize_back(total[at, :], gain[...], xhat, scale)).astype(BF16)


def finish(core, keep, from_sib, edge, own, grad_residual, gain):
    rows, width = keep.shape
    vmem = pl.BlockSpec(memory_space=pltpu.VMEM)
    return pl.pallas_call(
        functools.partial(finish_kernel, rows // SEGS),
        in_specs=[SMEM] + [vmem] * 6,
        out_shape=jax.ShapeDtypeStruct((rows, width), BF16),
        scratch_shapes=[pltpu.VMEM((rows, width), F32)],
        compiler_params=pltpu.CompilerParams(vmem_limit_bytes=VMEM_LIMIT),
        cost_estimate=pl.CostEstimate(flops=10**6, bytes_accessed=10**4, transcendentals=0),
        name="finish",
    )(core, keep, from_sib, edge, own, grad_residual, gain)


def feed_forward_kernel(reads, writes, n_state, n_arrays, n_outs, core, bias, *refs):
    state, arrays, refs = refs[:n_state], refs[n_state : n_state + n_arrays], refs[n_state + n_arrays :]
    first = n_state > 5
    branch, grad_x, grad_bias = refs[:2], refs[2], refs[3]
    if first:
        own, sib, mixed_own, mixed_sib, c_own, c_sib, lines = state
        residual, xs, cs = refs[4:7]
    else:
        *branch_in, grad_in, xs, cs = state
    at = 7 if first else 4
    outs, (acts, backs, weights, grads, read_sems, write_sems) = refs[at : at + n_outs], refs[at + n_outs :]
    me = core[0]
    half = xs.shape[0] // 2
    n_sets, units = bias.shape

    def place(buffer, s, which, row, n):
        return buffer.at[which, pl.ds(s * units + row, n), :]

    def incoming(s, i):
        array, at, which, row, n = reads[s][i]
        return pltpu.make_async_copy(
            arrays[array].at[pl.ds(at, n), :], place(weights, s, which, row, n), read_sems.at[s, i]
        )

    def outgoing(s, i):
        array, slot, at, which, row, n = writes[s][i]
        return pltpu.make_async_copy(
            place(grads, s, which, row, n), outs[array].at[slot, pl.ds(at, n), :], write_sems.at[s, i]
        )

    for s in range(len(reads)):
        for i in range(len(reads[s])):
            incoming(s, i).start()
    for c in range(2 if first else 0):
        for r in range(0, half, LN_TILE):
            at, part = pl.ds(c * half + r, LN_TILE), pl.ds(r, LN_TILE)
            v = chunk_of(own, sib, me, c, part) + mixed_own[at, :].astype(F32) + mixed_sib[at, :].astype(F32)
            v = v + lines[pl.ds(0, 1), :]
            residual[at, :] = v
            xhat, _ = normalize(v)
            xs[at, :] = (xhat * lines[pl.ds(1, 1), :] + lines[pl.ds(2, 1), :]).astype(BF16)
            cs[at, :] = chunk_of(c_own, c_sib, me, c, part).astype(BF16)
    for s in range(n_sets):
        for i in range(len(reads[s])):
            incoming(s, i).wait()
    total = [jnp.zeros((1, units), F32)] * n_sets
    for r in range(0, 2 * half, TILE):
        at = pl.ds(r, TILE)
        c, place_of = r // half, pl.ds(r % half, TILE)
        for s in range(n_sets):
            mine = pl.ds(s * units, units)
            v = dot_nt(xs[at, :], weights[0, mine, :]) + bias[pl.ds(s, 1), :]
            square = v * v
            th = jnp.tanh(v * (0.79788456 + 0.79788456 * 0.044715 * square))
            half_up = 0.5 + 0.5 * th
            slope = half_up + v * (0.5 - 0.5 * th * th) * (0.79788456 + 0.79788456 * 3.0 * 0.044715 * square)
            back = dot_nt(cs[at, :], weights[1, mine, :]) * slope
            acts[at, mine] = (v * half_up).astype(BF16)
            low = back.astype(BF16)
            backs[at, mine] = low
            total[s] = total[s] + jnp.sum(low.astype(F32), axis=0, keepdims=True)
        out = dot_nn(acts[at, :], weights[1])
        grad = dot_nn(backs[at, :], weights[0])
        grad_x[at, :] = (grad if first else grad_in[at, :] + grad).astype(grad_x.dtype)
        for side in range(2):

            @pl.when(me == (c if side == 0 else 1 - c))
            def _():
                branch[side][place_of, :] = out if first else branch_in[side][place_of, :] + out

    for s in range(n_sets):
        mine = pl.ds(s * units, units)
        grad_bias[pl.ds(s, 1), :] = total[s]
        grads[0, mine, :] = dot_tn(backs[:, mine], xs[...]).astype(BF16)
        grads[1, mine, :] = dot_tn(acts[:, mine], cs[...]).astype(BF16)
        for i in range(len(writes[s])):
            outgoing(s, i).start()
    for s in range(len(writes)):
        for i in range(len(writes[s])):
            outgoing(s, i).wait()


def feed_forward(core, bias, state, arrays, reads, out_shapes, writes, final):
    first = len(state) > 5
    width = state[2].shape[1]
    rows = state[4].shape[0] * 2 if first else state[2].shape[0]
    n_sets, units = bias.shape
    full, low = jax.ShapeDtypeStruct((rows, width), F32), jax.ShapeDtypeStruct((rows, width), BF16)
    part = jax.ShapeDtypeStruct((rows // 2, width), F32)
    vmem, hbm = pl.BlockSpec(memory_space=pltpu.VMEM), pl.BlockSpec(memory_space=pl.ANY)
    kept = [part, part, low if final else full, jax.ShapeDtypeStruct(bias.shape, F32)] + [full, low, low] * first
    out = pl.pallas_call(
        functools.partial(feed_forward_kernel, reads, writes, len(state), len(arrays), len(out_shapes)),
        in_specs=[SMEM] + [vmem] * (1 + len(state)) + [hbm] * len(arrays),
        out_specs=[vmem] * len(kept) + [hbm] * len(out_shapes),
        out_shape=kept + [jax.ShapeDtypeStruct((n, rows_of, width), BF16) for n, rows_of in out_shapes],
        scratch_shapes=[pltpu.VMEM((rows, n_sets * units), BF16)] * 2 + [pltpu.VMEM((2, n_sets * units, width), BF16)] * 2
        + [pltpu.SemaphoreType.DMA((n_sets, max(map(len, p)))) for p in (reads, writes)],
        compiler_params=pltpu.CompilerParams(vmem_limit_bytes=VMEM_LIMIT),
        cost_estimate=pl.CostEstimate(flops=10**6, bytes_accessed=10**4, transcendentals=0),
        name="feed_forward" if first else "feed_forward_more",
    )(core, bias, *state, *arrays)
    return out[: len(kept)], out[len(kept) :]


def local(
    groups, chips,
    hidden_in, mix_gain, mix_shift, w_query, bias_query, w_key, bias_key, w_value, bias_value, shift_taps,
    log_step, log_decay, frequency, out_real, out_imag, skip_gain, w_out, bias_out, mlp_gain, mlp_shift,
    w_up, bias_up, w_down, bias_down, cotangent, seq_blocks,
):
    rows, width = hidden_in.shape
    shard, shard_units = w_query.shape[1], w_up.shape[1]
    chans, channels = 2 * chips, chips * shard
    cut, unit_cut = shard // groups, shard_units // groups
    steps = rows // SEGS
    me_group, me_chan = lax.axis_index("group"), lax.axis_index("chan")
    me_chip, me_core = me_chan // 2, me_chan % 2
    same_core = [[2 * z + k for z in range(chips)] for k in range(2)]
    square = groups == 4

    def swap_z(x):
        return lax.all_to_all(x, "chan", 0, 0, axis_index_groups=same_core, tiled=True)

    def group_swap(x, bits):
        return lax.ppermute(x, "group", [(i, i ^ bits) for i in range(groups)])

    def sibling(x):
        return lax.ppermute(x, "chan", [(i, i ^ 1) for i in range(chans)])

    def chip_shift(x, by):
        pairs = [(i, i + 2 * by) for i in range(chans) if 0 <= i + 2 * by < chans]
        return lax.ppermute(x, "chan", pairs)

    def chip_turn(x, by):
        return lax.ppermute(x, "chan", [(i, (i + 2 * by) % chans) for i in range(chans)])

    def gather_z(x):
        return jnp.concatenate([x] + [chip_turn(x, by) for by in range(1, chips)])

    def gather_group(x):
        return [x] + [group_swap(x, r) for r in range(1, groups)]

    def add(*xs):
        return sum(x.astype(F32) for x in xs).astype(BF16)

    def fold_z(parts):
        return add(parts[0], *(chip_turn(p, -by) for by, p in enumerate(parts) if by))

    def fold_group(parts):
        return add(parts[0], *(group_swap(p, r) for r, p in enumerate(parts) if r))

    def pieces(x, count):
        n = x.shape[0] // count
        return [x[i * n : (i + 1) * n] for i in range(count)]

    def by_index(parts):
        out = []
        for g in range(groups):
            x = parts[0]
            for r in range(1, groups):
                x = jnp.where(me_group == g ^ r, parts[r], x)
            out.append(x)
        return jnp.stack(out)

    def first_round(a):
        return (group_swap(a, 1), group_swap(a, 2)) if square else tuple(gather_group(a)[1:])

    def second_round(one):
        n = one[0].shape[0] // 2
        return (group_swap(one[1][:n], 1), group_swap(one[0][n:], 2)) if square else ()

    def fold_first(send_a, send_b):
        return [group_swap(x, 1) for x in send_a], [group_swap(x, 2) for x in send_b]

    def fold_second(one, ay, bx):
        return group_swap(add(ay, one[0][1]), 2), group_swap(add(bx, one[1][1]), 1)

    def fold_end(one, two, a0, b0):
        return add(a0, one[0][0], two[0]), add(b0, one[1][0], two[1])

    def fence(*xs):
        return lax.optimization_barrier(xs)

    def share(x):
        return lax.dynamic_index_in_dim(x.reshape(groups, -1, width), me_group, 0, keepdims=False)

    def to_steps(x):
        return x.reshape(SEGS, steps, width).transpose(1, 0, 2).reshape(rows, width)

    def to_rows(x):
        return x.reshape(steps, SEGS, width).transpose(1, 0, 2).reshape(rows, width)

    first = seq_blocks[0, 0]
    second = first + seq_blocks[0, 1]

    def keep(block):
        starts = (block == 0) | (block == first) | (block == second)
        return jnp.where(starts, 0.0, 1.0).astype(F32)

    blocks = 4 * me_chip + jnp.arange(4)
    keeps = keep(blocks).reshape(2, 2)
    near = me_chip + jnp.stack([-jnp.arange(chips), jnp.arange(chips)])
    masks = jnp.prod(keep(4 * near[..., None] + jnp.arange(4)), axis=-1)

    def two_shares(a, b):
        return jnp.concatenate([share(a), share(b)])

    turns = (me_chip - jnp.arange(chips)) % chips
    flips = me_group ^ jnp.arange(groups)
    place = flips[None, None, :, None] * chips + turns[None, :, None, None]
    place = (place * 2 + jnp.arange(2)[:, None, None, None]) * cut + jnp.arange(cut)
    order = (place.reshape(-1, 1) == jnp.arange(2 * channels)).astype(BF16)
    z_turn = (turns[:, None] == jnp.arange(chips)).astype(F32)
    g_flip = (flips[:, None] == jnp.arange(groups)).astype(F32)
    exact = lax.Precision.HIGHEST

    core = jnp.stack([me_core, me_chip])
    line = lambda x: x.reshape(1, width)
    kv_z = gather_z(two_shares(w_key.T, w_value.T))
    edge = lax.ppermute(hidden_in[rows - HALO :], "chan", [(2 * z + 1, 2 * z + 3) for z in range(chips - 1)])
    own = jnp.concatenate([to_steps(hidden_in), edge])
    kv_z, own, w_query, w_out, w_up, w_down, cotangent, log_decay, frequency, out_real, out_imag = fence(
        kv_z, own, w_query, w_out, w_up, w_down, cotangent, log_decay, frequency, out_real, out_imag
    )

    mixed_kv = gather_group(kv_z)
    small = jnp.concatenate(
        [
            log_decay.T, frequency.T, out_real.T, out_imag.T, shift_taps.T,
            jnp.stack([log_step, skip_gain, bias_query, bias_key, bias_value]),
            bias_up.reshape(shard_units // shard, shard),
        ]
    )
    small = swap_z(jnp.broadcast_to(small, (chips,) + small.shape))
    sib = sibling(own)
    qo_z = gather_z(two_shares(w_query.T, w_out))
    params = jnp.moveaxis(small[:, :PARAM_ROWS], 0, 1).reshape(PARAM_ROWS, channels)
    units_bias = small[:, PARAM_ROWS:].reshape(chips, groups, unit_cut)
    units_bias = jnp.einsum("rg,zgu->rzu", g_flip, units_bias, precision=exact).reshape(groups, -1)
    mixed_kv, sib, qo_z, params, units_bias, order, keeps, masks, w_up, w_down, cotangent = fence(
        mixed_kv, sib, qo_z, params, units_bias, order, keeps, masks, w_up, w_down, cotangent
    )

    ff_z = two_shares(w_up.T, w_down)
    ff_z = swap_z(jnp.broadcast_to(ff_z, (chips,) + ff_z.shape))
    mixed_qo = gather_group(qo_z)
    mixer = Mixer(rows, channels, width, groups)
    normed, wkv, tables, kern, key, value, prod, shifted, er, ei, dr, di, ends, chip = mixer.before(
        core, keeps, own, sib, line(mix_gain), line(mix_shift), order, mixed_kv, params
    )
    chip, ends, cotangent, mixed_qo = fence(chip, ends, cotangent, mixed_qo)

    recv = [chip_shift(chip, by) for by in range(1, chips)]
    wqo, query, near = mixer.near(normed, prod, mixed_qo, order, params, kern)
    cot = to_steps(cotangent)
    recv, near, ff_z, cot = fence(recv, near, ff_z, cot)

    if not square:
        ff_z = jnp.moveaxis(ff_z.reshape(chips, 2, unit_cut, width), 1, 0)
    ff_z = ff_z.reshape(-1, width)
    ff_one = first_round(ff_z)
    cot_sib = sibling(cot)
    conv, core_low, state_r, state_i, mixed = mixer.conv(
        keeps, masks, near, query, er, ei, ends, recv, wqo, tables
    )
    mixed, cot_sib, ff_one = fence(mixed, cot_sib, ff_one)

    mixed_sib = sibling(mixed)
    ff_two = second_round(ff_one)
    (mixed_sib,) = fence(mixed_sib)

    units = chips * unit_cut
    if square:
        arrays = [ff_z, *ff_one]
        near_half = chips // 2

        def rows_of(z, which):
            return (z % near_half * 2 + which) * unit_cut

        every = [(z, which) for z in range(chips) for which in range(2)]
        reads = [
            [(s, (z * 2 + w) * unit_cut, w, z * unit_cut, unit_cut) for z, w in every] for s in range(3)
        ] + [[(z // near_half, rows_of(z, w), w, z * unit_cut, unit_cut) for z, w in every]]
        to = ((0, 3), (2, 4), (1, 5), (0, 1))
        slots = ((0, 0),) * 4
        writes = [
            [
                (to[s][z // near_half], slots[s][z // near_half], rows_of(z, w), w, z * unit_cut, unit_cut)
                for z, w in every
            ]
            for s in range(4)
        ]
        out_shapes = [(1, units)] * 2 + [(1, units)] + [(1, units)] * 2 + [(1, units)]
    else:
        arrays = [ff_z, *ff_one]
        reads = [[(s, w * units, w, 0, units) for w in range(2)] for s in range(groups)]
        writes = [[(s, 0, w * units, w, 0, units) for w in range(2)] for s in range(groups)]
        out_shapes = [(1, 2 * units)] * groups
    lines = jnp.stack([bias_out, mlp_gain, mlp_shift])
    state = (own, sib, mixed, mixed_sib, cot, cot_sib, lines)
    n_first = 3 if square else groups
    (*branch, grad_two, grad_units_bias, residual, xs, cs), grad_ff = feed_forward(
        core, units_bias[:n_first], state, arrays[:n_first], reads[:n_first], out_shapes, writes[:n_first], not square
    )
    if square:
        branch, grad_two, xs, cs, ff_two = fence(branch, grad_two, xs, cs, ff_two)
        (*branch, grad_two, more_bias), grad_diagonal = feed_forward(
            core, units_bias[3:], (*branch, grad_two, xs, cs), ff_two, reads[3:], [(1, units)] * 2, writes[3:], True
        )
        grad_units_bias = jnp.concatenate([grad_units_bias, more_bias])

    grad_two_sib, branch_sib = sibling(grad_two), sibling(branch[1])
    if square:
        fold_one = fold_first((grad_ff[2][0], grad_diagonal[0][0]), (grad_ff[5][0], grad_diagonal[1][0]))
    else:
        fold_one = ()
    after = mixer.after(
        core, keeps, residual, grad_two, grad_two_sib, cot, cot_sib, line(mlp_gain), order, wqo, normed, query, conv,
        core_low, tables,
    )
    grad_residual, g, grad_query, *qsums, ends, chip, sums = after[:10]
    grad_qo = after[10:]
    chip, grad_qo, branch, branch_sib, ends, g = fence(chip, grad_qo, branch, branch_sib, ends, g)

    recv = [chip_shift(chip, -by) for by in range(1, chips)]
    near, lags = mixer.near_back(g, prod, params, kern)
    recv, near, lags, fold_one, grad_qo = fence(recv, near, lags, fold_one, grad_qo)

    bias_rows = grad_units_bias.reshape(groups, chips, unit_cut)
    bias_rows = jnp.einsum("kz,rg,rzu->kgu", z_turn, g_flip, bias_rows, precision=exact)
    bias_rows = jnp.pad(bias_rows.reshape(chips, -1, shard), ((0, 0), (0, 0), (0, LANES - shard)))
    used = PARAM_ROWS + 8 + bias_rows.shape[1]

    fold_two = fold_second(fold_one, grad_ff[1][0], grad_ff[4][0]) if square else ()
    blocks = channels // LANES
    grads_of = lambda base, count, before: mixer.grads(
        base, count, core, keeps, masks, near, lags, qsums, (state_r, state_i), (dr, di), ends, recv, params, tables, key,
        value, shifted, grad_query, normed, wkv, wqo, order, before,
    )
    grad_keep, grad_send, params_most, grad_w = grads_of(0, 1, None)
    fold_two, grad_keep, grad_w = fence(fold_two, grad_keep, grad_w)

    if square:
        ff = jnp.concatenate(fold_end(fold_one, fold_two, grad_ff[0][0], grad_ff[3][0]))
    else:
        ff = fold_group([x[0] for x in grad_ff]).reshape(2, chips, unit_cut, width)
        ff = jnp.moveaxis(ff, 1, 0)
    ff = ff.reshape(chips, 2 * unit_cut, width)
    ff = [lax.dynamic_index_in_dim(ff, (me_chip + k) % chips, 0, keepdims=False) for k in range(chips)]
    ff_odd = [chip_turn(ff[k], k) for k in range(1, chips, 2)]
    grad_keep, grad_send, params_rest, *grad_kv = grads_of(1, blocks - 1, (grad_keep, grad_send, grad_w))
    grad_kv, grad_keep, grad_send, params_rest, ff, ff_odd = fence(
        grad_kv, grad_keep, grad_send, params_rest, ff, ff_odd
    )

    kv = fold_group(grad_kv)
    ff = add(ff[0], *ff_odd, *(chip_turn(ff[k], k) for k in range(2, chips, 2)))
    from_sib = sibling(grad_send)
    tail = tail_of(core, grad_keep, grad_send, own, sib, sums, params_most, params_rest, bias_rows, shard)
    kv, tail, ff, from_sib = fence(kv, tail, ff, from_sib)

    kv = fold_z([jnp.concatenate(p) for p in zip(pieces(kv, chips), tail)])
    qo = fold_group(grad_qo)
    ff = gather_group(ff)
    mine = lax.dynamic_slice_in_dim(residual, me_core * rows, rows, axis=0)
    output = to_rows((mine + branch[0] + branch_sib + bias_down).astype(BF16))
    edge = grad_send[rows:] + from_sib[rows:]
    edge = lax.ppermute(edge, "chan", [(2 * z + 3, 2 * z + 1) for z in range(chips - 1)])
    kv, qo, output, edge, ff = fence(kv, qo, output, edge, ff)

    kv = gather_group(kv)
    qo = gather_group(fold_z(pieces(qo, chips)))
    grad_input = to_rows(finish(core, grad_keep, from_sib, edge, own, grad_residual, line(mix_gain)))
    grad_wf = by_index(ff).reshape(groups, 2, unit_cut, width)
    grad_wf = jnp.moveaxis(grad_wf, 1, 0).reshape(2, shard_units, width).astype(F32)

    def halves(parts):
        x = by_index(parts).reshape(groups, 2, cut, width)
        return jnp.moveaxis(x, 1, 0).reshape(2, shard, width).astype(F32)

    (grad_wk, grad_wv), (grad_wq, grad_wo) = halves([x[: 2 * cut] for x in kv]), halves(qo)
    tail = sum(x[2 * cut :].astype(F32) for x in kv)
    tail = tail.reshape(-1, width // LANES, LANES).transpose(1, 0, 2).reshape(-1, LANES)[:used, :shard]
    modes = [tail[i * MODES : (i + 1) * MODES].T for i in range(4)]
    biases = tail[BIAS_ROW:PARAM_ROWS]
    feat_part = tail[PARAM_ROWS : PARAM_ROWS + 6]
    first_two = feat_part[:2] + sibling(tail[PARAM_ROWS + 6 : PARAM_ROWS + 8])
    sum_bias_up = tail[PARAM_ROWS + 8 :].reshape(shard_units)
    return (
        output,
        grad_input,
        first_two[0],
        first_two[1],
        grad_wq.T,
        biases[0],
        grad_wk.T,
        biases[1],
        grad_wv.T,
        biases[2],
        tail[TAP_ROW : TAP_ROW + TAPS].T,
        tail[STEP_ROW],
        modes[0],
        modes[1],
        modes[2],
        modes[3],
        tail[SKIP_ROW],
        grad_wo,
        feat_part[2],
        feat_part[3],
        feat_part[4],
        grad_wf[0].T,
        sum_bias_up,
        grad_wf[1],
        feat_part[5],
    )


def solution(mesh):
    rows = P(("group", "chan"), None)
    columns, channels, vector, copied = P(None, "chan"), P("chan", None), P("chan"), P()
    return jax.shard_map(
        functools.partial(local, mesh.shape["group"], mesh.shape["chan"] // 2),
        mesh=mesh,
        in_specs=(
            rows, copied, copied, columns, vector, columns, vector, columns, vector, channels,
            vector, channels, channels, channels, channels, vector, channels, copied, copied, copied,
            columns, vector, channels, copied, rows, P("group", None),
        ),
        out_specs=(
            rows, rows, vector, vector, columns, vector, columns, vector, columns, vector,
            channels, vector, channels, channels, channels, channels, vector, channels, vector, vector,
            vector, columns, vector, channels, vector,
        ),
        check_vma=False,
    )
```

```python
import functools

import jax
import jax.numpy as jnp
import numpy as np
from jax import lax
from jax.experimental import pallas as pl
from jax.experimental.pallas import tpu as pltpu
from jax.sharding import PartitionSpec as P

F32 = jnp.float32
BF16 = jnp.bfloat16
MODES = 32
LANES = 128
SEGS = 8
TAPS = 4
BLOCK = 8
HALO = 16
TILE = 128
LN_TILE = 64
EPSILON = 1e-05
VMEM_LIMIT = 60 * 1024 * 1024
SMEM = pl.BlockSpec(memory_space=pltpu.SMEM)

TAP_ROW = 4 * MODES
STEP_ROW = TAP_ROW + TAPS
SKIP_ROW = STEP_ROW + 1
BIAS_ROW = SKIP_ROW + 1
PARAM_ROWS = BIAS_ROW + 3


def ssm_tables(log_step, log_decay, frequency, out_real, out_imag):
    step_size = jnp.exp(log_step)
    rate = -jnp.exp(log_decay)
    decay = rate * step_size
    turn = frequency * step_size
    growth = jnp.exp(decay)
    ratio_re = growth * jnp.cos(turn) - 1.0
    ratio_im = growth * jnp.sin(turn)
    denom = rate * rate + frequency * frequency
    scaled_re = (ratio_re * rate + ratio_im * frequency) / denom
    scaled_im = (ratio_im * rate - ratio_re * frequency) / denom
    weight_re = out_real * scaled_re - out_imag * scaled_im
    weight_im = out_real * scaled_im + out_imag * scaled_re
    return decay, turn, weight_re, weight_im


def table_inputs(params):
    parts = [params[pl.ds(i * MODES, MODES), :] for i in range(4)]
    return [params[pl.ds(STEP_ROW, 1), :], *parts]


def read_tables(tables):
    return [tables[pl.ds(i * MODES, MODES), :] for i in range(4)]


def dot_nn(a, b):
    return lax.dot_general(a, b, (((1,), (0,)), ((), ())), preferred_element_type=F32)


def dot_nt(a, b):
    return lax.dot_general(a, b, (((1,), (1,)), ((), ())), preferred_element_type=F32)


def dot_tn(a, b):
    return lax.dot_general(a, b, (((0,), (0,)), ((), ())), preferred_element_type=F32)


def cmul(ar, ai, br, bi):
    return ar * br - ai * bi, ar * bi + ai * br


def normalize(values):
    center = values - jnp.mean(values, axis=-1, keepdims=True)
    scale = lax.rsqrt(jnp.mean(center * center, axis=-1, keepdims=True) + EPSILON)
    return center * scale, scale


def normalize_back(grad, gain, xhat, scale):
    gy = grad * gain
    mean_gy = jnp.mean(gy, axis=-1, keepdims=True)
    mean_gx = jnp.mean(gy * xhat, axis=-1, keepdims=True)
    return scale * (gy - mean_gy - xhat * mean_gx)


def pack_kernel(decay, freq, real, imag, taps, step, skip, bias_q, bias_k, bias_v, bias_up, out, rows_of):
    shard = decay.shape[1]
    at = 0
    for x in (decay, freq, real, imag, taps):
        n = x.shape[0]
        rows_of[pl.ds(at, n), :] = x[...]
        at += n
    for x in (step, skip, bias_q, bias_k, bias_v):
        rows_of[pl.ds(at, 1), :] = x[...]
        at += 1
    for i in range(bias_up.shape[1] // shard):
        rows_of[pl.ds(at + i, 1), :] = bias_up[:, pl.ds(i * shard, shard)]
    for i in range(out.shape[0]):
        out[i] = rows_of[...]


def pack(chips, matrices, vectors, bias_up):
    shard = matrices[0].shape[1]
    rows = PARAM_ROWS + bias_up.shape[0] // shard
    return pl.pallas_call(
        pack_kernel,
        out_shape=jax.ShapeDtypeStruct((chips, rows, shard), F32),
        scratch_shapes=[pltpu.VMEM((rows, shard), F32)],
        cost_estimate=pl.CostEstimate(flops=10**6, bytes_accessed=10**4, transcendentals=0),
        name="pack",
    )(*matrices, *(v.reshape(1, -1) for v in vectors), bias_up.reshape(1, -1))


def fill_powers(zr, zi, pr, pi, steps):
    ar, ai = jnp.ones_like(zr), jnp.zeros_like(zi)
    pr[pl.ds(0, MODES), :] = ar
    pi[pl.ds(0, MODES), :] = ai
    for j in range(1, steps + 1):
        ar, ai = cmul(ar, ai, zr, zi)
        pr[pl.ds(j * MODES, MODES), :] = ar
        pi[pl.ds(j * MODES, MODES), :] = ai
    return ar, ai


def over_chunk(ar, ai):
    n = 1
    while n < SEGS:
        ar, ai = cmul(ar, ai, ar, ai)
        n *= 2
    return ar, ai


def fill_kern(wr, wi, pr, pi, kern, steps):
    for j in range(steps):
        v = wr * pr[pl.ds(j * MODES, MODES), :] - wi * pi[pl.ds(j * MODES, MODES), :]
        kern[pl.ds(j, 1), :] = 2.0 * jnp.sum(v, axis=0, keepdims=True)


def row(ref, i):
    return jnp.broadcast_to(ref[pl.ds(i, 1), :], (SEGS, LANES))


def group(ref, steps, c, t):
    return ref[pl.ds((c * steps + t) * SEGS, SEGS), :]


def put(ref, steps, c, t, value):
    ref[pl.ds((c * steps + t) * SEGS, SEGS), :] = value


def put_low(ref, steps, c, t, pair):
    ref[pl.ds((c * steps + t) * SEGS, 2 * SEGS), :] = jnp.concatenate(pair).astype(BF16)


def sublanes():
    return lax.broadcasted_iota(jnp.int32, (SEGS, LANES), 0)


def seg_mask(keep0, keep4):
    ids = sublanes()
    m = jnp.where(ids == 0, keep0, 1.0)
    return jnp.where(ids == SEGS // 2, keep4, m)


def seg_rows(c, k):
    return pl.ds(c * MODES * SEGS + k, MODES, stride=SEGS)


def mode_rows(c, m):
    return pl.ds(pl.multiple_of(c * MODES * SEGS + m * SEGS, SEGS), SEGS)


def weigh(pr, pi, steps, order, power, last, data, outs):
    outs_r, outs_i, runs_r, runs_i = outs
    half = steps // 2
    for part in range(2):
        ts = order[part * half : (part + 1) * half]
        values = [[data(c, t) for t in ts] for c in range(2)]

        def per_mode(m, carry):
            acc = []
            for c in range(2):
                if part == 0:
                    acc.append([jnp.zeros((SEGS, LANES), F32)] * 4)
                else:
                    acc.append([r[mode_rows(c, m), :] for r in (outs_r, outs_i, runs_r, runs_i)])
            for i, t in enumerate(ts):
                a, b = row(pr, power(t) * MODES + m), row(pi, power(t) * MODES + m)
                for c in range(2):
                    sr, si, tr, ti = acc[c]
                    sr, si = sr + a * values[c][i], si + b * values[c][i]
                    if last or t != order[-1]:
                        tr, ti = tr + sr, ti + si
                    acc[c] = [sr, si, tr, ti]
            for c in range(2):
                for r, v in zip((outs_r, outs_i, runs_r, runs_i), acc[c]):
                    r[mode_rows(c, m), :] = v
            return carry

        lax.fori_loop(0, MODES, per_mode, 0, unroll=2)


def unfold(pr, pi, steps, power, states, base, done):
    half = steps // 2
    for part in range(2):
        ts = range(part * half, (part + 1) * half)
        init = tuple(base(c, t) for c in range(2) for t in ts)

        def per_mode(m, acc):
            acc = list(acc)
            u = [states[0][mode_rows(c, m), :] for c in range(2)]
            v = [states[1][mode_rows(c, m), :] for c in range(2)]
            for i, t in enumerate(ts):
                a, b = row(pr, power(t) * MODES + m), row(pi, power(t) * MODES + m)
                for c in range(2):
                    at = c * half + i
                    acc[at] = acc[at] + (a * u[c] - b * v[c])
            return tuple(acc)

        acc = lax.fori_loop(0, MODES, per_mode, init, unroll=2)
        for c in range(2):
            for i in range(0, half, 2):
                done(c, ts[i], acc[c * half + i : c * half + i + 2])


def lags_apply(kern, steps, base, source, out, adjoint):
    n = steps // BLOCK
    for tb in range(n):
        ts = range(tb * BLOCK, (tb + 1) * BLOCK)
        ys = {(c, t): base(c, t) for c in range(2) for t in ts}
        for sb in range(tb, n) if adjoint else range(tb + 1):
            ss = range(sb * BLOCK, (sb + 1) * BLOCK)
            xs = {(c, s): source(c, s) for c in range(2) for s in ss}
            for lag in range(steps):
                pairs = [(t, s) for t in ts for s in ss if (s - t if adjoint else t - s) == lag]
                if pairs:
                    k = row(kern, lag)
                    for t, s in pairs:
                        for c in range(2):
                            ys[c, t] = ys[c, t] + k * xs[c, s]
        for (c, t), y in ys.items():
            put(out, steps, c, t, y)


def lag_sums(steps, left, right):
    n = steps // BLOCK
    sums = []
    for jb in range(n):
        acc = [jnp.zeros((SEGS, LANES), F32)] * BLOCK
        for c in range(2):
            for tb in range(jb, n):
                ts = range(tb * BLOCK, (tb + 1) * BLOCK)
                base = (tb - jb) * BLOCK
                xs = {s: right(c, s) for s in range(max(base - BLOCK + 1, 0), base + BLOCK)}
                for t in ts:
                    g = left(c, t)
                    for j in range(BLOCK):
                        s = t - jb * BLOCK - j
                        if s >= 0:
                            acc[j] = acc[j] + g * xs[s]
        sums.extend(jnp.sum(a, axis=0, keepdims=True) for a in acc)
    return sums


def earlier_keys(key, steps, keeps):
    ids = sublanes()
    out = []
    rolled = None
    for c in range(2):
        mask = seg_mask(keeps[c, 0], keeps[c, 1])
        new, windows = [], []
        for back in (1, 2, 3):
            v = pltpu.roll(group(key, steps, c, steps - back), 1, 0)
            new.append(v)
            before = row(key, 2 * steps * SEGS + HALO - back) if c == 0 else rolled[back - 1]
            windows.append(jnp.where(ids == 0, before, v) * mask)
        rolled = new
        out.append(windows)
    return out


def chunk_of(own, sib, core, c, at):
    return jnp.where(core == c, own[at, :].astype(F32), sib[at, :].astype(F32))


def join(parts, out):
    at = 0
    for p in parts:
        n = p.shape[0]
        out[pl.ds(at, n), :] = p[...]
        at += n


def part_to(outs, value):
    at = 0
    for o in outs:
        n = o.shape[0]
        o[...] = value[at : at + n].astype(BF16)
        at += n


def before_kernel(steps, n_parts, core, keeps, own, sib, gain, shift, order, *refs):
    mixed_kv, params = refs[:n_parts], refs[n_parts]
    normed, wkv, tables, kern, key, value, prod, shifted, er, ei, dr, di, ends, chip, pr, pi, joined = refs[n_parts + 1 :]
    lane = pl.program_id(0)
    rows = steps * SEGS
    channels = wkv.shape[0] // 2

    @pl.when(lane == 0)
    def _():
        me = core[0]
        join(mixed_kv, joined)
        wkv[...] = dot_nn(order[...], joined[...]).astype(BF16)

        def rows_of(x):
            xhat, _ = normalize(x)
            return (xhat * gain[...] + shift[...]).astype(BF16)

        for c in range(2):
            for r in range(0, rows, LN_TILE):
                normed[pl.ds(c * rows + r, LN_TILE), :] = rows_of(chunk_of(own, sib, me, c, pl.ds(r, LN_TILE)))
        normed[pl.ds(2 * rows, HALO), :] = rows_of(chunk_of(own, sib, me, 1, pl.ds(rows, HALO)))

    decay, turn, wr, wi = ssm_tables(*table_inputs(params))
    mag = jnp.exp(decay)
    zr, zi = mag * jnp.cos(turn), mag * jnp.sin(turn)
    for i, v in enumerate((zr, zi, wr, wi)):
        tables[pl.ds(i * MODES, MODES), :] = v
    ar, ai = fill_powers(zr, zi, pr, pi, steps)
    fill_kern(wr, wi, pr, pi, kern, steps)
    at = pl.ds(pl.multiple_of(lane * LANES, LANES), LANES)
    also = pl.ds(pl.multiple_of(channels + lane * LANES, LANES), LANES)
    key[...] = dot_nt(normed[...], wkv[at, :]) + params[pl.ds(BIAS_ROW + 1, 1), :]
    value[...] = dot_nt(normed[pl.ds(0, 2 * rows), :], wkv[also, :]) + params[pl.ds(BIAS_ROW + 2, 1), :]
    tap = [row(params, TAP_ROW + j) for j in range(TAPS)]
    windows = earlier_keys(key, steps, keeps)
    for c in range(2):
        window = windows[c]
        for t in range(steps):
            cur = group(key, steps, c, t)
            s = tap[0] * cur + tap[1] * window[0] + tap[2] * window[1] + tap[3] * window[2]
            window = [cur] + window[:2]
            put(shifted, steps, c, t, s)
            put(prod, steps, c, t, s * group(value, steps, c, t))
    weigh(
        pr, pi, steps, list(range(steps)), lambda t: steps - 1 - t, False,
        lambda c, t: group(prod, steps, c, t), (er, ei, dr, di),
    )
    states = []
    for c in range(2):
        k4 = keeps[c, 1]
        sr = si = jnp.zeros((MODES, LANES), F32)
        for k in range(SEGS):
            if k == SEGS // 2:
                sr, si = sr * k4, si * k4
            cr, ci = cmul(sr, si, ar, ai)
            sr = cr + er[seg_rows(c, k), :]
            si = ci + ei[seg_rows(c, k), :]
        states.append((sr, si))
    ends[pl.ds(0, MODES), :], ends[pl.ds(MODES, MODES), :] = states[0]
    br, bi = over_chunk(ar, ai)
    cr, ci = cmul(*states[0], br, bi)
    keep = keeps[1, 0] * keeps[1, 1]
    chip[pl.ds(0, MODES), :] = (cr * keep + states[1][0]).astype(BF16)
    chip[pl.ds(MODES, MODES), :] = (ci * keep + states[1][1]).astype(BF16)


def incoming(ref_list, masks, which, ar, ai):
    br, bi = cmul(ar, ai, ar, ai)
    read = lambda r: (r[pl.ds(0, MODES), :].astype(F32), r[pl.ds(MODES, MODES), :].astype(F32))
    sr, si = read(ref_list[-1])
    for by in range(len(ref_list) - 1, 0, -1):
        m = masks[which, by]
        cr, ci = cmul(sr, si, br * m, bi * m)
        rr, ri = read(ref_list[by - 1])
        sr, si = cr + rr, ci + ri
    return sr, si


def near_kernel(steps, n_parts, normed, prod, *refs):
    mixed_qo = refs[:n_parts]
    order, params, kern, wqo, query, near, joined = refs[n_parts:]
    lane = pl.program_id(0)
    rows = steps * SEGS

    @pl.when(lane == 0)
    def _():
        join(mixed_qo, joined)
        wqo[...] = dot_nn(order[...], joined[...]).astype(BF16)

    at = pl.ds(pl.multiple_of(lane * LANES, LANES), LANES)
    query[...] = dot_nt(normed[pl.ds(0, 2 * rows), :], wqo[at, :]) + params[pl.ds(BIAS_ROW, 1), :]
    source = lambda c, t: group(prod, steps, c, t)
    sk = row(params, SKIP_ROW)
    lags_apply(kern, steps, lambda c, t: sk * source(c, t), source, near, False)


def conv_kernel(steps, n_recv, keeps, masks, near, query, er, ei, ends, *refs):
    recv = refs[:n_recv]
    wo, tables, conv, core_low, state_r, state_i, mixed_low, pr, pi, twice_r, twice_i, mixed = refs[n_recv:]
    lane = pl.program_id(0)
    zr, zi, wr, wi = read_tables(tables)
    ar, ai = fill_powers(zr, zi, pr, pi, steps)
    w2r, w2i = 2.0 * wr, 2.0 * wi
    br, bi = over_chunk(ar, ai)
    sr, si = incoming(recv, masks, 0, br, bi)
    for c in range(2):
        if c == 1:
            sr, si = cmul(first_r, first_i, br * keeps[0, 1], bi * keeps[0, 1])
            sr, si = sr + ends[pl.ds(0, MODES), :], si + ends[pl.ds(MODES, MODES), :]
        sr, si = sr * keeps[c, 0], si * keeps[c, 0]
        first_r, first_i = sr, si
        for k in range(SEGS):
            if k == SEGS // 2:
                sr, si = sr * keeps[c, 1], si * keeps[c, 1]
            state_r[seg_rows(c, k), :] = sr
            state_i[seg_rows(c, k), :] = si
            twice_r[seg_rows(c, k), :], twice_i[seg_rows(c, k), :] = cmul(w2r, w2i, sr, si)
            if k < SEGS - 1:
                cr, ci = cmul(sr, si, ar, ai)
                sr = cr + er[seg_rows(c, k), :]
                si = ci + ei[seg_rows(c, k), :]

    def done(c, t, values):
        low = []
        for i, v in zip((t, t + 1), values):
            put(conv, steps, c, i, v)
            low.append(v * group(query, steps, c, i))
        put_low(core_low, steps, c, t, low)

    unfold(pr, pi, steps, lambda t: t + 1, (twice_r, twice_i), lambda c, t: group(near, steps, c, t), done)
    out = dot_nn(core_low[...], wo[...])

    @pl.when(lane == 0)
    def _():
        mixed[...] = out

    @pl.when(jnp.logical_and(lane > 0, lane < pl.num_programs(0) - 1))
    def _():
        mixed[...] += out

    @pl.when(lane == pl.num_programs(0) - 1)
    def _():
        mixed_low[...] = (mixed[...] + out).astype(BF16)


def after_kernel(
    steps, core, keeps, residual, grad_own, grad_sib, cot_own, cot_sib, gain, order, wo, normed, query, conv, core_low,
    tables, grad_residual, g, grad_query, qr, qi, rr, ri, ends, chip, sums, *refs,
):
    grad_qo, (pr, pi, low, grad_core, grad_w) = refs[:-5], refs[-5:]
    lane = pl.program_id(0)
    rows = steps * SEGS
    channels = grad_w.shape[0] // 2

    @pl.when(lane == 0)
    def _():
        me = core[0]
        total = [jnp.zeros((1, low.shape[1]), F32)] * 4
        for c in range(2):
            for r in range(0, rows, LN_TILE):
                at = pl.ds(c * rows + r, LN_TILE)
                xhat, scale = normalize(residual[at, :])
                grad = grad_own[at, :].astype(F32) + grad_sib[at, :].astype(F32)
                cot = chunk_of(cot_own, cot_sib, me, c, pl.ds(r, LN_TILE))
                out = cot + normalize_back(grad, gain[...], xhat, scale)
                grad_residual[at, :] = out
                low[at, :] = out.astype(BF16)
                for i, v in enumerate((out, grad * xhat, grad, cot)):
                    total[i] = total[i] + jnp.sum(v, axis=0, keepdims=True)
        sums[...] = jnp.concatenate(total, axis=0)

    zr, zi, wr, wi = read_tables(tables)
    ar, ai = fill_powers(zr, zi, pr, pi, steps)
    grad_core[...] = dot_nt(low[...], wo[...])
    for c in range(2):
        for t in range(0, steps, 2):
            pair = []
            for i in (t, t + 1):
                d = group(grad_core, steps, c, i)
                put(g, steps, c, i, d * group(query, steps, c, i))
                pair.append(d * group(conv, steps, c, i))
            put_low(grad_query, steps, c, t, pair)
    at = pl.ds(pl.multiple_of(lane * LANES, LANES), LANES)
    also = pl.ds(pl.multiple_of(channels + lane * LANES, LANES), LANES)
    grad_w[at, :] = dot_tn(grad_query[...], normed[pl.ds(0, 2 * rows), :]).astype(BF16)
    grad_w[also, :] = dot_tn(core_low[...], low[...]).astype(BF16)

    @pl.when(lane == pl.num_programs(0) - 1)
    def _():
        part_to(grad_qo, dot_tn(order[...], grad_w[...]))

    weigh(
        pr, pi, steps, list(reversed(range(steps))), lambda t: t + 1, True,
        lambda c, t: group(g, steps, c, t), (qr, qi, rr, ri),
    )
    w2r, w2i = 2.0 * wr, 2.0 * wi
    lr = li = jnp.zeros((MODES, LANES), F32)
    for c in (1, 0):
        for k in reversed(range(SEGS)):
            cr, ci = cmul(lr, li, ar, ai)
            ur, ui = cmul(w2r, w2i, qr[seg_rows(c, k), :], qi[seg_rows(c, k), :])
            lr, li = ur + cr, ui + ci
            if k == SEGS // 2:
                lr, li = lr * keeps[c, 1], li * keeps[c, 1]
        lr, li = lr * keeps[c, 0], li * keeps[c, 0]
        if c == 1:
            ends[pl.ds(0, MODES), :] = lr
            ends[pl.ds(MODES, MODES), :] = li
    chip[pl.ds(0, MODES), :] = lr.astype(BF16)
    chip[pl.ds(MODES, MODES), :] = li.astype(BF16)


def near_back_kernel(steps, g, prod, params, kern, near, lags):
    source = lambda c, t: group(g, steps, c, t)
    other = lambda c, t: group(prod, steps, c, t)
    sk = row(params, SKIP_ROW)
    for j, lag in enumerate(lag_sums(steps, source, other)):
        lags[pl.ds(j, 1), :] = lag
    dsk = jnp.zeros((SEGS, LANES), F32)
    for c in range(2):
        for t in range(steps):
            dsk = dsk + source(c, t) * other(c, t)
    lags[pl.ds(steps, 1), :] = jnp.sum(dsk, axis=0, keepdims=True)
    lags_apply(kern, steps, lambda c, t: sk * source(c, t), source, near, True)


def grads_kernel(steps, n_recv, base, last, core, keeps, masks, near, lags, qr, qi, rr, ri, state_r, state_i, dr, di, ends, *refs):
    recv = refs[:n_recv]
    params, tables, key, value, shifted, grad_query, normed, wk, wv, wq = refs[n_recv : n_recv + 10]
    refs = refs[n_recv + 10 :]
    if last:
        order, before_keep, before_send, before_w, *refs = refs
        grad_keep, grad_send, grad_params, *grad_kv = refs[:-8]
        pr, pi, mur, mui, back, cat, cat_w, grad_w = refs[-8:]
    else:
        before_keep = before_send = None
        grad_keep, grad_send, grad_params, grad_w, pr, pi, mur, mui, back, cat, cat_w = refs
    lane = pl.program_id(0)
    rows = steps * SEGS
    channels = grad_w.shape[0] // 2
    ids = sublanes()
    zr, zi, wr, wi = read_tables(tables)
    ar, ai = fill_powers(zr, zi, pr, pi, steps)
    w2r, w2i = 2.0 * wr, 2.0 * wi
    br, bi = over_chunk(ar, ai)
    mr, mi = incoming(recv, masks, 1, br, bi)
    zero = jnp.zeros((MODES, LANES), F32)
    awr = awi = azr = azi = acr = aci = zero
    for c in (1, 0):
        if c == 0:
            keep = keeps[1, 0] * keeps[1, 1]
            mr, mi = cmul(last_r, last_i, br * keep, bi * keep)
            mr, mi = mr + ends[pl.ds(0, MODES), :], mi + ends[pl.ds(MODES, MODES), :]
        last_r, last_i = mr, mi
        for k in reversed(range(SEGS)):
            at = seg_rows(c, k)
            mur[at, :] = mr
            mui[at, :] = mi
            s_r, s_i = state_r[at, :], state_i[at, :]
            q_r, q_i = qr[at, :], qi[at, :]
            u = cmul(s_r, s_i, q_r, q_i)
            awr, awi = awr + u[0], awi + u[1]
            u = cmul(s_r, s_i, rr[at, :], ri[at, :])
            azr, azi = azr + u[0], azi + u[1]
            u = cmul(mr, mi, dr[at, :], di[at, :])
            acr, aci = acr + u[0], aci + u[1]
            u = cmul(mr, mi, s_r, s_i)
            u = cmul(u[0], u[1], ar, ai)
            acr, aci = acr + float(steps) * u[0], aci + float(steps) * u[1]
            if k > 0:
                ur, ui = cmul(w2r, w2i, q_r, q_i)
                cr, ci = cmul(mr, mi, ar, ai)
                mr, mi = ur + cr, ui + ci
                if k == SEGS // 2:
                    mr, mi = mr * keeps[c, 1], mi * keeps[c, 1]
    for j in range(steps):
        lag = lags[pl.ds(j, 1), :]
        u, v = pr[pl.ds(j * MODES, MODES), :] * lag, pi[pl.ds(j * MODES, MODES), :] * lag
        awr, awi = awr + u, awi + v
        azr, azi = azr + float(j) * u, azi + float(j) * v
    u = cmul(w2r, w2i, azr, azi)
    _, tables_back = jax.vjp(ssm_tables, *table_inputs(params))
    dstep, *dmodes = tables_back((u[0] + acr, -(u[1] + aci), 2.0 * awr, -2.0 * awi))
    for i, v in enumerate(dmodes):
        grad_params[pl.ds(i * MODES, MODES), :] = v
    grad_params[pl.ds(STEP_ROW, 1), :] = dstep
    grad_params[pl.ds(SKIP_ROW, 1), :] = lags[pl.ds(steps, 1), :]

    def done(c, t, values):
        low = []
        for i, v in zip((t, t + 1), values):
            low.append(v * group(shifted, steps, c, i))
            put(back, steps, c, i, v * group(value, steps, c, i))
        cat[pl.ds((c * steps + t) * SEGS, 2 * SEGS), pl.ds(LANES, LANES)] = jnp.concatenate(low).astype(BF16)

    unfold(pr, pi, steps, lambda t: steps - 1 - t, (mur, mui), lambda c, t: group(near, steps, c, t), done)
    tap = [row(params, TAP_ROW + j) for j in range(TAPS)]
    windows = earlier_keys(key, steps, keeps)
    acc = [jnp.zeros((SEGS, LANES), F32)] * TAPS
    for c in range(2):
        window = windows[c]
        for t in range(steps):
            cur = group(key, steps, c, t)
            v = group(back, steps, c, t)
            for j, w in enumerate([cur] + window):
                acc[j] = acc[j] + v * w
            window = [cur] + window[:2]
    for j, a in enumerate(acc):
        grad_params[pl.ds(TAP_ROW + j, 1), :] = jnp.sum(a, axis=0, keepdims=True)
    following = [jnp.zeros((SEGS, LANES), F32)] * (TAPS - 1)
    for c in (1, 0):
        mask = seg_mask(keeps[c, 0], keeps[c, 1])
        begin = [group(back, steps, c, t) * mask for t in range(TAPS - 1)]
        later = [pltpu.roll(jnp.where(ids == 0, f, v), SEGS - 1, 0) for f, v in zip(following, begin)]
        following = begin
        ext = lambda t: group(back, steps, c, t) if t < steps else later[t - steps]
        for t in range(0, steps, 2):
            low = [
                tap[0] * ext(i) + tap[1] * ext(i + 1) + tap[2] * ext(i + 2) + tap[3] * ext(i + 3) for i in (t, t + 1)
            ]
            cat[pl.ds((c * steps + t) * SEGS, 2 * SEGS), pl.ds(0, LANES)] = jnp.concatenate(low).astype(BF16)
    edge = [jnp.zeros((HALO - TAPS + 1, LANES), F32)]
    for b in (3, 2, 1):
        v = jnp.zeros((1, LANES), F32)
        for j in range(b, TAPS):
            v = v + params[pl.ds(TAP_ROW + j, 1), :] * following[j - b][0:1, :]
        edge.append(v)
    halo_at = pl.ds(2 * rows, HALO)
    cat[halo_at, pl.ds(0, LANES)] = jnp.concatenate(edge, axis=0).astype(BF16)
    cat[halo_at, pl.ds(LANES, 2 * LANES)] = jnp.zeros((HALO, 2 * LANES), BF16)
    cat[pl.ds(0, 2 * rows), pl.ds(2 * LANES, LANES)] = grad_query[...]
    for i, w in enumerate((wk, wv, wq)):
        cat_w[pl.ds(i * LANES, LANES), :] = w[...]
    both = dot_tn(cat[:, pl.ds(0, 2 * LANES)], normed[...])
    if last:

        @pl.when(lane == 0)
        def _():
            grad_w[...] = before_w[...]

    at = (base + lane) * LANES
    grad_w[pl.ds(pl.multiple_of(at, LANES), LANES), :] = both[:LANES].astype(BF16)
    grad_w[pl.ds(pl.multiple_of(channels + at, LANES), LANES), :] = both[LANES:].astype(BF16)
    if last:

        @pl.when(lane == pl.num_programs(0) - 1)
        def _():
            part_to(grad_kv, dot_tn(order[...], grad_w[...]))

    for i, part in enumerate((2, 0, 1)):
        grad_params[pl.ds(BIAS_ROW + i, 1), :] = jnp.sum(cat[:, pl.ds(part * LANES, LANES)].astype(F32), axis=0, keepdims=True)
    me = core[0]
    for c in range(2):
        out = dot_nn(cat[pl.ds(c * rows, rows), :], cat_w[...])

        @pl.when(me == c)
        def _():
            add_to(grad_keep, pl.ds(0, rows), out, lane, before_keep)

        @pl.when(me != c)
        def _():
            add_to(grad_send, pl.ds(0, rows), out, lane, before_send)

    add_to(grad_send, pl.ds(rows, HALO), dot_nn(cat[halo_at, :], cat_w[...]), lane, before_send)


def add_to(ref, at, value, step, before):
    @pl.when(step == 0)
    def _():
        ref[at, :] = value if before is None else before[at, :] + value

    @pl.when(step > 0)
    def _():
        ref[at, :] += value


class Mixer:
    def __init__(self, rows, channels, width, groups):
        self.rows, self.channels, self.width, self.groups = rows, channels, width, groups
        self.steps = rows // SEGS

    def lanes(self, rows):
        return pl.BlockSpec((rows, LANES), lambda l: (0, l))

    def whole(self, *shape):
        return pl.BlockSpec(shape, lambda l: (0,) * len(shape))

    def shape(self, rows, kind=F32):
        return jax.ShapeDtypeStruct((rows, self.channels), kind)

    def wide(self, rows, kind):
        return jax.ShapeDtypeStruct((rows, self.width), kind)

    def call(self, name, kernel, in_specs, outs, scratch, work, powers=True, count=None):
        table = pltpu.VMEM(((self.steps + 1) * MODES, LANES), F32)
        return pl.pallas_call(
            kernel,
            grid=(count or self.channels // LANES,),
            in_specs=in_specs,
            out_specs=[s for s, _ in outs],
            out_shape=[s for _, s in outs],
            scratch_shapes=[table, table] * powers + scratch,
            compiler_params=pltpu.CompilerParams(vmem_limit_bytes=VMEM_LIMIT),
            cost_estimate=pl.CostEstimate(flops=work // 10000, bytes_accessed=work // 4000000, transcendentals=0),
            name=name,
        )

    def units(self, part=0):
        return pl.BlockSpec((LANES, self.width), lambda l: (l + part * self.channels // LANES, 0))

    def pair(self):
        n = 2 * self.channels
        return self.whole(n, self.width), self.wide(n, BF16)

    def parts(self):
        n = 2 * self.channels // self.groups
        return [(self.whole(n, self.width), self.wide(n, BF16))] * self.groups

    def order(self):
        return self.whole(2 * self.channels, 2 * self.channels)

    def before(self, core, keeps, own, sib, gain, shift, order, mixed_kv, params):
        n, ms, w = 2 * self.rows, 2 * MODES * SEGS, self.width
        line, states, ends = self.whole(1, w), (self.lanes(ms), self.shape(ms)), self.lanes(2 * MODES)
        return self.call(
            "ssm_before",
            functools.partial(before_kernel, self.steps, len(mixed_kv)),
            [SMEM, SMEM, self.whole(*own.shape), self.whole(*own.shape), line, line, self.order()]
            + [self.whole(*p.shape) for p in mixed_kv] + [self.lanes(PARAM_ROWS)],
            [(self.whole(n + HALO, w), self.wide(n + HALO, BF16)), self.pair(), (self.lanes(4 * MODES), self.shape(4 * MODES))]
            + [(self.lanes(self.steps), self.shape(self.steps))]
            + [(self.lanes(n + HALO), self.shape(n + HALO))] + [(self.lanes(n), self.shape(n))] * 3 + [states] * 4
            + [(ends, self.shape(2 * MODES)), (ends, self.shape(2 * MODES, BF16))],
            [pltpu.VMEM((2 * self.channels, w), BF16)],
            10**10,
        )(core, keeps, own, sib, gain, shift, order, *mixed_kv, params)

    def near(self, normed, prod, mixed_qo, order, params, kern):
        n, w = 2 * self.rows, self.width
        big = self.lanes(n)
        return self.call(
            "ssm_near",
            functools.partial(near_kernel, self.steps, len(mixed_qo)),
            [self.whole(*normed.shape), big] + [self.whole(*p.shape) for p in mixed_qo]
            + [self.order(), self.lanes(PARAM_ROWS), self.lanes(self.steps)],
            [self.pair(), (big, self.shape(n)), (big, self.shape(n))],
            [pltpu.VMEM((2 * self.channels, w), BF16)],
            6 * 10**9,
            False,
        )(normed, prod, *mixed_qo, order, params, kern)

    def conv(self, keeps, masks, near, query, er, ei, ends, recv, wqo, tables):
        n, ms, w = 2 * self.rows, 2 * MODES * SEGS, self.width
        big, states, last = self.lanes(n), self.lanes(ms), self.lanes(2 * MODES)
        return self.call(
            "ssm_conv",
            functools.partial(conv_kernel, self.steps, len(recv)),
            [SMEM, SMEM, big, big, states, states] + [last] * (1 + len(recv)) + [self.units(1), self.lanes(4 * MODES)],
            [(big, self.shape(n)), (big, self.shape(n, BF16))] + [(states, self.shape(ms))] * 2
            + [(self.whole(n, w), self.wide(n, BF16))],
            [pltpu.VMEM((ms, LANES), F32)] * 2 + [pltpu.VMEM((n, w), F32)],
            10**10,
        )(keeps, masks, near, query, er, ei, ends, *recv, wqo, tables)

    def after(
        self, core, keeps, residual, grad_own, grad_sib, cot_own, cot_sib, gain, order, wqo, normed, query, conv, core_low,
        tables,
    ):
        n, ms, w = 2 * self.rows, 2 * MODES * SEGS, self.width
        big, states, last = self.lanes(n), self.lanes(ms), self.lanes(2 * MODES)
        full, half = self.whole(n, w), self.whole(n // 2, w)
        return self.call(
            "ssm_after",
            functools.partial(after_kernel, self.steps),
            [SMEM, SMEM, full, full, full, half, half, self.whole(1, w), self.order(), self.units(1), self.whole(*normed.shape)]
            + [big] * 3 + [self.lanes(4 * MODES)],
            [(full, self.wide(n, F32)), (big, self.shape(n)), (big, self.shape(n, BF16))]
            + [(states, self.shape(ms))] * 4 + [(last, self.shape(2 * MODES)), (last, self.shape(2 * MODES, BF16))]
            + [(self.whole(4, w), self.wide(4, F32))] + self.parts(),
            [pltpu.VMEM((n, w), BF16), pltpu.VMEM((n, LANES), F32), pltpu.VMEM((2 * self.channels, w), BF16)],
            10**10,
        )(
            core, keeps, residual, grad_own, grad_sib, cot_own, cot_sib, gain, order, wqo, normed, query, conv, core_low,
            tables,
        )

    def near_back(self, g, prod, params, kern):
        big = self.lanes(2 * self.rows)
        tall = self.steps + SEGS
        return self.call(
            "ssm_near_back",
            functools.partial(near_back_kernel, self.steps),
            [big, big, self.lanes(PARAM_ROWS), self.lanes(self.steps)],
            [(big, self.shape(2 * self.rows)), (self.lanes(tall), self.shape(tall))],
            [],
            8 * 10**9,
            False,
        )(g, prod, params, kern)

    def grads(
        self, base, count, core, keeps, masks, near, lags, q, state, d, ends, recv, params, tables, key, value, shifted,
        grad_query, normed, wkv, wqo, order, before,
    ):
        n, ms, w = 2 * self.rows, 2 * MODES * SEGS, self.width
        lanes = lambda rows: pl.BlockSpec((rows, LANES), lambda l: (0, l + base))
        units = lambda part: pl.BlockSpec((LANES, w), lambda l: (l + base + part * self.channels // LANES, 0))
        big, states, ends_at = lanes(n), lanes(ms), lanes(2 * MODES)
        normed_at = [(self.whole(r, w), self.wide(r, F32)) for r in (self.rows, self.rows + HALO)]
        params_at = (lanes_from(PARAM_ROWS), jax.ShapeDtypeStruct((PARAM_ROWS, count * LANES), F32))
        last = before is not None
        return self.call(
            "ssm_grads_last" if last else "ssm_grads",
            functools.partial(grads_kernel, self.steps, len(recv), base, last),
            [SMEM, SMEM, SMEM, big, lanes(lags.shape[0])] + [states] * 8 + [ends_at] * (1 + len(recv))
            + [lanes(PARAM_ROWS), lanes(4 * MODES), lanes(n + HALO), big, big, big, self.whole(*normed.shape)]
            + [units(0), units(1), units(0)] + [self.order(), normed_at[0][0], normed_at[1][0], self.pair()[0]] * last,
            [*normed_at, params_at] + (self.parts() if last else [self.pair()]),
            [pltpu.VMEM((ms, LANES), F32)] * 2
            + [pltpu.VMEM((n, LANES), F32), pltpu.VMEM((n + HALO, 3 * LANES), BF16), pltpu.VMEM((3 * LANES, w), BF16)]
            + [pltpu.VMEM((2 * self.channels, w), BF16)] * last,
            10**9,
            True,
            count,
        )(
            core, keeps, masks, near, lags, *q, *state, *d, ends, *recv, params, tables, key, value, shifted, grad_query,
            normed, wkv, wkv, wqo, *([order, *before] if last else []),
        )


def lanes_from(rows):
    return pl.BlockSpec((rows, LANES), lambda l: (0, l))


def tail_kernel(steps, shard, core, keep, send, own, sib, sums, params_most, params_rest, bias, tail, rows_of):
    rows = steps * SEGS
    me, me_chip = core[0], core[1]
    total = [jnp.zeros((1, keep.shape[1]), F32)] * 2

    def more(total, grad, x):
        xhat, _ = normalize(x)
        return [t + jnp.sum(v, axis=0, keepdims=True) for t, v in zip(total, (grad * xhat, grad))]

    for r in range(0, rows, LN_TILE):
        at = pl.ds(r, LN_TILE)
        total = more(total, keep[at, :], own[at, :].astype(F32))
        total = more(total, send[at, :], sib[at, :].astype(F32))
    edge = pl.ds(rows, HALO)
    total = more(total, send[edge, :], chunk_of(own, sib, me, 1, edge))
    features = jnp.concatenate([*total, sums[...]], axis=0).astype(BF16)
    params = jnp.concatenate([params_most[...], params_rest[...]], axis=1).astype(BF16)
    chips, deep = tail.shape[0], tail.shape[1]
    rows_of[...] = jnp.zeros_like(rows_of)

    def columns(x, first):
        width = x.shape[1]
        i = lax.broadcasted_iota(jnp.int32, (width, LANES), 0)
        j = lax.broadcasted_iota(jnp.int32, (width, LANES), 1)
        pick = jnp.where(jnp.logical_and(i == first + j, j < shard), 1.0, 0.0).astype(BF16)
        return dot_nn(x, pick)

    for k in range(chips):
        z = lax.rem(me_chip - k + chips, chips)
        rows_of[pl.ds(0, PARAM_ROWS), :] = columns(params, z * shard)
        rows_of[pl.ds(PARAM_ROWS, 6), :] = columns(features, (2 * z + me) * shard)
        rows_of[pl.ds(PARAM_ROWS + 6, 2), :] = columns(features, (2 * z + 1 - me) * shard)[0:2]
        rows_of[pl.ds(PARAM_ROWS + 8, bias.shape[1]), :] = bias[k]
        for i in range(tail.shape[2] // LANES):
            tail[k, :, pl.ds(i * LANES, LANES)] = rows_of[pl.ds(i * deep, deep), :].astype(BF16)


def tail_of(core, keep, send, own, sib, sums, params_most, params_rest, bias, shard):
    width = keep.shape[1]
    across = width // LANES
    used = PARAM_ROWS + 8 + bias.shape[1]
    deep = -(-used // (across * 16)) * 16
    vmem = pl.BlockSpec(memory_space=pltpu.VMEM)
    return pl.pallas_call(
        functools.partial(tail_kernel, keep.shape[0] // SEGS, shard),
        in_specs=[SMEM] + [vmem] * 8,
        out_shape=jax.ShapeDtypeStruct((bias.shape[0], deep, width), BF16),
        scratch_shapes=[pltpu.VMEM((across * deep, LANES), F32)],
        compiler_params=pltpu.CompilerParams(vmem_limit_bytes=VMEM_LIMIT),
        cost_estimate=pl.CostEstimate(flops=10**6, bytes_accessed=10**4, transcendentals=0),
        name="tail_of",
    )(core, keep, send, own, sib, sums, params_most, params_rest, bias)


def finish_kernel(steps, core, keep, from_sib, edge, own, grad_residual, gain, out, total):
    rows = steps * SEGS
    total[...] = keep[...] + from_sib[pl.ds(0, rows), :]
    for b in range(1, TAPS):
        total[pl.ds((steps - b) * SEGS + SEGS - 1, 1), :] += edge[pl.ds(HALO - b, 1), :]
    first = pl.multiple_of(core[0] * rows, rows)
    for r in range(0, rows, LN_TILE):
        at = pl.ds(r, LN_TILE)
        xhat, scale = normalize(own[at, :].astype(F32))
        res = grad_residual[pl.ds(first + r, LN_TILE), :]
        out[at, :] = (res + normalize_back(total[at, :], gain[...], xhat, scale)).astype(BF16)


def finish(core, keep, from_sib, edge, own, grad_residual, gain):
    rows, width = keep.shape
    vmem = pl.BlockSpec(memory_space=pltpu.VMEM)
    return pl.pallas_call(
        functools.partial(finish_kernel, rows // SEGS),
        in_specs=[SMEM] + [vmem] * 6,
        out_shape=jax.ShapeDtypeStruct((rows, width), BF16),
        scratch_shapes=[pltpu.VMEM((rows, width), F32)],
        compiler_params=pltpu.CompilerParams(vmem_limit_bytes=VMEM_LIMIT),
        cost_estimate=pl.CostEstimate(flops=10**6, bytes_accessed=10**4, transcendentals=0),
        name="finish",
    )(core, keep, from_sib, edge, own, grad_residual, gain)


def feed_forward_kernel(reads, writes, first, n_arrays, n_outs, core, bias, lines, *refs):
    n_state = 6 if first else 5
    state, arrays, refs = refs[:n_state], refs[n_state : n_state + n_arrays], refs[n_state + n_arrays :]
    n_kept = 6 if first else 3
    kept, grad_bias, outs, refs = refs[:n_kept], refs[n_kept], refs[n_kept + 1 : n_kept + 1 + n_outs], refs[n_kept + 1 + n_outs :]
    held, refs = refs[:n_state], refs[n_state:]
    branch, grad_x, refs = refs[:2], refs[2], refs[3:]
    if first:
        own, sib, mixed_own, mixed_sib, c_own, c_sib = held
        residual, xs, cs, refs = *refs[:3], refs[3:]
    else:
        *branch_in, grad_in, xs, cs = held
    acts, backs, weights, grads, state_sems, read_sems, kept_sems, write_sems = refs
    me = core[0]
    half = xs.shape[0] // 2
    n_sets, units = bias.shape
    tiles = 2 * half // TILE

    def place(buffer, s, which, row, n):
        return buffer.at[which, pl.ds(s * units + row, n), :]

    def taken(i):
        return pltpu.make_async_copy(state[i], held[i], state_sems.at[i])

    def incoming(s, i):
        array, at, which, row, n = reads[s][i]
        return pltpu.make_async_copy(
            arrays[array].at[pl.ds(at, n), :], place(weights, s, which, row, n), read_sems.at[s, i]
        )

    def outgoing(s, i):
        array, slot, at, which, row, n = writes[s][i]
        return pltpu.make_async_copy(
            place(grads, s, which, row, n), outs[array].at[slot, pl.ds(at, n), :], write_sems.at[s, i]
        )

    def leaving(what, r, to=0):
        at = pl.ds(r * TILE, TILE)
        if what == 0:
            rows = pl.ds(r * TILE % half, TILE)
            return pltpu.make_async_copy(branch[r * TILE // half].at[rows, :], kept[to].at[rows, :], kept_sems.at[0, r])
        if what == 1:
            return pltpu.make_async_copy(grad_x.at[at, :], kept[2].at[at, :], kept_sems.at[1, r])
        return pltpu.make_async_copy((residual, xs, cs)[r], kept[3 + r], kept_sems.at[2, r])

    for i in range(n_state):
        taken(i).start()
    for s in range(n_sets):
        for i in range(len(reads[s])):
            incoming(s, i).start()
    for i in range(n_state):
        taken(i).wait()
    for c in range(2 if first else 0):
        for r in range(0, half, LN_TILE):
            at, part = pl.ds(c * half + r, LN_TILE), pl.ds(r, LN_TILE)
            v = chunk_of(own, sib, me, c, part) + mixed_own[at, :].astype(F32) + mixed_sib[at, :].astype(F32)
            v = v + lines[pl.ds(0, 1), :]
            residual[at, :] = v
            xhat, _ = normalize(v)
            xs[at, :] = (xhat * lines[pl.ds(1, 1), :] + lines[pl.ds(2, 1), :]).astype(BF16)
            cs[at, :] = chunk_of(c_own, c_sib, me, c, part).astype(BF16)
    for i in range(3 if first else 0):
        leaving(2, i).start()
    for s in range(n_sets):
        for i in range(len(reads[s])):
            incoming(s, i).wait()
    total = [jnp.zeros((1, units), F32)] * n_sets
    for r in range(0, 2 * half, TILE):
        at = pl.ds(r, TILE)
        c, place_of = r // half, pl.ds(r % half, TILE)
        for s in range(n_sets):
            mine = pl.ds(s * units, units)
            v = dot_nt(xs[at, :], weights[0, mine, :]) + bias[pl.ds(s, 1), :]
            square = v * v
            th = jnp.tanh(v * (0.79788456 + 0.79788456 * 0.044715 * square))
            half_up = 0.5 + 0.5 * th
            slope = half_up + v * (0.5 - 0.5 * th * th) * (0.79788456 + 0.79788456 * 3.0 * 0.044715 * square)
            back = dot_nt(cs[at, :], weights[1, mine, :]) * slope
            acts[at, mine] = (v * half_up).astype(BF16)
            low = back.astype(BF16)
            backs[at, mine] = low
            total[s] = total[s] + jnp.sum(low.astype(F32), axis=0, keepdims=True)
        out = dot_nn(acts[at, :], weights[1])
        grad = dot_nn(backs[at, :], weights[0])
        grad_x[at, :] = (grad if first else grad_in[at, :] + grad).astype(grad_x.dtype)
        leaving(1, r // TILE).start()
        if not first:
            out = out + jnp.where(me == c, branch_in[0][place_of, :], branch_in[1][place_of, :])
        branch[c][place_of, :] = out

        @pl.when(me == c)
        def _():
            leaving(0, r // TILE, 0).start()

        @pl.when(me != c)
        def _():
            leaving(0, r // TILE, 1).start()

    for s in range(n_sets):
        mine = pl.ds(s * units, units)
        grad_bias[pl.ds(s, 1), :] = total[s]
        for which, (left, right) in enumerate(((backs, xs), (acts, cs))):
            grads[which, mine, :] = dot_tn(left[:, mine], right[...]).astype(BF16)
            for i in range(len(writes[s])):
                if writes[s][i][3] == which:
                    outgoing(s, i).start()
    for r in range(tiles):
        leaving(0, r).wait()
        leaving(1, r).wait()
    for i in range(3 if first else 0):
        leaving(2, i).wait()
    for s in range(n_sets):
        for i in range(len(writes[s])):
            outgoing(s, i).wait()


def feed_forward(core, bias, lines, state, arrays, reads, out_shapes, writes, final):
    first = len(state) > 5
    width = state[2].shape[1]
    rows = state[4].shape[0] * 2 if first else state[2].shape[0]
    n_sets, units = bias.shape
    full, low = ((rows, width), F32), ((rows, width), BF16)
    part = ((rows // 2, width), F32)
    kept = [part, part, low if final else full] + [full, low, low] * first
    vmem, hbm = pl.BlockSpec(memory_space=pltpu.VMEM), pl.BlockSpec(memory_space=pl.ANY)
    shapes = [jax.ShapeDtypeStruct(*x) for x in kept]
    buffers = [pltpu.VMEM(x.shape, x.dtype) for x in state]
    buffers += [pltpu.VMEM(*x) for x in kept]
    out = pl.pallas_call(
        functools.partial(feed_forward_kernel, reads, writes, first, len(arrays), len(out_shapes)),
        in_specs=[SMEM, vmem, vmem] + [hbm] * (len(state) + len(arrays)),
        out_specs=[hbm] * len(kept) + [vmem] + [hbm] * len(out_shapes),
        out_shape=shapes + [jax.ShapeDtypeStruct(bias.shape, F32)]
        + [jax.ShapeDtypeStruct((n, rows_of, width), BF16) for n, rows_of in out_shapes],
        scratch_shapes=buffers
        + [pltpu.VMEM((rows, n_sets * units), BF16)] * 2 + [pltpu.VMEM((2, n_sets * units, width), BF16)] * 2
        + [
            pltpu.SemaphoreType.DMA((len(state),)),
            pltpu.SemaphoreType.DMA((n_sets, max(map(len, reads)))),
            pltpu.SemaphoreType.DMA((3, max(rows // TILE, 3))),
            pltpu.SemaphoreType.DMA((n_sets, max(map(len, writes)))),
        ],
        compiler_params=pltpu.CompilerParams(vmem_limit_bytes=VMEM_LIMIT),
        cost_estimate=pl.CostEstimate(flops=10**6, bytes_accessed=10**4, transcendentals=0),
        name="feed_forward" if first else "feed_forward_more",
    )(core, bias, lines, *state, *arrays)
    return out[: len(kept) + 1], out[len(kept) + 1 :]


def local(
    groups, chips,
    hidden_in, mix_gain, mix_shift, w_query, bias_query, w_key, bias_key, w_value, bias_value, shift_taps,
    log_step, log_decay, frequency, out_real, out_imag, skip_gain, w_out, bias_out, mlp_gain, mlp_shift,
    w_up, bias_up, w_down, bias_down, cotangent, seq_blocks,
):
    rows, width = hidden_in.shape
    shard, shard_units = w_query.shape[1], w_up.shape[1]
    chans, channels = 2 * chips, chips * shard
    cut, unit_cut = shard // groups, shard_units // groups
    steps = rows // SEGS
    me_group, me_chan = lax.axis_index("group"), lax.axis_index("chan")
    me_chip, me_core = me_chan // 2, me_chan % 2
    same_core = [[2 * z + k for z in range(chips)] for k in range(2)]
    square = groups == 4

    def swap_z(x):
        return lax.all_to_all(x, "chan", 0, 0, axis_index_groups=same_core, tiled=True)

    def group_swap(x, bits):
        return lax.ppermute(x, "group", [(i, i ^ bits) for i in range(groups)])

    def sibling(x):
        return lax.ppermute(x, "chan", [(i, i ^ 1) for i in range(chans)])

    def chip_shift(x, by):
        pairs = [(i, i + 2 * by) for i in range(chans) if 0 <= i + 2 * by < chans]
        return lax.ppermute(x, "chan", pairs)

    def chip_turn(x, by):
        return lax.ppermute(x, "chan", [(i, (i + 2 * by) % chans) for i in range(chans)])

    def gather_z(x):
        return jnp.concatenate([x] + [chip_turn(x, by) for by in range(1, chips)])

    def gather_group(x):
        return [x] + [group_swap(x, r) for r in range(1, groups)]

    def add(*xs):
        return sum(x.astype(F32) for x in xs).astype(BF16)

    def fold_z(parts):
        return add(parts[0], *(chip_turn(p, -by) for by, p in enumerate(parts) if by))

    def fold_group(parts):
        return add(parts[0], *(group_swap(p, r) for r, p in enumerate(parts) if r))

    def pieces(x, count):
        n = x.shape[0] // count
        return [x[i * n : (i + 1) * n] for i in range(count)]

    def by_index(parts):
        out = []
        for g in range(groups):
            x = parts[0]
            for r in range(1, groups):
                x = jnp.where(me_group == g ^ r, parts[r], x)
            out.append(x)
        return jnp.stack(out)

    def first_round(a):
        return (group_swap(a, 1), group_swap(a, 2)) if square else tuple(gather_group(a)[1:])

    def second_round(one):
        n = one[0].shape[0] // 2
        return (group_swap(one[1][:n], 1), group_swap(one[0][n:], 2)) if square else ()

    def fold_first(send_a, send_b):
        return [group_swap(x, 1) for x in send_a], [group_swap(x, 2) for x in send_b]

    def fold_second(one, ay, bx):
        return group_swap(add(ay, one[0][1]), 2), group_swap(add(bx, one[1][1]), 1)

    def fold_end(one, two, a0, b0):
        return add(a0, one[0][0], two[0]), add(b0, one[1][0], two[1])

    def fence(*xs):
        return lax.optimization_barrier(xs)

    def share(x):
        return lax.dynamic_index_in_dim(x.reshape(groups, -1, width), me_group, 0, keepdims=False)

    def to_steps(x):
        return x.reshape(SEGS, steps, width).transpose(1, 0, 2).reshape(rows, width)

    def to_rows(x):
        return x.reshape(steps, SEGS, width).transpose(1, 0, 2).reshape(rows, width)

    first = seq_blocks[0, 0]
    second = first + seq_blocks[0, 1]

    def keep(block):
        starts = (block == 0) | (block == first) | (block == second)
        return jnp.where(starts, 0.0, 1.0).astype(F32)

    blocks = 4 * me_chip + jnp.arange(4)
    keeps = keep(blocks).reshape(2, 2)
    near = me_chip + jnp.stack([-jnp.arange(chips), jnp.arange(chips)])
    masks = jnp.prod(keep(4 * near[..., None] + jnp.arange(4)), axis=-1)

    def two_shares(a, b):
        return jnp.concatenate([share(a), share(b)])

    turns = (me_chip - jnp.arange(chips)) % chips
    flips = me_group ^ jnp.arange(groups)
    place = flips[None, None, :, None] * chips + turns[None, :, None, None]
    place = (place * 2 + jnp.arange(2)[:, None, None, None]) * cut + jnp.arange(cut)
    order = (place.reshape(-1, 1) == jnp.arange(2 * channels)).astype(BF16)
    z_turn = (turns[:, None] == jnp.arange(chips)).astype(F32)
    g_flip = (flips[:, None] == jnp.arange(groups)).astype(F32)
    exact = lax.Precision.HIGHEST

    core = jnp.stack([me_core, me_chip])
    line = lambda x: x.reshape(1, width)
    kv_z = gather_z(two_shares(w_key.T, w_value.T))
    edge = lax.ppermute(hidden_in[rows - HALO :], "chan", [(2 * z + 1, 2 * z + 3) for z in range(chips - 1)])
    own = jnp.concatenate([to_steps(hidden_in), edge])
    kv_z, own, w_query, w_out, w_up, w_down, cotangent, log_decay, frequency, out_real, out_imag = fence(
        kv_z, own, w_query, w_out, w_up, w_down, cotangent, log_decay, frequency, out_real, out_imag
    )

    mixed_kv = gather_group(kv_z)
    small = jnp.concatenate(
        [
            log_decay.T, frequency.T, out_real.T, out_imag.T, shift_taps.T,
            jnp.stack([log_step, skip_gain, bias_query, bias_key, bias_value]),
            bias_up.reshape(shard_units // shard, shard),
        ]
    )
    small = swap_z(jnp.broadcast_to(small, (chips,) + small.shape))
    sib = sibling(own)
    qo_z = gather_z(two_shares(w_query.T, w_out))
    params = jnp.moveaxis(small[:, :PARAM_ROWS], 0, 1).reshape(PARAM_ROWS, channels)
    units_bias = small[:, PARAM_ROWS:].reshape(chips, groups, unit_cut)
    units_bias = jnp.einsum("rg,zgu->rzu", g_flip, units_bias, precision=exact).reshape(groups, -1)
    mixed_kv, sib, qo_z, params, units_bias, order, keeps, masks, w_up, w_down, cotangent = fence(
        mixed_kv, sib, qo_z, params, units_bias, order, keeps, masks, w_up, w_down, cotangent
    )

    ff_z = two_shares(w_up.T, w_down)
    ff_z = swap_z(jnp.broadcast_to(ff_z, (chips,) + ff_z.shape))
    mixed_qo = gather_group(qo_z)
    mixer = Mixer(rows, channels, width, groups)
    normed, wkv, tables, kern, key, value, prod, shifted, er, ei, dr, di, ends, chip = mixer.before(
        core, keeps, own, sib, line(mix_gain), line(mix_shift), order, mixed_kv, params
    )
    chip, ends, cotangent, mixed_qo = fence(chip, ends, cotangent, mixed_qo)

    recv = [chip_shift(chip, by) for by in range(1, chips)]
    wqo, query, near = mixer.near(normed, prod, mixed_qo, order, params, kern)
    cot = to_steps(cotangent)
    recv, near, ff_z, cot = fence(recv, near, ff_z, cot)

    if not square:
        ff_z = jnp.moveaxis(ff_z.reshape(chips, 2, unit_cut, width), 1, 0)
    ff_z = ff_z.reshape(-1, width)
    ff_one = first_round(ff_z)
    cot_sib = sibling(cot)
    conv, core_low, state_r, state_i, mixed = mixer.conv(
        keeps, masks, near, query, er, ei, ends, recv, wqo, tables
    )
    mixed, cot_sib, ff_one = fence(mixed, cot_sib, ff_one)

    mixed_sib = sibling(mixed)
    ff_two = second_round(ff_one)
    (mixed_sib,) = fence(mixed_sib)

    units = chips * unit_cut
    if square:
        arrays = [ff_z, *ff_one]
        near_half = chips // 2

        def rows_of(z, which):
            return (z % near_half * 2 + which) * unit_cut

        every = [(z, which) for z in range(chips) for which in range(2)]
        reads = [
            [(s, (z * 2 + w) * unit_cut, w, z * unit_cut, unit_cut) for z, w in every] for s in range(3)
        ] + [[(z // near_half, rows_of(z, w), w, z * unit_cut, unit_cut) for z, w in every]]
        to = ((0, 3), (2, 4), (1, 5), (0, 1))
        slots = ((0, 0),) * 4
        writes = [
            [
                (to[s][z // near_half], slots[s][z // near_half], rows_of(z, w), w, z * unit_cut, unit_cut)
                for z, w in every
            ]
            for s in range(4)
        ]
        out_shapes = [(1, units)] * 2 + [(1, units)] + [(1, units)] * 2 + [(1, units)]
    else:
        arrays = [ff_z, *ff_one]
        reads = [[(s, w * units, w, 0, units) for w in range(2)] for s in range(groups)]
        writes = [[(s, 0, w * units, w, 0, units) for w in range(2)] for s in range(groups)]
        out_shapes = [(1, 2 * units)] * groups
    lines = jnp.stack([bias_out, mlp_gain, mlp_shift])
    state = (own, sib, mixed, mixed_sib, cot, cot_sib)
    n_first = 3 if square else groups
    (*branch, grad_two, residual, xs, cs, grad_units_bias), grad_ff = feed_forward(
        core, units_bias[:n_first], lines, state, arrays[:n_first], reads[:n_first], out_shapes, writes[:n_first], not square
    )
    if square:
        branch, grad_two, xs, cs, ff_two = fence(branch, grad_two, xs, cs, ff_two)
        (*branch, grad_two, more_bias), grad_diagonal = feed_forward(
            core, units_bias[3:], lines, (*branch, grad_two, xs, cs), ff_two, reads[3:], [(1, units)] * 2, writes[3:], True
        )
        grad_units_bias = jnp.concatenate([grad_units_bias, more_bias])

    branch_own = branch[0]
    grad_two_sib, branch_sib = sibling(grad_two), sibling(branch[1])
    if square:
        fold_one = fold_first((grad_ff[2][0], grad_diagonal[0][0]), (grad_ff[5][0], grad_diagonal[1][0]))
    else:
        fold_one = ()
    after = mixer.after(
        core, keeps, residual, grad_two, grad_two_sib, cot, cot_sib, line(mlp_gain), order, wqo, normed, query, conv,
        core_low, tables,
    )
    grad_residual, g, grad_query, *qsums, ends, chip, sums = after[:10]
    grad_qo = after[10:]
    chip, grad_qo, branch_own, branch_sib, ends, g = fence(chip, grad_qo, branch_own, branch_sib, ends, g)

    recv = [chip_shift(chip, -by) for by in range(1, chips)]
    near, lags = mixer.near_back(g, prod, params, kern)
    recv, near, lags, fold_one, grad_qo = fence(recv, near, lags, fold_one, grad_qo)

    bias_rows = grad_units_bias.reshape(groups, chips, unit_cut)
    bias_rows = jnp.einsum("kz,rg,rzu->kgu", z_turn, g_flip, bias_rows, precision=exact)
    bias_rows = jnp.pad(bias_rows.reshape(chips, -1, shard), ((0, 0), (0, 0), (0, LANES - shard)))
    used = PARAM_ROWS + 8 + bias_rows.shape[1]

    fold_two = fold_second(fold_one, grad_ff[1][0], grad_ff[4][0]) if square else ()
    blocks = channels // LANES
    grads_of = lambda base, count, before: mixer.grads(
        base, count, core, keeps, masks, near, lags, qsums, (state_r, state_i), (dr, di), ends, recv, params, tables, key,
        value, shifted, grad_query, normed, wkv, wqo, order, before,
    )
    grad_keep, grad_send, params_most, grad_w = grads_of(0, 1, None)
    fold_two, grad_keep, grad_w = fence(fold_two, grad_keep, grad_w)

    if square:
        ff = jnp.concatenate(fold_end(fold_one, fold_two, grad_ff[0][0], grad_ff[3][0]))
    else:
        ff = fold_group([x[0] for x in grad_ff]).reshape(2, chips, unit_cut, width)
        ff = jnp.moveaxis(ff, 1, 0)
    ff = ff.reshape(chips, 2 * unit_cut, width)
    ff = [lax.dynamic_index_in_dim(ff, (me_chip + k) % chips, 0, keepdims=False) for k in range(chips)]
    ff_odd = [chip_turn(ff[k], k) for k in range(1, chips, 2)]
    grad_keep, grad_send, params_rest, *grad_kv = grads_of(1, blocks - 1, (grad_keep, grad_send, grad_w))
    grad_kv, grad_keep, grad_send, params_rest, ff, ff_odd, grad_qo = fence(
        grad_kv, grad_keep, grad_send, params_rest, ff, ff_odd, grad_qo
    )

    kv = fold_group(grad_kv)
    ff = add(ff[0], *ff_odd, *(chip_turn(ff[k], k) for k in range(2, chips, 2)))
    from_sib = sibling(grad_send)
    tail = tail_of(core, grad_keep, grad_send, own, sib, sums, params_most, params_rest, bias_rows, shard)
    edge = grad_send[rows:] + from_sib[rows:]
    edge = lax.ppermute(edge, "chan", [(2 * z + 3, 2 * z + 1) for z in range(chips - 1)])
    kv, tail, ff, from_sib, edge = fence(kv, tail, ff, from_sib, edge)

    qo = fold_group(grad_qo)
    kv = fold_z([jnp.concatenate(p) for p in zip(pieces(kv, chips), tail)])
    ff = gather_group(ff)
    mine = lax.dynamic_slice_in_dim(residual, me_core * rows, rows, axis=0)
    output = to_rows((mine + branch_own + branch_sib + bias_down).astype(BF16))
    grad_input = to_rows(finish(core, grad_keep, from_sib, edge, own, grad_residual, line(mix_gain)))
    qo = fold_z(pieces(qo, chips))
    kv, qo, output, grad_input, ff = fence(kv, qo, output, grad_input, ff)

    kv = gather_group(kv)
    qo = gather_group(qo)
    grad_wf = by_index(ff).reshape(groups, 2, unit_cut, width)
    grad_wf = jnp.moveaxis(grad_wf, 1, 0).reshape(2, shard_units, width).astype(F32)

    def halves(parts):
        x = by_index(parts).reshape(groups, 2, cut, width)
        return jnp.moveaxis(x, 1, 0).reshape(2, shard, width).astype(F32)

    (grad_wk, grad_wv), (grad_wq, grad_wo) = halves([x[: 2 * cut] for x in kv]), halves(qo)
    tail = sum(x[2 * cut :].astype(F32) for x in kv)
    tail = tail.reshape(-1, width // LANES, LANES).transpose(1, 0, 2).reshape(-1, LANES)[:used, :shard]
    modes = [tail[i * MODES : (i + 1) * MODES].T for i in range(4)]
    biases = tail[BIAS_ROW:PARAM_ROWS]
    feat_part = tail[PARAM_ROWS : PARAM_ROWS + 6]
    first_two = feat_part[:2] + sibling(tail[PARAM_ROWS + 6 : PARAM_ROWS + 8])
    sum_bias_up = tail[PARAM_ROWS + 8 :].reshape(shard_units)
    return (
        output,
        grad_input,
        first_two[0],
        first_two[1],
        grad_wq.T,
        biases[0],
        grad_wk.T,
        biases[1],
        grad_wv.T,
        biases[2],
        tail[TAP_ROW : TAP_ROW + TAPS].T,
        tail[STEP_ROW],
        modes[0],
        modes[1],
        modes[2],
        modes[3],
        tail[SKIP_ROW],
        grad_wo,
        feat_part[2],
        feat_part[3],
        feat_part[4],
        grad_wf[0].T,
        sum_bias_up,
        grad_wf[1],
        feat_part[5],
    )


def solution(mesh):
    rows = P(("group", "chan"), None)
    columns, channels, vector, copied = P(None, "chan"), P("chan", None), P("chan"), P()
    return jax.shard_map(
        functools.partial(local, mesh.shape["group"], mesh.shape["chan"] // 2),
        mesh=mesh,
        in_specs=(
            rows, copied, copied, columns, vector, columns, vector, columns, vector, channels,
            vector, channels, channels, channels, channels, vector, channels, copied, copied, copied,
            columns, vector, channels, copied, rows, P("group", None),
        ),
        out_specs=(
            rows, rows, vector, vector, columns, vector, columns, vector, columns, vector,
            channels, vector, channels, channels, channels, channels, vector, channels, vector, vector,
            vector, columns, vector, channels, vector,
        ),
        check_vma=False,
    )
```

```python
import functools

import jax
import jax.numpy as jnp
import numpy as np
from jax import lax
from jax.experimental import pallas as pl
from jax.experimental.pallas import tpu as pltpu
from jax.sharding import PartitionSpec as P

F32 = jnp.float32
BF16 = jnp.bfloat16
MODES = 32
LANES = 128
SEGS = 8
TAPS = 4
BLOCK = 8
HALO = 16
TILE = 128
LN_TILE = 64
EPSILON = 1e-05
VMEM_LIMIT = 60 * 1024 * 1024
SMEM = pl.BlockSpec(memory_space=pltpu.SMEM)

TAP_ROW = 4 * MODES
STEP_ROW = TAP_ROW + TAPS
SKIP_ROW = STEP_ROW + 1
BIAS_ROW = SKIP_ROW + 1
PARAM_ROWS = BIAS_ROW + 3


def ssm_tables(log_step, log_decay, frequency, out_real, out_imag):
    step_size = jnp.exp(log_step)
    rate = -jnp.exp(log_decay)
    decay = rate * step_size
    turn = frequency * step_size
    growth = jnp.exp(decay)
    ratio_re = growth * jnp.cos(turn) - 1.0
    ratio_im = growth * jnp.sin(turn)
    denom = rate * rate + frequency * frequency
    scaled_re = (ratio_re * rate + ratio_im * frequency) / denom
    scaled_im = (ratio_im * rate - ratio_re * frequency) / denom
    weight_re = out_real * scaled_re - out_imag * scaled_im
    weight_im = out_real * scaled_im + out_imag * scaled_re
    return decay, turn, weight_re, weight_im


def table_inputs(params):
    parts = [params[pl.ds(i * MODES, MODES), :] for i in range(4)]
    return [params[pl.ds(STEP_ROW, 1), :], *parts]


def read_tables(tables):
    return [tables[pl.ds(i * MODES, MODES), :] for i in range(4)]


def dot_nn(a, b):
    return lax.dot_general(a, b, (((1,), (0,)), ((), ())), preferred_element_type=F32)


def dot_nt(a, b):
    return lax.dot_general(a, b, (((1,), (1,)), ((), ())), preferred_element_type=F32)


def dot_tn(a, b):
    return lax.dot_general(a, b, (((0,), (0,)), ((), ())), preferred_element_type=F32)


def cmul(ar, ai, br, bi):
    return ar * br - ai * bi, ar * bi + ai * br


def normalize(values):
    center = values - jnp.mean(values, axis=-1, keepdims=True)
    scale = lax.rsqrt(jnp.mean(center * center, axis=-1, keepdims=True) + EPSILON)
    return center * scale, scale


def normalize_back(grad, gain, xhat, scale):
    gy = grad * gain
    mean_gy = jnp.mean(gy, axis=-1, keepdims=True)
    mean_gx = jnp.mean(gy * xhat, axis=-1, keepdims=True)
    return scale * (gy - mean_gy - xhat * mean_gx)


def pack_kernel(decay, freq, real, imag, taps, step, skip, bias_q, bias_k, bias_v, bias_up, out, rows_of):
    shard = decay.shape[1]
    at = 0
    for x in (decay, freq, real, imag, taps):
        n = x.shape[0]
        rows_of[pl.ds(at, n), :] = x[...]
        at += n
    for x in (step, skip, bias_q, bias_k, bias_v):
        rows_of[pl.ds(at, 1), :] = x[...]
        at += 1
    for i in range(bias_up.shape[1] // shard):
        rows_of[pl.ds(at + i, 1), :] = bias_up[:, pl.ds(i * shard, shard)]
    for i in range(out.shape[0]):
        out[i] = rows_of[...]


def pack(chips, matrices, vectors, bias_up):
    shard = matrices[0].shape[1]
    rows = PARAM_ROWS + bias_up.shape[0] // shard
    return pl.pallas_call(
        pack_kernel,
        out_shape=jax.ShapeDtypeStruct((chips, rows, shard), F32),
        scratch_shapes=[pltpu.VMEM((rows, shard), F32)],
        cost_estimate=pl.CostEstimate(flops=10**6, bytes_accessed=10**4, transcendentals=0),
        name="pack",
    )(*matrices, *(v.reshape(1, -1) for v in vectors), bias_up.reshape(1, -1))


def fill_powers(zr, zi, pr, pi, steps):
    ar, ai = jnp.ones_like(zr), jnp.zeros_like(zi)
    pr[pl.ds(0, MODES), :] = ar
    pi[pl.ds(0, MODES), :] = ai
    for j in range(1, steps + 1):
        ar, ai = cmul(ar, ai, zr, zi)
        pr[pl.ds(j * MODES, MODES), :] = ar
        pi[pl.ds(j * MODES, MODES), :] = ai
    return ar, ai


def over_chunk(ar, ai):
    n = 1
    while n < SEGS:
        ar, ai = cmul(ar, ai, ar, ai)
        n *= 2
    return ar, ai


def fill_kern(wr, wi, pr, pi, kern, steps):
    for j in range(steps):
        v = wr * pr[pl.ds(j * MODES, MODES), :] - wi * pi[pl.ds(j * MODES, MODES), :]
        kern[pl.ds(j, 1), :] = 2.0 * jnp.sum(v, axis=0, keepdims=True)


def row(ref, i):
    return jnp.broadcast_to(ref[pl.ds(i, 1), :], (SEGS, LANES))


def group(ref, steps, c, t):
    return ref[pl.ds((c * steps + t) * SEGS, SEGS), :]


def put(ref, steps, c, t, value):
    ref[pl.ds((c * steps + t) * SEGS, SEGS), :] = value


def put_low(ref, steps, c, t, pair):
    ref[pl.ds((c * steps + t) * SEGS, 2 * SEGS), :] = jnp.concatenate(pair).astype(BF16)


def sublanes():
    return lax.broadcasted_iota(jnp.int32, (SEGS, LANES), 0)


def seg_mask(keep0, keep4):
    ids = sublanes()
    m = jnp.where(ids == 0, keep0, 1.0)
    return jnp.where(ids == SEGS // 2, keep4, m)


def seg_rows(c, k):
    return pl.ds(c * MODES * SEGS + k, MODES, stride=SEGS)


def mode_rows(c, m):
    return pl.ds(pl.multiple_of(c * MODES * SEGS + m * SEGS, SEGS), SEGS)


def weigh(pr, pi, steps, order, power, last, data, outs):
    outs_r, outs_i, runs_r, runs_i = outs
    half = steps // 2
    for part in range(2):
        ts = order[part * half : (part + 1) * half]
        values = [[data(c, t) for t in ts] for c in range(2)]

        def per_mode(m, carry):
            acc = []
            for c in range(2):
                if part == 0:
                    acc.append([jnp.zeros((SEGS, LANES), F32)] * 4)
                else:
                    acc.append([r[mode_rows(c, m), :] for r in (outs_r, outs_i, runs_r, runs_i)])
            for i, t in enumerate(ts):
                a, b = row(pr, power(t) * MODES + m), row(pi, power(t) * MODES + m)
                for c in range(2):
                    sr, si, tr, ti = acc[c]
                    sr, si = sr + a * values[c][i], si + b * values[c][i]
                    if last or t != order[-1]:
                        tr, ti = tr + sr, ti + si
                    acc[c] = [sr, si, tr, ti]
            for c in range(2):
                for r, v in zip((outs_r, outs_i, runs_r, runs_i), acc[c]):
                    r[mode_rows(c, m), :] = v
            return carry

        lax.fori_loop(0, MODES, per_mode, 0, unroll=8)


def unfold(pr, pi, steps, power, states, base, done):
    half = steps // 2
    for part in range(2):
        ts = range(part * half, (part + 1) * half)
        init = tuple(base(c, t) for c in range(2) for t in ts)

        def per_mode(m, acc):
            acc = list(acc)
            u = [states[0][mode_rows(c, m), :] for c in range(2)]
            v = [states[1][mode_rows(c, m), :] for c in range(2)]
            for i, t in enumerate(ts):
                a, b = row(pr, power(t) * MODES + m), row(pi, power(t) * MODES + m)
                for c in range(2):
                    at = c * half + i
                    acc[at] = acc[at] + (a * u[c] - b * v[c])
            return tuple(acc)

        acc = lax.fori_loop(0, MODES, per_mode, init, unroll=8)
        for c in range(2):
            for i in range(0, half, 2):
                done(c, ts[i], acc[c * half + i : c * half + i + 2])


def lags_apply(kern, steps, base, source, out, adjoint):
    n = steps // BLOCK
    for tb in range(n):
        ts = range(tb * BLOCK, (tb + 1) * BLOCK)
        ys = {(c, t): base(c, t) for c in range(2) for t in ts}
        for sb in range(tb, n) if adjoint else range(tb + 1):
            ss = range(sb * BLOCK, (sb + 1) * BLOCK)
            xs = {(c, s): source(c, s) for c in range(2) for s in ss}
            for lag in range(steps):
                pairs = [(t, s) for t in ts for s in ss if (s - t if adjoint else t - s) == lag]
                if pairs:
                    k = row(kern, lag)
                    for t, s in pairs:
                        for c in range(2):
                            ys[c, t] = ys[c, t] + k * xs[c, s]
        for (c, t), y in ys.items():
            put(out, steps, c, t, y)


def lag_sums(steps, left, right):
    n = steps // BLOCK
    sums = []
    for jb in range(n):
        acc = [jnp.zeros((SEGS, LANES), F32)] * BLOCK
        for c in range(2):
            for tb in range(jb, n):
                ts = range(tb * BLOCK, (tb + 1) * BLOCK)
                base = (tb - jb) * BLOCK
                xs = {s: right(c, s) for s in range(max(base - BLOCK + 1, 0), base + BLOCK)}
                for t in ts:
                    g = left(c, t)
                    for j in range(BLOCK):
                        s = t - jb * BLOCK - j
                        if s >= 0:
                            acc[j] = acc[j] + g * xs[s]
        sums.extend(jnp.sum(a, axis=0, keepdims=True) for a in acc)
    return sums


def earlier_keys(key, steps, keeps):
    ids = sublanes()
    out = []
    rolled = None
    for c in range(2):
        mask = seg_mask(keeps[c, 0], keeps[c, 1])
        new, windows = [], []
        for back in (1, 2, 3):
            v = pltpu.roll(group(key, steps, c, steps - back), 1, 0)
            new.append(v)
            before = row(key, 2 * steps * SEGS + HALO - back) if c == 0 else rolled[back - 1]
            windows.append(jnp.where(ids == 0, before, v) * mask)
        rolled = new
        out.append(windows)
    return out


def chunk_of(own, sib, core, c, at):
    return jnp.where(core == c, own[at, :].astype(F32), sib[at, :].astype(F32))


def join(parts, out):
    at = 0
    for p in parts:
        n = p.shape[0]
        out[pl.ds(at, n), :] = p[...]
        at += n


def part_to(outs, value):
    at = 0
    for o in outs:
        n = o.shape[0]
        o[...] = value[at : at + n].astype(BF16)
        at += n


def before_kernel(steps, n_parts, core, keeps, own, sib, gain, shift, order, *refs):
    mixed_kv, params = refs[:n_parts], refs[n_parts]
    normed, wkv, tables, kern, key, value, prod, shifted, er, ei, dr, di, ends, chip, pr, pi, joined = refs[n_parts + 1 :]
    lane = pl.program_id(0)
    rows = steps * SEGS
    channels = wkv.shape[0] // 2

    @pl.when(lane == 0)
    def _():
        me = core[0]
        join(mixed_kv, joined)
        wkv[...] = dot_nn(order[...], joined[...]).astype(BF16)

        def rows_of(x):
            xhat, _ = normalize(x)
            return (xhat * gain[...] + shift[...]).astype(BF16)

        for c in range(2):
            for r in range(0, rows, LN_TILE):
                normed[pl.ds(c * rows + r, LN_TILE), :] = rows_of(chunk_of(own, sib, me, c, pl.ds(r, LN_TILE)))
        normed[pl.ds(2 * rows, HALO), :] = rows_of(chunk_of(own, sib, me, 1, pl.ds(rows, HALO)))

    decay, turn, wr, wi = ssm_tables(*table_inputs(params))
    mag = jnp.exp(decay)
    zr, zi = mag * jnp.cos(turn), mag * jnp.sin(turn)
    for i, v in enumerate((zr, zi, wr, wi)):
        tables[pl.ds(i * MODES, MODES), :] = v
    ar, ai = fill_powers(zr, zi, pr, pi, steps)
    fill_kern(wr, wi, pr, pi, kern, steps)
    at = pl.ds(pl.multiple_of(lane * LANES, LANES), LANES)
    also = pl.ds(pl.multiple_of(channels + lane * LANES, LANES), LANES)
    key[...] = dot_nt(normed[...], wkv[at, :]) + params[pl.ds(BIAS_ROW + 1, 1), :]
    value[...] = dot_nt(normed[pl.ds(0, 2 * rows), :], wkv[also, :]) + params[pl.ds(BIAS_ROW + 2, 1), :]
    tap = [row(params, TAP_ROW + j) for j in range(TAPS)]
    windows = earlier_keys(key, steps, keeps)
    for c in range(2):
        window = windows[c]
        for t in range(steps):
            cur = group(key, steps, c, t)
            s = tap[0] * cur + tap[1] * window[0] + tap[2] * window[1] + tap[3] * window[2]
            window = [cur] + window[:2]
            put(shifted, steps, c, t, s)
            put(prod, steps, c, t, s * group(value, steps, c, t))
    weigh(
        pr, pi, steps, list(range(steps)), lambda t: steps - 1 - t, False,
        lambda c, t: group(prod, steps, c, t), (er, ei, dr, di),
    )
    states = []
    for c in range(2):
        k4 = keeps[c, 1]
        sr = si = jnp.zeros((MODES, LANES), F32)
        for k in range(SEGS):
            if k == SEGS // 2:
                sr, si = sr * k4, si * k4
            cr, ci = cmul(sr, si, ar, ai)
            sr = cr + er[seg_rows(c, k), :]
            si = ci + ei[seg_rows(c, k), :]
        states.append((sr, si))
    ends[pl.ds(0, MODES), :], ends[pl.ds(MODES, MODES), :] = states[0]
    br, bi = over_chunk(ar, ai)
    cr, ci = cmul(*states[0], br, bi)
    keep = keeps[1, 0] * keeps[1, 1]
    chip[pl.ds(0, MODES), :] = (cr * keep + states[1][0]).astype(BF16)
    chip[pl.ds(MODES, MODES), :] = (ci * keep + states[1][1]).astype(BF16)


def incoming(ref_list, masks, which, ar, ai):
    br, bi = cmul(ar, ai, ar, ai)
    read = lambda r: (r[pl.ds(0, MODES), :].astype(F32), r[pl.ds(MODES, MODES), :].astype(F32))
    sr, si = read(ref_list[-1])
    for by in range(len(ref_list) - 1, 0, -1):
        m = masks[which, by]
        cr, ci = cmul(sr, si, br * m, bi * m)
        rr, ri = read(ref_list[by - 1])
        sr, si = cr + rr, ci + ri
    return sr, si


def near_kernel(steps, n_parts, normed, prod, *refs):
    mixed_qo = refs[:n_parts]
    order, params, kern, wqo, query, near, joined = refs[n_parts:]
    lane = pl.program_id(0)
    rows = steps * SEGS

    @pl.when(lane == 0)
    def _():
        join(mixed_qo, joined)
        wqo[...] = dot_nn(order[...], joined[...]).astype(BF16)

    at = pl.ds(pl.multiple_of(lane * LANES, LANES), LANES)
    query[...] = dot_nt(normed[pl.ds(0, 2 * rows), :], wqo[at, :]) + params[pl.ds(BIAS_ROW, 1), :]
    source = lambda c, t: group(prod, steps, c, t)
    sk = row(params, SKIP_ROW)
    lags_apply(kern, steps, lambda c, t: sk * source(c, t), source, near, False)


def conv_kernel(steps, n_recv, keeps, masks, near, query, er, ei, ends, *refs):
    recv = refs[:n_recv]
    wo, tables, conv, core_low, state_r, state_i, mixed_low, pr, pi, twice_r, twice_i, mixed = refs[n_recv:]
    lane = pl.program_id(0)
    zr, zi, wr, wi = read_tables(tables)
    ar, ai = fill_powers(zr, zi, pr, pi, steps)
    w2r, w2i = 2.0 * wr, 2.0 * wi
    br, bi = over_chunk(ar, ai)
    sr, si = incoming(recv, masks, 0, br, bi)
    for c in range(2):
        if c == 1:
            sr, si = cmul(first_r, first_i, br * keeps[0, 1], bi * keeps[0, 1])
            sr, si = sr + ends[pl.ds(0, MODES), :], si + ends[pl.ds(MODES, MODES), :]
        sr, si = sr * keeps[c, 0], si * keeps[c, 0]
        first_r, first_i = sr, si
        for k in range(SEGS):
            if k == SEGS // 2:
                sr, si = sr * keeps[c, 1], si * keeps[c, 1]
            state_r[seg_rows(c, k), :] = sr
            state_i[seg_rows(c, k), :] = si
            twice_r[seg_rows(c, k), :], twice_i[seg_rows(c, k), :] = cmul(w2r, w2i, sr, si)
            if k < SEGS - 1:
                cr, ci = cmul(sr, si, ar, ai)
                sr = cr + er[seg_rows(c, k), :]
                si = ci + ei[seg_rows(c, k), :]

    def done(c, t, values):
        low = []
        for i, v in zip((t, t + 1), values):
            put(conv, steps, c, i, v)
            low.append(v * group(query, steps, c, i))
        put_low(core_low, steps, c, t, low)

    unfold(pr, pi, steps, lambda t: t + 1, (twice_r, twice_i), lambda c, t: group(near, steps, c, t), done)
    out = dot_nn(core_low[...], wo[...])

    @pl.when(lane == 0)
    def _():
        mixed[...] = out

    @pl.when(jnp.logical_and(lane > 0, lane < pl.num_programs(0) - 1))
    def _():
        mixed[...] += out

    @pl.when(lane == pl.num_programs(0) - 1)
    def _():
        mixed_low[...] = (mixed[...] + out).astype(BF16)


def after_kernel(
    steps, core, keeps, residual, grad_own, grad_sib, cot_own, cot_sib, gain, order, wo, normed, query, conv, core_low,
    tables, grad_residual, g, grad_query, qr, qi, rr, ri, ends, chip, sums, *refs,
):
    grad_qo, (pr, pi, low, grad_core, grad_w) = refs[:-5], refs[-5:]
    lane = pl.program_id(0)
    rows = steps * SEGS
    channels = grad_w.shape[0] // 2

    @pl.when(lane == 0)
    def _():
        me = core[0]
        total = [jnp.zeros((1, low.shape[1]), F32)] * 4
        for c in range(2):
            for r in range(0, rows, LN_TILE):
                at = pl.ds(c * rows + r, LN_TILE)
                xhat, scale = normalize(residual[at, :])
                grad = grad_own[at, :].astype(F32) + grad_sib[at, :].astype(F32)
                cot = chunk_of(cot_own, cot_sib, me, c, pl.ds(r, LN_TILE))
                out = cot + normalize_back(grad, gain[...], xhat, scale)
                grad_residual[at, :] = out
                low[at, :] = out.astype(BF16)
                for i, v in enumerate((out, grad * xhat, grad, cot)):
                    total[i] = total[i] + jnp.sum(v, axis=0, keepdims=True)
        sums[...] = jnp.concatenate(total, axis=0)

    zr, zi, wr, wi = read_tables(tables)
    ar, ai = fill_powers(zr, zi, pr, pi, steps)
    grad_core[...] = dot_nt(low[...], wo[...])
    for c in range(2):
        for t in range(0, steps, 2):
            pair = []
            for i in (t, t + 1):
                d = group(grad_core, steps, c, i)
                put(g, steps, c, i, d * group(query, steps, c, i))
                pair.append(d * group(conv, steps, c, i))
            put_low(grad_query, steps, c, t, pair)
    at = pl.ds(pl.multiple_of(lane * LANES, LANES), LANES)
    also = pl.ds(pl.multiple_of(channels + lane * LANES, LANES), LANES)
    grad_w[at, :] = dot_tn(grad_query[...], normed[pl.ds(0, 2 * rows), :]).astype(BF16)
    grad_w[also, :] = dot_tn(core_low[...], low[...]).astype(BF16)

    @pl.when(lane == pl.num_programs(0) - 1)
    def _():
        part_to(grad_qo, dot_tn(order[...], grad_w[...]))

    weigh(
        pr, pi, steps, list(reversed(range(steps))), lambda t: t + 1, True,
        lambda c, t: group(g, steps, c, t), (qr, qi, rr, ri),
    )
    w2r, w2i = 2.0 * wr, 2.0 * wi
    lr = li = jnp.zeros((MODES, LANES), F32)
    for c in (1, 0):
        for k in reversed(range(SEGS)):
            cr, ci = cmul(lr, li, ar, ai)
            ur, ui = cmul(w2r, w2i, qr[seg_rows(c, k), :], qi[seg_rows(c, k), :])
            lr, li = ur + cr, ui + ci
            if k == SEGS // 2:
                lr, li = lr * keeps[c, 1], li * keeps[c, 1]
        lr, li = lr * keeps[c, 0], li * keeps[c, 0]
        if c == 1:
            ends[pl.ds(0, MODES), :] = lr
            ends[pl.ds(MODES, MODES), :] = li
    chip[pl.ds(0, MODES), :] = lr.astype(BF16)
    chip[pl.ds(MODES, MODES), :] = li.astype(BF16)


def near_back_kernel(steps, g, prod, params, kern, near, lags):
    source = lambda c, t: group(g, steps, c, t)
    other = lambda c, t: group(prod, steps, c, t)
    sk = row(params, SKIP_ROW)
    for j, lag in enumerate(lag_sums(steps, source, other)):
        lags[pl.ds(j, 1), :] = lag
    dsk = jnp.zeros((SEGS, LANES), F32)
    for c in range(2):
        for t in range(steps):
            dsk = dsk + source(c, t) * other(c, t)
    lags[pl.ds(steps, 1), :] = jnp.sum(dsk, axis=0, keepdims=True)
    lags_apply(kern, steps, lambda c, t: sk * source(c, t), source, near, True)


def grads_kernel(steps, n_recv, base, last, core, keeps, masks, near, lags, qr, qi, rr, ri, state_r, state_i, dr, di, ends, *refs):
    recv = refs[:n_recv]
    params, tables, key, value, shifted, grad_query, normed, wk, wv, wq = refs[n_recv : n_recv + 10]
    refs = refs[n_recv + 10 :]
    if last:
        order, before_keep, before_send, before_w, *refs = refs
        grad_keep, grad_send, grad_params, *grad_kv = refs[:-8]
        pr, pi, mur, mui, back, cat, cat_w, grad_w = refs[-8:]
    else:
        before_keep = before_send = None
        grad_keep, grad_send, grad_params, grad_w, pr, pi, mur, mui, back, cat, cat_w = refs
    lane = pl.program_id(0)
    rows = steps * SEGS
    channels = grad_w.shape[0] // 2
    ids = sublanes()
    zr, zi, wr, wi = read_tables(tables)
    ar, ai = fill_powers(zr, zi, pr, pi, steps)
    w2r, w2i = 2.0 * wr, 2.0 * wi
    br, bi = over_chunk(ar, ai)
    mr, mi = incoming(recv, masks, 1, br, bi)
    zero = jnp.zeros((MODES, LANES), F32)
    awr = awi = azr = azi = acr = aci = zero
    for c in (1, 0):
        if c == 0:
            keep = keeps[1, 0] * keeps[1, 1]
            mr, mi = cmul(last_r, last_i, br * keep, bi * keep)
            mr, mi = mr + ends[pl.ds(0, MODES), :], mi + ends[pl.ds(MODES, MODES), :]
        last_r, last_i = mr, mi
        for k in reversed(range(SEGS)):
            at = seg_rows(c, k)
            mur[at, :] = mr
            mui[at, :] = mi
            s_r, s_i = state_r[at, :], state_i[at, :]
            q_r, q_i = qr[at, :], qi[at, :]
            u = cmul(s_r, s_i, q_r, q_i)
            awr, awi = awr + u[0], awi + u[1]
            u = cmul(s_r, s_i, rr[at, :], ri[at, :])
            azr, azi = azr + u[0], azi + u[1]
            u = cmul(mr, mi, dr[at, :], di[at, :])
            acr, aci = acr + u[0], aci + u[1]
            u = cmul(mr, mi, s_r, s_i)
            u = cmul(u[0], u[1], ar, ai)
            acr, aci = acr + float(steps) * u[0], aci + float(steps) * u[1]
            if k > 0:
                ur, ui = cmul(w2r, w2i, q_r, q_i)
                cr, ci = cmul(mr, mi, ar, ai)
                mr, mi = ur + cr, ui + ci
                if k == SEGS // 2:
                    mr, mi = mr * keeps[c, 1], mi * keeps[c, 1]
    for j in range(steps):
        lag = lags[pl.ds(j, 1), :]
        u, v = pr[pl.ds(j * MODES, MODES), :] * lag, pi[pl.ds(j * MODES, MODES), :] * lag
        awr, awi = awr + u, awi + v
        azr, azi = azr + float(j) * u, azi + float(j) * v
    u = cmul(w2r, w2i, azr, azi)
    _, tables_back = jax.vjp(ssm_tables, *table_inputs(params))
    dstep, *dmodes = tables_back((u[0] + acr, -(u[1] + aci), 2.0 * awr, -2.0 * awi))
    for i, v in enumerate(dmodes):
        grad_params[pl.ds(i * MODES, MODES), :] = v
    grad_params[pl.ds(STEP_ROW, 1), :] = dstep
    grad_params[pl.ds(SKIP_ROW, 1), :] = lags[pl.ds(steps, 1), :]

    def done(c, t, values):
        low = []
        for i, v in zip((t, t + 1), values):
            low.append(v * group(shifted, steps, c, i))
            put(back, steps, c, i, v * group(value, steps, c, i))
        cat[pl.ds((c * steps + t) * SEGS, 2 * SEGS), pl.ds(LANES, LANES)] = jnp.concatenate(low).astype(BF16)

    unfold(pr, pi, steps, lambda t: steps - 1 - t, (mur, mui), lambda c, t: group(near, steps, c, t), done)
    tap = [row(params, TAP_ROW + j) for j in range(TAPS)]
    windows = earlier_keys(key, steps, keeps)
    acc = [jnp.zeros((SEGS, LANES), F32)] * TAPS
    for c in range(2):
        window = windows[c]
        for t in range(steps):
            cur = group(key, steps, c, t)
            v = group(back, steps, c, t)
            for j, w in enumerate([cur] + window):
                acc[j] = acc[j] + v * w
            window = [cur] + window[:2]
    for j, a in enumerate(acc):
        grad_params[pl.ds(TAP_ROW + j, 1), :] = jnp.sum(a, axis=0, keepdims=True)
    following = [jnp.zeros((SEGS, LANES), F32)] * (TAPS - 1)
    for c in (1, 0):
        mask = seg_mask(keeps[c, 0], keeps[c, 1])
        begin = [group(back, steps, c, t) * mask for t in range(TAPS - 1)]
        later = [pltpu.roll(jnp.where(ids == 0, f, v), SEGS - 1, 0) for f, v in zip(following, begin)]
        following = begin
        ext = lambda t: group(back, steps, c, t) if t < steps else later[t - steps]
        for t in range(0, steps, 2):
            low = [
                tap[0] * ext(i) + tap[1] * ext(i + 1) + tap[2] * ext(i + 2) + tap[3] * ext(i + 3) for i in (t, t + 1)
            ]
            cat[pl.ds((c * steps + t) * SEGS, 2 * SEGS), pl.ds(0, LANES)] = jnp.concatenate(low).astype(BF16)
    edge = [jnp.zeros((HALO - TAPS + 1, LANES), F32)]
    for b in (3, 2, 1):
        v = jnp.zeros((1, LANES), F32)
        for j in range(b, TAPS):
            v = v + params[pl.ds(TAP_ROW + j, 1), :] * following[j - b][0:1, :]
        edge.append(v)
    halo_at = pl.ds(2 * rows, HALO)
    cat[halo_at, pl.ds(0, LANES)] = jnp.concatenate(edge, axis=0).astype(BF16)
    cat[halo_at, pl.ds(LANES, 2 * LANES)] = jnp.zeros((HALO, 2 * LANES), BF16)
    cat[pl.ds(0, 2 * rows), pl.ds(2 * LANES, LANES)] = grad_query[...]
    for i, w in enumerate((wk, wv, wq)):
        cat_w[pl.ds(i * LANES, LANES), :] = w[...]
    both = dot_tn(cat[:, pl.ds(0, 2 * LANES)], normed[...])
    if last:

        @pl.when(lane == 0)
        def _():
            grad_w[...] = before_w[...]

    at = (base + lane) * LANES
    grad_w[pl.ds(pl.multiple_of(at, LANES), LANES), :] = both[:LANES].astype(BF16)
    grad_w[pl.ds(pl.multiple_of(channels + at, LANES), LANES), :] = both[LANES:].astype(BF16)
    if last:

        @pl.when(lane == pl.num_programs(0) - 1)
        def _():
            part_to(grad_kv, dot_tn(order[...], grad_w[...]))

    for i, part in enumerate((2, 0, 1)):
        grad_params[pl.ds(BIAS_ROW + i, 1), :] = jnp.sum(cat[:, pl.ds(part * LANES, LANES)].astype(F32), axis=0, keepdims=True)
    me = core[0]
    for c in range(2):
        out = dot_nn(cat[pl.ds(c * rows, rows), :], cat_w[...])

        @pl.when(me == c)
        def _():
            add_to(grad_keep, pl.ds(0, rows), out, lane, before_keep)

        @pl.when(me != c)
        def _():
            add_to(grad_send, pl.ds(0, rows), out, lane, before_send)

    add_to(grad_send, pl.ds(rows, HALO), dot_nn(cat[halo_at, :], cat_w[...]), lane, before_send)


def add_to(ref, at, value, step, before):
    @pl.when(step == 0)
    def _():
        ref[at, :] = value if before is None else before[at, :] + value

    @pl.when(step > 0)
    def _():
        ref[at, :] += value


class Mixer:
    def __init__(self, rows, channels, width, groups):
        self.rows, self.channels, self.width, self.groups = rows, channels, width, groups
        self.steps = rows // SEGS

    def lanes(self, rows):
        return pl.BlockSpec((rows, LANES), lambda l: (0, l))

    def whole(self, *shape):
        return pl.BlockSpec(shape, lambda l: (0,) * len(shape))

    def shape(self, rows, kind=F32):
        return jax.ShapeDtypeStruct((rows, self.channels), kind)

    def wide(self, rows, kind):
        return jax.ShapeDtypeStruct((rows, self.width), kind)

    def call(self, name, kernel, in_specs, outs, scratch, work, powers=True, count=None):
        table = pltpu.VMEM(((self.steps + 1) * MODES, LANES), F32)
        return pl.pallas_call(
            kernel,
            grid=(count or self.channels // LANES,),
            in_specs=in_specs,
            out_specs=[s for s, _ in outs],
            out_shape=[s for _, s in outs],
            scratch_shapes=[table, table] * powers + scratch,
            compiler_params=pltpu.CompilerParams(vmem_limit_bytes=VMEM_LIMIT),
            cost_estimate=pl.CostEstimate(flops=work // 10000, bytes_accessed=work // 4000000, transcendentals=0),
            name=name,
        )

    def units(self, part=0):
        return pl.BlockSpec((LANES, self.width), lambda l: (l + part * self.channels // LANES, 0))

    def pair(self):
        n = 2 * self.channels
        return self.whole(n, self.width), self.wide(n, BF16)

    def parts(self):
        n = 2 * self.channels // self.groups
        return [(self.whole(n, self.width), self.wide(n, BF16))] * self.groups

    def order(self):
        return self.whole(2 * self.channels, 2 * self.channels)

    def before(self, core, keeps, own, sib, gain, shift, order, mixed_kv, params):
        n, ms, w = 2 * self.rows, 2 * MODES * SEGS, self.width
        line, states, ends = self.whole(1, w), (self.lanes(ms), self.shape(ms)), self.lanes(2 * MODES)
        return self.call(
            "ssm_before",
            functools.partial(before_kernel, self.steps, len(mixed_kv)),
            [SMEM, SMEM, self.whole(*own.shape), self.whole(*own.shape), line, line, self.order()]
            + [self.whole(*p.shape) for p in mixed_kv] + [self.lanes(PARAM_ROWS)],
            [(self.whole(n + HALO, w), self.wide(n + HALO, BF16)), self.pair(), (self.lanes(4 * MODES), self.shape(4 * MODES))]
            + [(self.lanes(self.steps), self.shape(self.steps))]
            + [(self.lanes(n + HALO), self.shape(n + HALO))] + [(self.lanes(n), self.shape(n))] * 3 + [states] * 4
            + [(ends, self.shape(2 * MODES)), (ends, self.shape(2 * MODES, BF16))],
            [pltpu.VMEM((2 * self.channels, w), BF16)],
            10**10,
        )(core, keeps, own, sib, gain, shift, order, *mixed_kv, params)

    def near(self, normed, prod, mixed_qo, order, params, kern):
        n, w = 2 * self.rows, self.width
        big = self.lanes(n)
        return self.call(
            "ssm_near",
            functools.partial(near_kernel, self.steps, len(mixed_qo)),
            [self.whole(*normed.shape), big] + [self.whole(*p.shape) for p in mixed_qo]
            + [self.order(), self.lanes(PARAM_ROWS), self.lanes(self.steps)],
            [self.pair(), (big, self.shape(n)), (big, self.shape(n))],
            [pltpu.VMEM((2 * self.channels, w), BF16)],
            6 * 10**9,
            False,
        )(normed, prod, *mixed_qo, order, params, kern)

    def conv(self, keeps, masks, near, query, er, ei, ends, recv, wqo, tables):
        n, ms, w = 2 * self.rows, 2 * MODES * SEGS, self.width
        big, states, last = self.lanes(n), self.lanes(ms), self.lanes(2 * MODES)
        return self.call(
            "ssm_conv",
            functools.partial(conv_kernel, self.steps, len(recv)),
            [SMEM, SMEM, big, big, states, states] + [last] * (1 + len(recv)) + [self.units(1), self.lanes(4 * MODES)],
            [(big, self.shape(n)), (big, self.shape(n, BF16))] + [(states, self.shape(ms))] * 2
            + [(self.whole(n, w), self.wide(n, BF16))],
            [pltpu.VMEM((ms, LANES), F32)] * 2 + [pltpu.VMEM((n, w), F32)],
            10**10,
        )(keeps, masks, near, query, er, ei, ends, *recv, wqo, tables)

    def after(
        self, core, keeps, residual, grad_own, grad_sib, cot_own, cot_sib, gain, order, wqo, normed, query, conv, core_low,
        tables,
    ):
        n, ms, w = 2 * self.rows, 2 * MODES * SEGS, self.width
        big, states, last = self.lanes(n), self.lanes(ms), self.lanes(2 * MODES)
        full, half = self.whole(n, w), self.whole(n // 2, w)
        return self.call(
            "ssm_after",
            functools.partial(after_kernel, self.steps),
            [SMEM, SMEM, full, full, full, half, half, self.whole(1, w), self.order(), self.units(1), self.whole(*normed.shape)]
            + [big] * 3 + [self.lanes(4 * MODES)],
            [(full, self.wide(n, F32)), (big, self.shape(n)), (big, self.shape(n, BF16))]
            + [(states, self.shape(ms))] * 4 + [(last, self.shape(2 * MODES)), (last, self.shape(2 * MODES, BF16))]
            + [(self.whole(4, w), self.wide(4, F32))] + self.parts(),
            [pltpu.VMEM((n, w), BF16), pltpu.VMEM((n, LANES), F32), pltpu.VMEM((2 * self.channels, w), BF16)],
            10**10,
        )(
            core, keeps, residual, grad_own, grad_sib, cot_own, cot_sib, gain, order, wqo, normed, query, conv, core_low,
            tables,
        )

    def near_back(self, g, prod, params, kern):
        big = self.lanes(2 * self.rows)
        tall = self.steps + SEGS
        return self.call(
            "ssm_near_back",
            functools.partial(near_back_kernel, self.steps),
            [big, big, self.lanes(PARAM_ROWS), self.lanes(self.steps)],
            [(big, self.shape(2 * self.rows)), (self.lanes(tall), self.shape(tall))],
            [],
            8 * 10**9,
            False,
        )(g, prod, params, kern)

    def grads(
        self, base, count, core, keeps, masks, near, lags, q, state, d, ends, recv, params, tables, key, value, shifted,
        grad_query, normed, wkv, wqo, order, before,
    ):
        n, ms, w = 2 * self.rows, 2 * MODES * SEGS, self.width
        lanes = lambda rows: pl.BlockSpec((rows, LANES), lambda l: (0, l + base))
        units = lambda part: pl.BlockSpec((LANES, w), lambda l: (l + base + part * self.channels // LANES, 0))
        big, states, ends_at = lanes(n), lanes(ms), lanes(2 * MODES)
        normed_at = [(self.whole(r, w), self.wide(r, F32)) for r in (self.rows, self.rows + HALO)]
        params_at = (lanes_from(PARAM_ROWS), jax.ShapeDtypeStruct((PARAM_ROWS, count * LANES), F32))
        last = before is not None
        return self.call(
            "ssm_grads_last" if last else "ssm_grads",
            functools.partial(grads_kernel, self.steps, len(recv), base, last),
            [SMEM, SMEM, SMEM, big, lanes(lags.shape[0])] + [states] * 8 + [ends_at] * (1 + len(recv))
            + [lanes(PARAM_ROWS), lanes(4 * MODES), lanes(n + HALO), big, big, big, self.whole(*normed.shape)]
            + [units(0), units(1), units(0)] + [self.order(), normed_at[0][0], normed_at[1][0], self.pair()[0]] * last,
            [*normed_at, params_at] + (self.parts() if last else [self.pair()]),
            [pltpu.VMEM((ms, LANES), F32)] * 2
            + [pltpu.VMEM((n, LANES), F32), pltpu.VMEM((n + HALO, 3 * LANES), BF16), pltpu.VMEM((3 * LANES, w), BF16)]
            + [pltpu.VMEM((2 * self.channels, w), BF16)] * last,
            10**9,
            True,
            count,
        )(
            core, keeps, masks, near, lags, *q, *state, *d, ends, *recv, params, tables, key, value, shifted, grad_query,
            normed, wkv, wkv, wqo, *([order, *before] if last else []),
        )


def lanes_from(rows):
    return pl.BlockSpec((rows, LANES), lambda l: (0, l))


def tail_kernel(steps, shard, core, keep, send, own, sib, sums, params_most, params_rest, bias, tail, rows_of):
    rows = steps * SEGS
    me, me_chip = core[0], core[1]
    total = [jnp.zeros((1, keep.shape[1]), F32)] * 2

    def more(total, grad, x):
        xhat, _ = normalize(x)
        return [t + jnp.sum(v, axis=0, keepdims=True) for t, v in zip(total, (grad * xhat, grad))]

    for r in range(0, rows, LN_TILE):
        at = pl.ds(r, LN_TILE)
        total = more(total, keep[at, :], own[at, :].astype(F32))
        total = more(total, send[at, :], sib[at, :].astype(F32))
    edge = pl.ds(rows, HALO)
    total = more(total, send[edge, :], chunk_of(own, sib, me, 1, edge))
    features = jnp.concatenate([*total, sums[...]], axis=0).astype(BF16)
    params = jnp.concatenate([params_most[...], params_rest[...]], axis=1).astype(BF16)
    chips, deep = tail.shape[0], tail.shape[1]
    rows_of[...] = jnp.zeros_like(rows_of)

    def columns(x, first):
        width = x.shape[1]
        i = lax.broadcasted_iota(jnp.int32, (width, LANES), 0)
        j = lax.broadcasted_iota(jnp.int32, (width, LANES), 1)
        pick = jnp.where(jnp.logical_and(i == first + j, j < shard), 1.0, 0.0).astype(BF16)
        return dot_nn(x, pick)

    for k in range(chips):
        z = lax.rem(me_chip - k + chips, chips)
        rows_of[pl.ds(0, PARAM_ROWS), :] = columns(params, z * shard)
        rows_of[pl.ds(PARAM_ROWS, 6), :] = columns(features, (2 * z + me) * shard)
        rows_of[pl.ds(PARAM_ROWS + 6, 2), :] = columns(features, (2 * z + 1 - me) * shard)[0:2]
        rows_of[pl.ds(PARAM_ROWS + 8, bias.shape[1]), :] = bias[k]
        for i in range(tail.shape[2] // LANES):
            tail[k, :, pl.ds(i * LANES, LANES)] = rows_of[pl.ds(i * deep, deep), :].astype(BF16)


def tail_of(core, keep, send, own, sib, sums, params_most, params_rest, bias, shard):
    width = keep.shape[1]
    across = width // LANES
    used = PARAM_ROWS + 8 + bias.shape[1]
    deep = -(-used // (across * 16)) * 16
    vmem = pl.BlockSpec(memory_space=pltpu.VMEM)
    return pl.pallas_call(
        functools.partial(tail_kernel, keep.shape[0] // SEGS, shard),
        in_specs=[SMEM] + [vmem] * 8,
        out_shape=jax.ShapeDtypeStruct((bias.shape[0], deep, width), BF16),
        scratch_shapes=[pltpu.VMEM((across * deep, LANES), F32)],
        compiler_params=pltpu.CompilerParams(vmem_limit_bytes=VMEM_LIMIT),
        cost_estimate=pl.CostEstimate(flops=10**6, bytes_accessed=10**4, transcendentals=0),
        name="tail_of",
    )(core, keep, send, own, sib, sums, params_most, params_rest, bias)


def finish_kernel(steps, core, keep, from_sib, edge, own, grad_residual, gain, out, total):
    rows = steps * SEGS
    total[...] = keep[...] + from_sib[pl.ds(0, rows), :]
    for b in range(1, TAPS):
        total[pl.ds((steps - b) * SEGS + SEGS - 1, 1), :] += edge[pl.ds(HALO - b, 1), :]
    first = pl.multiple_of(core[0] * rows, rows)
    for r in range(0, rows, LN_TILE):
        at = pl.ds(r, LN_TILE)
        xhat, scale = normalize(own[at, :].astype(F32))
        res = grad_residual[pl.ds(first + r, LN_TILE), :]
        out[at, :] = (res + normalize_back(total[at, :], gain[...], xhat, scale)).astype(BF16)


def finish(core, keep, from_sib, edge, own, grad_residual, gain):
    rows, width = keep.shape
    vmem = pl.BlockSpec(memory_space=pltpu.VMEM)
    return pl.pallas_call(
        functools.partial(finish_kernel, rows // SEGS),
        in_specs=[SMEM] + [vmem] * 6,
        out_shape=jax.ShapeDtypeStruct((rows, width), BF16),
        scratch_shapes=[pltpu.VMEM((rows, width), F32)],
        compiler_params=pltpu.CompilerParams(vmem_limit_bytes=VMEM_LIMIT),
        cost_estimate=pl.CostEstimate(flops=10**6, bytes_accessed=10**4, transcendentals=0),
        name="finish",
    )(core, keep, from_sib, edge, own, grad_residual, gain)


def feed_forward_kernel(reads, writes, first, n_arrays, n_outs, core, bias, lines, *refs):
    n_state = 6 if first else 5
    state, arrays, refs = refs[:n_state], refs[n_state : n_state + n_arrays], refs[n_state + n_arrays :]
    n_kept = 6 if first else 3
    kept, grad_bias, outs, refs = refs[:n_kept], refs[n_kept], refs[n_kept + 1 : n_kept + 1 + n_outs], refs[n_kept + 1 + n_outs :]
    held, refs = refs[:n_state], refs[n_state:]
    branch, grad_x, refs = refs[:2], refs[2], refs[3:]
    if first:
        own, sib, mixed_own, mixed_sib, c_own, c_sib = held
        residual, xs, cs, refs = *refs[:3], refs[3:]
    else:
        *branch_in, grad_in, xs, cs = held
    acts, backs, weights, grads, state_sems, read_sems, kept_sems, write_sems = refs
    me = core[0]
    half = xs.shape[0] // 2
    n_sets, units = bias.shape
    tiles = 2 * half // TILE

    def place(buffer, s, which, row, n):
        return buffer.at[which, pl.ds(s * units + row, n), :]

    def taken(i):
        return pltpu.make_async_copy(state[i], held[i], state_sems.at[i])

    def incoming(s, i):
        array, at, which, row, n = reads[s][i]
        return pltpu.make_async_copy(
            arrays[array].at[pl.ds(at, n), :], place(weights, s, which, row, n), read_sems.at[s, i]
        )

    def outgoing(s, i):
        array, slot, at, which, row, n = writes[s][i]
        return pltpu.make_async_copy(
            place(grads, s, which, row, n), outs[array].at[slot, pl.ds(at, n), :], write_sems.at[s, i]
        )

    def leaving(what, r, to=0):
        at = pl.ds(r * TILE, TILE)
        if what == 0:
            rows = pl.ds(r * TILE % half, TILE)
            return pltpu.make_async_copy(branch[r * TILE // half].at[rows, :], kept[to].at[rows, :], kept_sems.at[0, r])
        if what == 1:
            return pltpu.make_async_copy(grad_x.at[at, :], kept[2].at[at, :], kept_sems.at[1, r])
        return pltpu.make_async_copy((residual, xs, cs)[r], kept[3 + r], kept_sems.at[2, r])

    for i in range(n_state):
        taken(i).start()
    for s in range(n_sets):
        for i in range(len(reads[s])):
            incoming(s, i).start()
    for i in range(n_state):
        taken(i).wait()
    for c in range(2 if first else 0):
        for r in range(0, half, LN_TILE):
            at, part = pl.ds(c * half + r, LN_TILE), pl.ds(r, LN_TILE)
            v = chunk_of(own, sib, me, c, part) + mixed_own[at, :].astype(F32) + mixed_sib[at, :].astype(F32)
            v = v + lines[pl.ds(0, 1), :]
            residual[at, :] = v
            xhat, _ = normalize(v)
            xs[at, :] = (xhat * lines[pl.ds(1, 1), :] + lines[pl.ds(2, 1), :]).astype(BF16)
            cs[at, :] = chunk_of(c_own, c_sib, me, c, part).astype(BF16)
    for i in range(3 if first else 0):
        leaving(2, i).start()
    for s in range(n_sets):
        for i in range(len(reads[s])):
            incoming(s, i).wait()
    total = [jnp.zeros((1, units), F32)] * n_sets
    for r in range(0, 2 * half, TILE):
        at = pl.ds(r, TILE)
        c, place_of = r // half, pl.ds(r % half, TILE)
        for s in range(n_sets):
            mine = pl.ds(s * units, units)
            v = dot_nt(xs[at, :], weights[0, mine, :]) + bias[pl.ds(s, 1), :]
            square = v * v
            th = jnp.tanh(v * (0.79788456 + 0.79788456 * 0.044715 * square))
            half_up = 0.5 + 0.5 * th
            slope = half_up + v * (0.5 - 0.5 * th * th) * (0.79788456 + 0.79788456 * 3.0 * 0.044715 * square)
            back = dot_nt(cs[at, :], weights[1, mine, :]) * slope
            acts[at, mine] = (v * half_up).astype(BF16)
            low = back.astype(BF16)
            backs[at, mine] = low
            total[s] = total[s] + jnp.sum(low.astype(F32), axis=0, keepdims=True)
        out = dot_nn(acts[at, :], weights[1])
        grad = dot_nn(backs[at, :], weights[0])
        grad_x[at, :] = (grad if first else grad_in[at, :] + grad).astype(grad_x.dtype)
        leaving(1, r // TILE).start()
        if not first:
            out = out + jnp.where(me == c, branch_in[0][place_of, :], branch_in[1][place_of, :])
        branch[c][place_of, :] = out

        @pl.when(me == c)
        def _():
            leaving(0, r // TILE, 0).start()

        @pl.when(me != c)
        def _():
            leaving(0, r // TILE, 1).start()

    for s in range(n_sets):
        mine = pl.ds(s * units, units)
        grad_bias[pl.ds(s, 1), :] = total[s]
        for which, (left, right) in enumerate(((backs, xs), (acts, cs))):
            grads[which, mine, :] = dot_tn(left[:, mine], right[...]).astype(BF16)
            for i in range(len(writes[s])):
                if writes[s][i][3] == which:
                    outgoing(s, i).start()
    for r in range(tiles):
        leaving(0, r).wait()
        leaving(1, r).wait()
    for i in range(3 if first else 0):
        leaving(2, i).wait()
    for s in range(n_sets):
        for i in range(len(writes[s])):
            outgoing(s, i).wait()


def feed_forward(core, bias, lines, state, arrays, reads, out_shapes, writes, final):
    first = len(state) > 5
    width = state[2].shape[1]
    rows = state[4].shape[0] * 2 if first else state[2].shape[0]
    n_sets, units = bias.shape
    full, low = ((rows, width), F32), ((rows, width), BF16)
    part = ((rows // 2, width), F32)
    kept = [part, part, low if final else full] + [full, low, low] * first
    vmem, hbm = pl.BlockSpec(memory_space=pltpu.VMEM), pl.BlockSpec(memory_space=pl.ANY)
    shapes = [jax.ShapeDtypeStruct(*x) for x in kept]
    buffers = [pltpu.VMEM(x.shape, x.dtype) for x in state]
    buffers += [pltpu.VMEM(*x) for x in kept]
    out = pl.pallas_call(
        functools.partial(feed_forward_kernel, reads, writes, first, len(arrays), len(out_shapes)),
        in_specs=[SMEM, vmem, vmem] + [hbm] * (len(state) + len(arrays)),
        out_specs=[hbm] * len(kept) + [vmem] + [hbm] * len(out_shapes),
        out_shape=shapes + [jax.ShapeDtypeStruct(bias.shape, F32)]
        + [jax.ShapeDtypeStruct((n, rows_of, width), BF16) for n, rows_of in out_shapes],
        scratch_shapes=buffers
        + [pltpu.VMEM((rows, n_sets * units), BF16)] * 2 + [pltpu.VMEM((2, n_sets * units, width), BF16)] * 2
        + [
            pltpu.SemaphoreType.DMA((len(state),)),
            pltpu.SemaphoreType.DMA((n_sets, max(map(len, reads)))),
            pltpu.SemaphoreType.DMA((3, max(rows // TILE, 3))),
            pltpu.SemaphoreType.DMA((n_sets, max(map(len, writes)))),
        ],
        compiler_params=pltpu.CompilerParams(vmem_limit_bytes=VMEM_LIMIT),
        cost_estimate=pl.CostEstimate(flops=10**6, bytes_accessed=10**4, transcendentals=0),
        name="feed_forward" if first else "feed_forward_more",
    )(core, bias, lines, *state, *arrays)
    return out[: len(kept) + 1], out[len(kept) + 1 :]


def local(
    groups, chips,
    hidden_in, mix_gain, mix_shift, w_query, bias_query, w_key, bias_key, w_value, bias_value, shift_taps,
    log_step, log_decay, frequency, out_real, out_imag, skip_gain, w_out, bias_out, mlp_gain, mlp_shift,
    w_up, bias_up, w_down, bias_down, cotangent, seq_blocks,
):
    rows, width = hidden_in.shape
    shard, shard_units = w_query.shape[1], w_up.shape[1]
    chans, channels = 2 * chips, chips * shard
    cut, unit_cut = shard // groups, shard_units // groups
    steps = rows // SEGS
    me_group, me_chan = lax.axis_index("group"), lax.axis_index("chan")
    me_chip, me_core = me_chan // 2, me_chan % 2
    same_core = [[2 * z + k for z in range(chips)] for k in range(2)]
    square = groups == 4

    def swap_z(x):
        return lax.all_to_all(x, "chan", 0, 0, axis_index_groups=same_core, tiled=True)

    def group_swap(x, bits):
        return lax.ppermute(x, "group", [(i, i ^ bits) for i in range(groups)])

    def sibling(x):
        return lax.ppermute(x, "chan", [(i, i ^ 1) for i in range(chans)])

    def chip_shift(x, by):
        pairs = [(i, i + 2 * by) for i in range(chans) if 0 <= i + 2 * by < chans]
        return lax.ppermute(x, "chan", pairs)

    def chip_turn(x, by):
        return lax.ppermute(x, "chan", [(i, (i + 2 * by) % chans) for i in range(chans)])

    def gather_z(x):
        return jnp.concatenate([x] + [chip_turn(x, by) for by in range(1, chips)])

    def gather_group(x):
        return [x] + [group_swap(x, r) for r in range(1, groups)]

    def add(*xs):
        return sum(x.astype(F32) for x in xs).astype(BF16)

    def fold_z(parts):
        return add(parts[0], *(chip_turn(p, -by) for by, p in enumerate(parts) if by))

    def fold_group(parts):
        return add(parts[0], *(group_swap(p, r) for r, p in enumerate(parts) if r))

    def pieces(x, count):
        n = x.shape[0] // count
        return [x[i * n : (i + 1) * n] for i in range(count)]

    def by_index(parts):
        out = []
        for g in range(groups):
            x = parts[0]
            for r in range(1, groups):
                x = jnp.where(me_group == g ^ r, parts[r], x)
            out.append(x)
        return jnp.stack(out)

    def first_round(a):
        return (group_swap(a, 1), group_swap(a, 2)) if square else tuple(gather_group(a)[1:])

    def second_round(one):
        n = one[0].shape[0] // 2
        return (group_swap(one[1][:n], 1), group_swap(one[0][n:], 2)) if square else ()

    def fold_first(send_a, send_b):
        return [group_swap(x, 1) for x in send_a], [group_swap(x, 2) for x in send_b]

    def fold_second(one, ay, bx):
        return group_swap(add(ay, one[0][1]), 2), group_swap(add(bx, one[1][1]), 1)

    def fold_end(one, two, a0, b0):
        return add(a0, one[0][0], two[0]), add(b0, one[1][0], two[1])

    def fence(*xs):
        return lax.optimization_barrier(xs)

    def share(x):
        return lax.dynamic_index_in_dim(x.reshape(groups, -1, width), me_group, 0, keepdims=False)

    def to_steps(x):
        return x.reshape(SEGS, steps, width).transpose(1, 0, 2).reshape(rows, width)

    def to_rows(x):
        return x.reshape(steps, SEGS, width).transpose(1, 0, 2).reshape(rows, width)

    first = seq_blocks[0, 0]
    second = first + seq_blocks[0, 1]

    def keep(block):
        starts = (block == 0) | (block == first) | (block == second)
        return jnp.where(starts, 0.0, 1.0).astype(F32)

    blocks = 4 * me_chip + jnp.arange(4)
    keeps = keep(blocks).reshape(2, 2)

    def two_shares(a, b):
        return jnp.concatenate([share(a), share(b)])

    turns = (me_chip - jnp.arange(chips)) % chips
    flips = me_group ^ jnp.arange(groups)
    place = flips[None, None, :, None] * chips + turns[None, :, None, None]
    place = (place * 2 + jnp.arange(2)[:, None, None, None]) * cut + jnp.arange(cut)
    order = (place.reshape(-1, 1) == jnp.arange(2 * channels)).astype(BF16)
    z_turn = (turns[:, None] == jnp.arange(chips)).astype(F32)
    g_flip = (flips[:, None] == jnp.arange(groups)).astype(F32)
    exact = lax.Precision.HIGHEST

    core = jnp.stack([me_core, me_chip])
    line = lambda x: x.reshape(1, width)
    kv_z = gather_z(two_shares(w_key.T, w_value.T))
    edge = lax.ppermute(hidden_in[rows - HALO :], "chan", [(2 * z + 1, 2 * z + 3) for z in range(chips - 1)])
    own = jnp.concatenate([to_steps(hidden_in), edge])
    kv_z, own, w_query, w_out, w_up, w_down, cotangent, log_decay, frequency, out_real, out_imag = fence(
        kv_z, own, w_query, w_out, w_up, w_down, cotangent, log_decay, frequency, out_real, out_imag
    )

    mixed_kv = gather_group(kv_z)
    small = jnp.concatenate(
        [
            log_decay.T, frequency.T, out_real.T, out_imag.T, shift_taps.T,
            jnp.stack([log_step, skip_gain, bias_query, bias_key, bias_value]),
            bias_up.reshape(shard_units // shard, shard),
        ]
    )
    small = swap_z(jnp.broadcast_to(small, (chips,) + small.shape))
    sib = sibling(own)
    qo_z = gather_z(two_shares(w_query.T, w_out))
    params = jnp.moveaxis(small[:, :PARAM_ROWS], 0, 1).reshape(PARAM_ROWS, channels)
    units_bias = small[:, PARAM_ROWS:].reshape(chips, groups, unit_cut)
    units_bias = jnp.einsum("rg,zgu->rzu", g_flip, units_bias, precision=exact).reshape(groups, -1)
    ff_z = two_shares(w_up.T, w_down)
    ff_z = jnp.broadcast_to(ff_z, (chips,) + ff_z.shape)
    mixed_kv, sib, qo_z, params, units_bias, order, keeps, ff_z, cotangent = fence(
        mixed_kv, sib, qo_z, params, units_bias, order, keeps, ff_z, cotangent
    )

    ff_z = swap_z(ff_z)
    mixed_qo = gather_group(qo_z)
    mixer = Mixer(rows, channels, width, groups)
    normed, wkv, tables, kern, key, value, prod, shifted, er, ei, dr, di, ends, chip = mixer.before(
        core, keeps, own, sib, line(mix_gain), line(mix_shift), order, mixed_kv, params
    )
    chip, ends, cotangent, mixed_qo, first, second = fence(chip, ends, cotangent, mixed_qo, first, second)

    recv = [chip_shift(chip, by) for by in range(1, chips)]
    wqo, query, near = mixer.near(normed, prod, mixed_qo, order, params, kern)
    cot = to_steps(cotangent)
    around = me_chip + jnp.stack([-jnp.arange(chips), jnp.arange(chips)])
    masks = jnp.prod(keep(4 * around[..., None] + jnp.arange(4)), axis=-1)
    recv, near, ff_z, cot = fence(recv, near, ff_z, cot)

    if not square:
        ff_z = jnp.moveaxis(ff_z.reshape(chips, 2, unit_cut, width), 1, 0)
    ff_z = ff_z.reshape(-1, width)
    ff_one = first_round(ff_z)
    cot_sib = sibling(cot)
    conv, core_low, state_r, state_i, mixed = mixer.conv(
        keeps, masks, near, query, er, ei, ends, recv, wqo, tables
    )
    mixed, cot_sib, ff_one = fence(mixed, cot_sib, ff_one)

    mixed_sib = sibling(mixed)
    ff_two = second_round(ff_one)
    (mixed_sib,) = fence(mixed_sib)

    units = chips * unit_cut
    if square:
        arrays = [ff_z, *ff_one]
        near_half = chips // 2

        def rows_of(z, which):
            return (z % near_half * 2 + which) * unit_cut

        every = [(z, which) for z in range(chips) for which in range(2)]
        reads = [
            [(s, (z * 2 + w) * unit_cut, w, z * unit_cut, unit_cut) for z, w in every] for s in range(3)
        ] + [[(z // near_half, rows_of(z, w), w, z * unit_cut, unit_cut) for z, w in every]]
        to = ((0, 3), (2, 4), (1, 5), (0, 1))
        slots = ((0, 0),) * 4
        writes = [
            [
                (to[s][z // near_half], slots[s][z // near_half], rows_of(z, w), w, z * unit_cut, unit_cut)
                for z, w in every
            ]
            for s in range(4)
        ]
        out_shapes = [(1, units)] * 2 + [(1, units)] + [(1, units)] * 2 + [(1, units)]
    else:
        arrays = [ff_z, *ff_one]
        reads = [[(s, w * units, w, 0, units) for w in range(2)] for s in range(groups)]
        writes = [[(s, 0, w * units, w, 0, units) for w in range(2)] for s in range(groups)]
        out_shapes = [(1, 2 * units)] * groups
    lines = jnp.stack([bias_out, mlp_gain, mlp_shift])
    state = (own, sib, mixed, mixed_sib, cot, cot_sib)
    n_first = 3 if square else groups
    (*branch, grad_two, residual, xs, cs, grad_units_bias), grad_ff = feed_forward(
        core, units_bias[:n_first], lines, state, arrays[:n_first], reads[:n_first], out_shapes, writes[:n_first], not square
    )
    if square:
        branch, grad_two, xs, cs, ff_two = fence(branch, grad_two, xs, cs, ff_two)
        (*branch, grad_two, more_bias), grad_diagonal = feed_forward(
            core, units_bias[3:], lines, (*branch, grad_two, xs, cs), ff_two, reads[3:], [(1, units)] * 2, writes[3:], True
        )
        grad_units_bias = jnp.concatenate([grad_units_bias, more_bias])

    branch_own = branch[0]
    grad_two_sib, branch_sib = sibling(grad_two), sibling(branch[1])
    if square:
        fold_one = fold_first((grad_ff[2][0], grad_diagonal[0][0]), (grad_ff[5][0], grad_diagonal[1][0]))
    else:
        fold_one = ()
    after = mixer.after(
        core, keeps, residual, grad_two, grad_two_sib, cot, cot_sib, line(mlp_gain), order, wqo, normed, query, conv,
        core_low, tables,
    )
    grad_residual, g, grad_query, *qsums, ends, chip, sums = after[:10]
    grad_qo = after[10:]
    chip, grad_qo, branch_own, branch_sib, ends, g = fence(chip, grad_qo, branch_own, branch_sib, ends, g)

    recv = [chip_shift(chip, -by) for by in range(1, chips)]
    near, lags = mixer.near_back(g, prod, params, kern)
    recv, near, lags, fold_one, grad_qo = fence(recv, near, lags, fold_one, grad_qo)

    bias_rows = grad_units_bias.reshape(groups, chips, unit_cut)
    bias_rows = jnp.einsum("kz,rg,rzu->kgu", z_turn, g_flip, bias_rows, precision=exact)
    bias_rows = jnp.pad(bias_rows.reshape(chips, -1, shard), ((0, 0), (0, 0), (0, LANES - shard)))
    used = PARAM_ROWS + 8 + bias_rows.shape[1]

    fold_two = fold_second(fold_one, grad_ff[1][0], grad_ff[4][0]) if square else ()
    blocks = channels // LANES
    grads_of = lambda base, count, before: mixer.grads(
        base, count, core, keeps, masks, near, lags, qsums, (state_r, state_i), (dr, di), ends, recv, params, tables, key,
        value, shifted, grad_query, normed, wkv, wqo, order, before,
    )
    grad_keep, grad_send, params_most, grad_w = grads_of(0, 1, None)
    fold_two, grad_keep, grad_w = fence(fold_two, grad_keep, grad_w)

    if square:
        ff = jnp.concatenate(fold_end(fold_one, fold_two, grad_ff[0][0], grad_ff[3][0]))
    else:
        ff = fold_group([x[0] for x in grad_ff]).reshape(2, chips, unit_cut, width)
        ff = jnp.moveaxis(ff, 1, 0)
    ff = ff.reshape(chips, 2 * unit_cut, width)
    ff = [lax.dynamic_index_in_dim(ff, (me_chip + k) % chips, 0, keepdims=False) for k in range(chips)]
    ff_odd = [chip_turn(ff[k], k) for k in range(1, chips, 2)]
    grad_keep, grad_send, params_rest, *grad_kv = grads_of(1, blocks - 1, (grad_keep, grad_send, grad_w))
    grad_kv, grad_keep, grad_send, params_rest, ff, ff_odd, grad_qo = fence(
        grad_kv, grad_keep, grad_send, params_rest, ff, ff_odd, grad_qo
    )

    kv = fold_group(grad_kv)
    ff = add(ff[0], *ff_odd, *(chip_turn(ff[k], k) for k in range(2, chips, 2)))
    from_sib = sibling(grad_send)
    tail = tail_of(core, grad_keep, grad_send, own, sib, sums, params_most, params_rest, bias_rows, shard)
    edge = grad_send[rows:] + from_sib[rows:]
    edge = lax.ppermute(edge, "chan", [(2 * z + 3, 2 * z + 1) for z in range(chips - 1)])
    kv, tail, ff, from_sib, edge = fence(kv, tail, ff, from_sib, edge)

    qo = fold_group(grad_qo)
    kv = fold_z([jnp.concatenate(p) for p in zip(pieces(kv, chips), tail)])
    ff = gather_group(ff)
    mine = lax.dynamic_slice_in_dim(residual, me_core * rows, rows, axis=0)
    output = to_rows((mine + branch_own + branch_sib + bias_down).astype(BF16))
    grad_input = to_rows(finish(core, grad_keep, from_sib, edge, own, grad_residual, line(mix_gain)))
    qo = fold_z(pieces(qo, chips))
    kv, qo, output, grad_input, ff = fence(kv, qo, output, grad_input, ff)

    kv = gather_group(kv)
    qo = gather_group(qo)
    grad_wf = by_index(ff).reshape(groups, 2, unit_cut, width)
    grad_wf = jnp.moveaxis(grad_wf, 1, 0).reshape(2, shard_units, width).astype(F32)

    def halves(parts):
        x = by_index(parts).reshape(groups, 2, cut, width)
        return jnp.moveaxis(x, 1, 0).reshape(2, shard, width).astype(F32)

    (grad_wk, grad_wv), (grad_wq, grad_wo) = halves([x[: 2 * cut] for x in kv]), halves(qo)
    tail = sum(x[2 * cut :].astype(F32) for x in kv)
    tail = tail.reshape(-1, width // LANES, LANES).transpose(1, 0, 2).reshape(-1, LANES)[:used, :shard]
    modes = [tail[i * MODES : (i + 1) * MODES].T for i in range(4)]
    biases = tail[BIAS_ROW:PARAM_ROWS]
    feat_part = tail[PARAM_ROWS : PARAM_ROWS + 6]
    first_two = feat_part[:2] + sibling(tail[PARAM_ROWS + 6 : PARAM_ROWS + 8])
    sum_bias_up = tail[PARAM_ROWS + 8 :].reshape(shard_units)
    return (
        output,
        grad_input,
        first_two[0],
        first_two[1],
        grad_wq.T,
        biases[0],
        grad_wk.T,
        biases[1],
        grad_wv.T,
        biases[2],
        tail[TAP_ROW : TAP_ROW + TAPS].T,
        tail[STEP_ROW],
        modes[0],
        modes[1],
        modes[2],
        modes[3],
        tail[SKIP_ROW],
        grad_wo,
        feat_part[2],
        feat_part[3],
        feat_part[4],
        grad_wf[0].T,
        sum_bias_up,
        grad_wf[1],
        feat_part[5],
    )


def solution(mesh):
    rows = P(("group", "chan"), None)
    columns, channels, vector, copied = P(None, "chan"), P("chan", None), P("chan"), P()
    return jax.shard_map(
        functools.partial(local, mesh.shape["group"], mesh.shape["chan"] // 2),
        mesh=mesh,
        in_specs=(
            rows, copied, copied, columns, vector, columns, vector, columns, vector, channels,
            vector, channels, channels, channels, channels, vector, channels, copied, copied, copied,
            columns, vector, channels, copied, rows, P("group", None),
        ),
        out_specs=(
            rows, rows, vector, vector, columns, vector, columns, vector, columns, vector,
            channels, vector, channels, channels, channels, channels, vector, channels, vector, vector,
            vector, columns, vector, channels, vector,
        ),
        check_vma=False,
    )
```

```python
import functools

import jax
import jax.numpy as jnp
import numpy as np
from jax import lax
from jax.experimental import pallas as pl
from jax.experimental.pallas import tpu as pltpu
from jax.sharding import PartitionSpec as P

F32 = jnp.float32
BF16 = jnp.bfloat16
MODES = 32
LANES = 128
SEGS = 8
TAPS = 4
BLOCK = 8
HALO = 16
TILE = 128
LN_TILE = 64
EPSILON = 1e-05
VMEM_LIMIT = 60 * 1024 * 1024
SMEM = pl.BlockSpec(memory_space=pltpu.SMEM)

TAP_ROW = 4 * MODES
STEP_ROW = TAP_ROW + TAPS
SKIP_ROW = STEP_ROW + 1
BIAS_ROW = SKIP_ROW + 1
PARAM_ROWS = BIAS_ROW + 3


def ssm_tables(log_step, log_decay, frequency, out_real, out_imag):
    step_size = jnp.exp(log_step)
    rate = -jnp.exp(log_decay)
    decay = rate * step_size
    turn = frequency * step_size
    growth = jnp.exp(decay)
    ratio_re = growth * jnp.cos(turn) - 1.0
    ratio_im = growth * jnp.sin(turn)
    denom = rate * rate + frequency * frequency
    scaled_re = (ratio_re * rate + ratio_im * frequency) / denom
    scaled_im = (ratio_im * rate - ratio_re * frequency) / denom
    weight_re = out_real * scaled_re - out_imag * scaled_im
    weight_im = out_real * scaled_im + out_imag * scaled_re
    return decay, turn, weight_re, weight_im


def table_inputs(params):
    parts = [params[pl.ds(i * MODES, MODES), :] for i in range(4)]
    return [params[pl.ds(STEP_ROW, 1), :], *parts]


def read_tables(tables):
    return [tables[pl.ds(i * MODES, MODES), :] for i in range(4)]


def dot_nn(a, b):
    return lax.dot_general(a, b, (((1,), (0,)), ((), ())), preferred_element_type=F32)


def dot_nt(a, b):
    return lax.dot_general(a, b, (((1,), (1,)), ((), ())), preferred_element_type=F32)


def dot_tn(a, b):
    return lax.dot_general(a, b, (((0,), (0,)), ((), ())), preferred_element_type=F32)


def cmul(ar, ai, br, bi):
    return ar * br - ai * bi, ar * bi + ai * br


def normalize(values):
    center = values - jnp.mean(values, axis=-1, keepdims=True)
    scale = lax.rsqrt(jnp.mean(center * center, axis=-1, keepdims=True) + EPSILON)
    return center * scale, scale


def normalize_back(grad, gain, xhat, scale):
    gy = grad * gain
    mean_gy = jnp.mean(gy, axis=-1, keepdims=True)
    mean_gx = jnp.mean(gy * xhat, axis=-1, keepdims=True)
    return scale * (gy - mean_gy - xhat * mean_gx)


def pack_kernel(decay, freq, real, imag, taps, step, skip, bias_q, bias_k, bias_v, bias_up, out, rows_of):
    shard = decay.shape[1]
    at = 0
    for x in (decay, freq, real, imag, taps):
        n = x.shape[0]
        rows_of[pl.ds(at, n), :] = x[...]
        at += n
    for x in (step, skip, bias_q, bias_k, bias_v):
        rows_of[pl.ds(at, 1), :] = x[...]
        at += 1
    for i in range(bias_up.shape[1] // shard):
        rows_of[pl.ds(at + i, 1), :] = bias_up[:, pl.ds(i * shard, shard)]
    for i in range(out.shape[0]):
        out[i] = rows_of[...]


def pack(chips, matrices, vectors, bias_up):
    shard = matrices[0].shape[1]
    rows = PARAM_ROWS + bias_up.shape[0] // shard
    return pl.pallas_call(
        pack_kernel,
        out_shape=jax.ShapeDtypeStruct((chips, rows, shard), F32),
        scratch_shapes=[pltpu.VMEM((rows, shard), F32)],
        cost_estimate=pl.CostEstimate(flops=10**6, bytes_accessed=10**4, transcendentals=0),
        name="pack",
    )(*matrices, *(v.reshape(1, -1) for v in vectors), bias_up.reshape(1, -1))


def fill_powers(zr, zi, pr, pi, steps):
    ar, ai = jnp.ones_like(zr), jnp.zeros_like(zi)
    pr[pl.ds(0, MODES), :] = ar
    pi[pl.ds(0, MODES), :] = ai
    for j in range(1, steps + 1):
        ar, ai = cmul(ar, ai, zr, zi)
        pr[pl.ds(j * MODES, MODES), :] = ar
        pi[pl.ds(j * MODES, MODES), :] = ai
    return ar, ai


def over_chunk(ar, ai):
    n = 1
    while n < SEGS:
        ar, ai = cmul(ar, ai, ar, ai)
        n *= 2
    return ar, ai


def fill_kern(wr, wi, pr, pi, kern, steps):
    for j in range(steps):
        v = wr * pr[pl.ds(j * MODES, MODES), :] - wi * pi[pl.ds(j * MODES, MODES), :]
        kern[pl.ds(j, 1), :] = 2.0 * jnp.sum(v, axis=0, keepdims=True)


def row(ref, i):
    return jnp.broadcast_to(ref[pl.ds(i, 1), :], (SEGS, LANES))


def group(ref, steps, c, t):
    return ref[pl.ds((c * steps + t) * SEGS, SEGS), :]


def put(ref, steps, c, t, value):
    ref[pl.ds((c * steps + t) * SEGS, SEGS), :] = value


def put_low(ref, steps, c, t, pair):
    ref[pl.ds((c * steps + t) * SEGS, 2 * SEGS), :] = jnp.concatenate(pair).astype(BF16)


def sublanes():
    return lax.broadcasted_iota(jnp.int32, (SEGS, LANES), 0)


def seg_mask(keep0, keep4):
    ids = sublanes()
    m = jnp.where(ids == 0, keep0, 1.0)
    return jnp.where(ids == SEGS // 2, keep4, m)


def seg_rows(c, k):
    return pl.ds(c * MODES * SEGS + k, MODES, stride=SEGS)


def mode_rows(c, m):
    return pl.ds(pl.multiple_of(c * MODES * SEGS + m * SEGS, SEGS), SEGS)


def weigh(pr, pi, steps, order, power, last, data, outs):
    outs_r, outs_i, runs_r, runs_i = outs
    half = steps // 2
    for part in range(2):
        ts = order[part * half : (part + 1) * half]
        values = [[data(c, t) for t in ts] for c in range(2)]

        def per_mode(m, carry):
            acc = []
            for c in range(2):
                if part == 0:
                    acc.append([jnp.zeros((SEGS, LANES), F32)] * 4)
                else:
                    acc.append([r[mode_rows(c, m), :] for r in (outs_r, outs_i, runs_r, runs_i)])
            for i, t in enumerate(ts):
                a, b = row(pr, power(t) * MODES + m), row(pi, power(t) * MODES + m)
                for c in range(2):
                    sr, si, tr, ti = acc[c]
                    sr, si = sr + a * values[c][i], si + b * values[c][i]
                    if last or t != order[-1]:
                        tr, ti = tr + sr, ti + si
                    acc[c] = [sr, si, tr, ti]
            for c in range(2):
                for r, v in zip((outs_r, outs_i, runs_r, runs_i), acc[c]):
                    r[mode_rows(c, m), :] = v
            return carry

        lax.fori_loop(0, MODES, per_mode, 0, unroll=8)


def unfold(pr, pi, steps, power, states, base, done):
    half = steps // 2
    for part in range(2):
        ts = range(part * half, (part + 1) * half)
        init = tuple(base(c, t) for c in range(2) for t in ts)

        def per_mode(m, acc):
            acc = list(acc)
            u = [states[0][mode_rows(c, m), :] for c in range(2)]
            v = [states[1][mode_rows(c, m), :] for c in range(2)]
            for i, t in enumerate(ts):
                a, b = row(pr, power(t) * MODES + m), row(pi, power(t) * MODES + m)
                for c in range(2):
                    at = c * half + i
                    acc[at] = acc[at] + (a * u[c] - b * v[c])
            return tuple(acc)

        acc = lax.fori_loop(0, MODES, per_mode, init, unroll=8)
        for c in range(2):
            for i in range(0, half, 2):
                done(c, ts[i], acc[c * half + i : c * half + i + 2])


def lags_apply(kern, steps, base, source, out, adjoint):
    n = steps // BLOCK
    for tb in range(n):
        ts = range(tb * BLOCK, (tb + 1) * BLOCK)
        ys = {(c, t): base(c, t) for c in range(2) for t in ts}
        for sb in range(tb, n) if adjoint else range(tb + 1):
            ss = range(sb * BLOCK, (sb + 1) * BLOCK)
            xs = {(c, s): source(c, s) for c in range(2) for s in ss}
            for lag in range(steps):
                pairs = [(t, s) for t in ts for s in ss if (s - t if adjoint else t - s) == lag]
                if pairs:
                    k = row(kern, lag)
                    for t, s in pairs:
                        for c in range(2):
                            ys[c, t] = ys[c, t] + k * xs[c, s]
        for (c, t), y in ys.items():
            put(out, steps, c, t, y)


def lag_sums(steps, left, right):
    n = steps // BLOCK
    sums = []
    for jb in range(n):
        acc = [jnp.zeros((SEGS, LANES), F32)] * BLOCK
        for c in range(2):
            for tb in range(jb, n):
                ts = range(tb * BLOCK, (tb + 1) * BLOCK)
                base = (tb - jb) * BLOCK
                xs = {s: right(c, s) for s in range(max(base - BLOCK + 1, 0), base + BLOCK)}
                for t in ts:
                    g = left(c, t)
                    for j in range(BLOCK):
                        s = t - jb * BLOCK - j
                        if s >= 0:
                            acc[j] = acc[j] + g * xs[s]
        sums.extend(jnp.sum(a, axis=0, keepdims=True) for a in acc)
    return sums


def earlier_keys(key, steps, keeps):
    ids = sublanes()
    out = []
    rolled = None
    for c in range(2):
        mask = seg_mask(keeps[c, 0], keeps[c, 1])
        new, windows = [], []
        for back in (1, 2, 3):
            v = pltpu.roll(group(key, steps, c, steps - back), 1, 0)
            new.append(v)
            before = row(key, 2 * steps * SEGS + HALO - back) if c == 0 else rolled[back - 1]
            windows.append(jnp.where(ids == 0, before, v) * mask)
        rolled = new
        out.append(windows)
    return out


def chunk_of(own, sib, core, c, at):
    return jnp.where(core == c, own[at, :].astype(F32), sib[at, :].astype(F32))


def join(parts, out):
    at = 0
    for p in parts:
        n = p.shape[0]
        out[pl.ds(at, n), :] = p[...]
        at += n


def part_to(outs, value):
    at = 0
    for o in outs:
        n = o.shape[0]
        o[...] = value[at : at + n].astype(BF16)
        at += n


def before_kernel(steps, n_parts, core, keeps, own, sib, gain, shift, order, *refs):
    mixed_kv, params = refs[:n_parts], refs[n_parts]
    normed, wkv, tables, kern, key, value, prod, shifted, er, ei, dr, di, ends, chip, pr, pi, joined = refs[n_parts + 1 :]
    lane = pl.program_id(0)
    rows = steps * SEGS
    channels = wkv.shape[0] // 2

    @pl.when(lane == 0)
    def _():
        me = core[0]
        join(mixed_kv, joined)
        wkv[...] = dot_nn(order[...], joined[...]).astype(BF16)

        def rows_of(x):
            xhat, _ = normalize(x)
            return (xhat * gain[...] + shift[...]).astype(BF16)

        for c in range(2):
            for r in range(0, rows, LN_TILE):
                normed[pl.ds(c * rows + r, LN_TILE), :] = rows_of(chunk_of(own, sib, me, c, pl.ds(r, LN_TILE)))
        normed[pl.ds(2 * rows, HALO), :] = rows_of(chunk_of(own, sib, me, 1, pl.ds(rows, HALO)))

    decay, turn, wr, wi = ssm_tables(*table_inputs(params))
    mag = jnp.exp(decay)
    zr, zi = mag * jnp.cos(turn), mag * jnp.sin(turn)
    for i, v in enumerate((zr, zi, wr, wi)):
        tables[pl.ds(i * MODES, MODES), :] = v
    ar, ai = fill_powers(zr, zi, pr, pi, steps)
    fill_kern(wr, wi, pr, pi, kern, steps)
    at = pl.ds(pl.multiple_of(lane * LANES, LANES), LANES)
    also = pl.ds(pl.multiple_of(channels + lane * LANES, LANES), LANES)
    key[...] = dot_nt(normed[...], wkv[at, :]) + params[pl.ds(BIAS_ROW + 1, 1), :]
    value[...] = dot_nt(normed[pl.ds(0, 2 * rows), :], wkv[also, :]) + params[pl.ds(BIAS_ROW + 2, 1), :]
    tap = [row(params, TAP_ROW + j) for j in range(TAPS)]
    windows = earlier_keys(key, steps, keeps)
    for c in range(2):
        window = windows[c]
        for t in range(steps):
            cur = group(key, steps, c, t)
            s = tap[0] * cur + tap[1] * window[0] + tap[2] * window[1] + tap[3] * window[2]
            window = [cur] + window[:2]
            put(shifted, steps, c, t, s)
            put(prod, steps, c, t, s * group(value, steps, c, t))
    weigh(
        pr, pi, steps, list(range(steps)), lambda t: steps - 1 - t, False,
        lambda c, t: group(prod, steps, c, t), (er, ei, dr, di),
    )
    states = []
    for c in range(2):
        k4 = keeps[c, 1]
        sr = si = jnp.zeros((MODES, LANES), F32)
        for k in range(SEGS):
            if k == SEGS // 2:
                sr, si = sr * k4, si * k4
            cr, ci = cmul(sr, si, ar, ai)
            sr = cr + er[seg_rows(c, k), :]
            si = ci + ei[seg_rows(c, k), :]
        states.append((sr, si))
    ends[pl.ds(0, MODES), :], ends[pl.ds(MODES, MODES), :] = states[0]
    br, bi = over_chunk(ar, ai)
    cr, ci = cmul(*states[0], br, bi)
    keep = keeps[1, 0] * keeps[1, 1]
    chip[pl.ds(0, MODES), :] = (cr * keep + states[1][0]).astype(BF16)
    chip[pl.ds(MODES, MODES), :] = (ci * keep + states[1][1]).astype(BF16)


def incoming(ref_list, masks, which, ar, ai):
    br, bi = cmul(ar, ai, ar, ai)
    read = lambda r: (r[pl.ds(0, MODES), :].astype(F32), r[pl.ds(MODES, MODES), :].astype(F32))
    sr, si = read(ref_list[-1])
    for by in range(len(ref_list) - 1, 0, -1):
        m = masks[which, by]
        cr, ci = cmul(sr, si, br * m, bi * m)
        rr, ri = read(ref_list[by - 1])
        sr, si = cr + rr, ci + ri
    return sr, si


def near_kernel(steps, n_parts, normed, prod, *refs):
    mixed_qo = refs[:n_parts]
    order, params, kern, wqo, query, near, joined = refs[n_parts:]
    lane = pl.program_id(0)
    rows = steps * SEGS

    @pl.when(lane == 0)
    def _():
        join(mixed_qo, joined)
        wqo[...] = dot_nn(order[...], joined[...]).astype(BF16)

    at = pl.ds(pl.multiple_of(lane * LANES, LANES), LANES)
    query[...] = dot_nt(normed[pl.ds(0, 2 * rows), :], wqo[at, :]) + params[pl.ds(BIAS_ROW, 1), :]
    source = lambda c, t: group(prod, steps, c, t)
    sk = row(params, SKIP_ROW)
    lags_apply(kern, steps, lambda c, t: sk * source(c, t), source, near, False)


def conv_kernel(steps, n_recv, keeps, masks, near, query, er, ei, ends, *refs):
    recv = refs[:n_recv]
    wo, tables, conv, core_low, state_r, state_i, mixed_low, pr, pi, twice_r, twice_i, mixed = refs[n_recv:]
    lane = pl.program_id(0)
    zr, zi, wr, wi = read_tables(tables)
    ar, ai = fill_powers(zr, zi, pr, pi, steps)
    w2r, w2i = 2.0 * wr, 2.0 * wi
    br, bi = over_chunk(ar, ai)
    sr, si = incoming(recv, masks, 0, br, bi)
    for c in range(2):
        if c == 1:
            sr, si = cmul(first_r, first_i, br * keeps[0, 1], bi * keeps[0, 1])
            sr, si = sr + ends[pl.ds(0, MODES), :], si + ends[pl.ds(MODES, MODES), :]
        sr, si = sr * keeps[c, 0], si * keeps[c, 0]
        first_r, first_i = sr, si
        for k in range(SEGS):
            if k == SEGS // 2:
                sr, si = sr * keeps[c, 1], si * keeps[c, 1]
            state_r[seg_rows(c, k), :] = sr
            state_i[seg_rows(c, k), :] = si
            twice_r[seg_rows(c, k), :], twice_i[seg_rows(c, k), :] = cmul(w2r, w2i, sr, si)
            if k < SEGS - 1:
                cr, ci = cmul(sr, si, ar, ai)
                sr = cr + er[seg_rows(c, k), :]
                si = ci + ei[seg_rows(c, k), :]

    def done(c, t, values):
        low = []
        for i, v in zip((t, t + 1), values):
            put(conv, steps, c, i, v)
            low.append(v * group(query, steps, c, i))
        put_low(core_low, steps, c, t, low)

    unfold(pr, pi, steps, lambda t: t + 1, (twice_r, twice_i), lambda c, t: group(near, steps, c, t), done)
    out = dot_nn(core_low[...], wo[...])

    @pl.when(lane == 0)
    def _():
        mixed[...] = out

    @pl.when(jnp.logical_and(lane > 0, lane < pl.num_programs(0) - 1))
    def _():
        mixed[...] += out

    @pl.when(lane == pl.num_programs(0) - 1)
    def _():
        mixed_low[...] = (mixed[...] + out).astype(BF16)


def after_kernel(
    steps, core, keeps, residual, grad_own, grad_sib, cot_own, cot_sib, gain, order, wo, normed, query, conv, core_low,
    tables, grad_residual, g, grad_query, qr, qi, rr, ri, ends, chip, sums, *refs,
):
    grad_qo, (pr, pi, low, grad_core, grad_w) = refs[:-5], refs[-5:]
    lane = pl.program_id(0)
    rows = steps * SEGS
    channels = grad_w.shape[0] // 2

    @pl.when(lane == 0)
    def _():
        me = core[0]
        total = [jnp.zeros((1, low.shape[1]), F32)] * 4
        for c in range(2):
            for r in range(0, rows, LN_TILE):
                at = pl.ds(c * rows + r, LN_TILE)
                xhat, scale = normalize(residual[at, :])
                grad = grad_own[at, :].astype(F32) + grad_sib[at, :].astype(F32)
                cot = chunk_of(cot_own, cot_sib, me, c, pl.ds(r, LN_TILE))
                out = cot + normalize_back(grad, gain[...], xhat, scale)
                grad_residual[at, :] = out
                low[at, :] = out.astype(BF16)
                for i, v in enumerate((out, grad * xhat, grad, cot)):
                    total[i] = total[i] + jnp.sum(v, axis=0, keepdims=True)
        sums[...] = jnp.concatenate(total, axis=0)

    zr, zi, wr, wi = read_tables(tables)
    ar, ai = fill_powers(zr, zi, pr, pi, steps)
    grad_core[...] = dot_nt(low[...], wo[...])
    for c in range(2):
        for t in range(0, steps, 2):
            pair = []
            for i in (t, t + 1):
                d = group(grad_core, steps, c, i)
                put(g, steps, c, i, d * group(query, steps, c, i))
                pair.append(d * group(conv, steps, c, i))
            put_low(grad_query, steps, c, t, pair)
    at = pl.ds(pl.multiple_of(lane * LANES, LANES), LANES)
    also = pl.ds(pl.multiple_of(channels + lane * LANES, LANES), LANES)
    grad_w[at, :] = dot_tn(grad_query[...], normed[pl.ds(0, 2 * rows), :]).astype(BF16)
    grad_w[also, :] = dot_tn(core_low[...], low[...]).astype(BF16)

    @pl.when(lane == pl.num_programs(0) - 1)
    def _():
        part_to(grad_qo, dot_tn(order[...], grad_w[...]))

    weigh(
        pr, pi, steps, list(reversed(range(steps))), lambda t: t + 1, True,
        lambda c, t: group(g, steps, c, t), (qr, qi, rr, ri),
    )
    w2r, w2i = 2.0 * wr, 2.0 * wi
    lr = li = jnp.zeros((MODES, LANES), F32)
    for c in (1, 0):
        for k in reversed(range(SEGS)):
            cr, ci = cmul(lr, li, ar, ai)
            ur, ui = cmul(w2r, w2i, qr[seg_rows(c, k), :], qi[seg_rows(c, k), :])
            lr, li = ur + cr, ui + ci
            if k == SEGS // 2:
                lr, li = lr * keeps[c, 1], li * keeps[c, 1]
        lr, li = lr * keeps[c, 0], li * keeps[c, 0]
        if c == 1:
            ends[pl.ds(0, MODES), :] = lr
            ends[pl.ds(MODES, MODES), :] = li
    chip[pl.ds(0, MODES), :] = lr.astype(BF16)
    chip[pl.ds(MODES, MODES), :] = li.astype(BF16)


def near_back_kernel(steps, g, prod, params, kern, near, lags):
    source = lambda c, t: group(g, steps, c, t)
    other = lambda c, t: group(prod, steps, c, t)
    sk = row(params, SKIP_ROW)
    for j, lag in enumerate(lag_sums(steps, source, other)):
        lags[pl.ds(j, 1), :] = lag
    dsk = jnp.zeros((SEGS, LANES), F32)
    for c in range(2):
        for t in range(steps):
            dsk = dsk + source(c, t) * other(c, t)
    lags[pl.ds(steps, 1), :] = jnp.sum(dsk, axis=0, keepdims=True)
    lags_apply(kern, steps, lambda c, t: sk * source(c, t), source, near, True)


def grads_kernel(steps, n_recv, base, last, core, keeps, masks, near, lags, qr, qi, rr, ri, state_r, state_i, dr, di, ends, *refs):
    recv = refs[:n_recv]
    params, tables, key, value, shifted, grad_query, normed, wk, wv, wq = refs[n_recv : n_recv + 10]
    refs = refs[n_recv + 10 :]
    if last:
        order, before_keep, before_send, before_w, *refs = refs
        grad_keep, grad_send, grad_params, *grad_kv = refs[:-8]
        pr, pi, mur, mui, back, cat, cat_w, grad_w = refs[-8:]
    else:
        before_keep = before_send = None
        grad_keep, grad_send, grad_params, grad_w, pr, pi, mur, mui, back, cat, cat_w = refs
    lane = pl.program_id(0)
    rows = steps * SEGS
    channels = grad_w.shape[0] // 2
    ids = sublanes()
    zr, zi, wr, wi = read_tables(tables)
    ar, ai = fill_powers(zr, zi, pr, pi, steps)
    w2r, w2i = 2.0 * wr, 2.0 * wi
    br, bi = over_chunk(ar, ai)
    mr, mi = incoming(recv, masks, 1, br, bi)
    zero = jnp.zeros((MODES, LANES), F32)
    awr = awi = azr = azi = acr = aci = zero
    for c in (1, 0):
        if c == 0:
            keep = keeps[1, 0] * keeps[1, 1]
            mr, mi = cmul(last_r, last_i, br * keep, bi * keep)
            mr, mi = mr + ends[pl.ds(0, MODES), :], mi + ends[pl.ds(MODES, MODES), :]
        last_r, last_i = mr, mi
        for k in reversed(range(SEGS)):
            at = seg_rows(c, k)
            mur[at, :] = mr
            mui[at, :] = mi
            s_r, s_i = state_r[at, :], state_i[at, :]
            q_r, q_i = qr[at, :], qi[at, :]
            u = cmul(s_r, s_i, q_r, q_i)
            awr, awi = awr + u[0], awi + u[1]
            u = cmul(s_r, s_i, rr[at, :], ri[at, :])
            azr, azi = azr + u[0], azi + u[1]
            u = cmul(mr, mi, dr[at, :], di[at, :])
            acr, aci = acr + u[0], aci + u[1]
            u = cmul(mr, mi, s_r, s_i)
            u = cmul(u[0], u[1], ar, ai)
            acr, aci = acr + float(steps) * u[0], aci + float(steps) * u[1]
            if k > 0:
                ur, ui = cmul(w2r, w2i, q_r, q_i)
                cr, ci = cmul(mr, mi, ar, ai)
                mr, mi = ur + cr, ui + ci
                if k == SEGS // 2:
                    mr, mi = mr * keeps[c, 1], mi * keeps[c, 1]
    for j in range(steps):
        lag = lags[pl.ds(j, 1), :]
        u, v = pr[pl.ds(j * MODES, MODES), :] * lag, pi[pl.ds(j * MODES, MODES), :] * lag
        awr, awi = awr + u, awi + v
        azr, azi = azr + float(j) * u, azi + float(j) * v
    u = cmul(w2r, w2i, azr, azi)
    _, tables_back = jax.vjp(ssm_tables, *table_inputs(params))
    dstep, *dmodes = tables_back((u[0] + acr, -(u[1] + aci), 2.0 * awr, -2.0 * awi))
    for i, v in enumerate(dmodes):
        grad_params[pl.ds(i * MODES, MODES), :] = v
    grad_params[pl.ds(STEP_ROW, 1), :] = dstep
    grad_params[pl.ds(SKIP_ROW, 1), :] = lags[pl.ds(steps, 1), :]

    def done(c, t, values):
        low = []
        for i, v in zip((t, t + 1), values):
            low.append(v * group(shifted, steps, c, i))
            put(back, steps, c, i, v * group(value, steps, c, i))
        cat[pl.ds((c * steps + t) * SEGS, 2 * SEGS), pl.ds(LANES, LANES)] = jnp.concatenate(low).astype(BF16)

    unfold(pr, pi, steps, lambda t: steps - 1 - t, (mur, mui), lambda c, t: group(near, steps, c, t), done)
    tap = [row(params, TAP_ROW + j) for j in range(TAPS)]
    windows = earlier_keys(key, steps, keeps)
    acc = [jnp.zeros((SEGS, LANES), F32)] * TAPS
    for c in range(2):
        window = windows[c]
        for t in range(steps):
            cur = group(key, steps, c, t)
            v = group(back, steps, c, t)
            for j, w in enumerate([cur] + window):
                acc[j] = acc[j] + v * w
            window = [cur] + window[:2]
    for j, a in enumerate(acc):
        grad_params[pl.ds(TAP_ROW + j, 1), :] = jnp.sum(a, axis=0, keepdims=True)
    following = [jnp.zeros((SEGS, LANES), F32)] * (TAPS - 1)
    for c in (1, 0):
        mask = seg_mask(keeps[c, 0], keeps[c, 1])
        begin = [group(back, steps, c, t) * mask for t in range(TAPS - 1)]
        later = [pltpu.roll(jnp.where(ids == 0, f, v), SEGS - 1, 0) for f, v in zip(following, begin)]
        following = begin
        ext = lambda t: group(back, steps, c, t) if t < steps else later[t - steps]
        for t in range(0, steps, 2):
            low = [
                tap[0] * ext(i) + tap[1] * ext(i + 1) + tap[2] * ext(i + 2) + tap[3] * ext(i + 3) for i in (t, t + 1)
            ]
            cat[pl.ds((c * steps + t) * SEGS, 2 * SEGS), pl.ds(0, LANES)] = jnp.concatenate(low).astype(BF16)
    edge = [jnp.zeros((HALO - TAPS + 1, LANES), F32)]
    for b in (3, 2, 1):
        v = jnp.zeros((1, LANES), F32)
        for j in range(b, TAPS):
            v = v + params[pl.ds(TAP_ROW + j, 1), :] * following[j - b][0:1, :]
        edge.append(v)
    halo_at = pl.ds(2 * rows, HALO)
    cat[halo_at, pl.ds(0, LANES)] = jnp.concatenate(edge, axis=0).astype(BF16)
    cat[halo_at, pl.ds(LANES, 2 * LANES)] = jnp.zeros((HALO, 2 * LANES), BF16)
    cat[pl.ds(0, 2 * rows), pl.ds(2 * LANES, LANES)] = grad_query[...]
    for i, w in enumerate((wk, wv, wq)):
        cat_w[pl.ds(i * LANES, LANES), :] = w[...]
    both = dot_tn(cat[:, pl.ds(0, 2 * LANES)], normed[...])
    if last:

        @pl.when(lane == 0)
        def _():
            grad_w[...] = before_w[...]

    at = (base + lane) * LANES
    grad_w[pl.ds(pl.multiple_of(at, LANES), LANES), :] = both[:LANES].astype(BF16)
    grad_w[pl.ds(pl.multiple_of(channels + at, LANES), LANES), :] = both[LANES:].astype(BF16)
    if last:

        @pl.when(lane == pl.num_programs(0) - 1)
        def _():
            part_to(grad_kv, dot_tn(order[...], grad_w[...]))

    for i, part in enumerate((2, 0, 1)):
        grad_params[pl.ds(BIAS_ROW + i, 1), :] = jnp.sum(cat[:, pl.ds(part * LANES, LANES)].astype(F32), axis=0, keepdims=True)
    me = core[0]
    for c in range(2):
        out = dot_nn(cat[pl.ds(c * rows, rows), :], cat_w[...])

        @pl.when(me == c)
        def _():
            add_to(grad_keep, pl.ds(0, rows), out, lane, before_keep)

        @pl.when(me != c)
        def _():
            add_to(grad_send, pl.ds(0, rows), out, lane, before_send)

    add_to(grad_send, pl.ds(rows, HALO), dot_nn(cat[halo_at, :], cat_w[...]), lane, before_send)


def add_to(ref, at, value, step, before):
    @pl.when(step == 0)
    def _():
        ref[at, :] = value if before is None else before[at, :] + value

    @pl.when(step > 0)
    def _():
        ref[at, :] += value


class Mixer:
    def __init__(self, rows, channels, width, groups):
        self.rows, self.channels, self.width, self.groups = rows, channels, width, groups
        self.steps = rows // SEGS

    def lanes(self, rows):
        return pl.BlockSpec((rows, LANES), lambda l: (0, l))

    def whole(self, *shape):
        return pl.BlockSpec(shape, lambda l: (0,) * len(shape))

    def shape(self, rows, kind=F32):
        return jax.ShapeDtypeStruct((rows, self.channels), kind)

    def wide(self, rows, kind):
        return jax.ShapeDtypeStruct((rows, self.width), kind)

    def call(self, name, kernel, in_specs, outs, scratch, work, powers=True, count=None):
        table = pltpu.VMEM(((self.steps + 1) * MODES, LANES), F32)
        return pl.pallas_call(
            kernel,
            grid=(count or self.channels // LANES,),
            in_specs=in_specs,
            out_specs=[s for s, _ in outs],
            out_shape=[s for _, s in outs],
            scratch_shapes=[table, table] * powers + scratch,
            compiler_params=pltpu.CompilerParams(vmem_limit_bytes=VMEM_LIMIT),
            cost_estimate=pl.CostEstimate(flops=work // 10000, bytes_accessed=work // 4000000, transcendentals=0),
            name=name,
        )

    def units(self, part=0):
        return pl.BlockSpec((LANES, self.width), lambda l: (l + part * self.channels // LANES, 0))

    def pair(self):
        n = 2 * self.channels
        return self.whole(n, self.width), self.wide(n, BF16)

    def parts(self):
        n = 2 * self.channels // self.groups
        return [(self.whole(n, self.width), self.wide(n, BF16))] * self.groups

    def order(self):
        return self.whole(2 * self.channels, 2 * self.channels)

    def before(self, core, keeps, own, sib, gain, shift, order, mixed_kv, params):
        n, ms, w = 2 * self.rows, 2 * MODES * SEGS, self.width
        line, states, ends = self.whole(1, w), (self.lanes(ms), self.shape(ms)), self.lanes(2 * MODES)
        return self.call(
            "ssm_before",
            functools.partial(before_kernel, self.steps, len(mixed_kv)),
            [SMEM, SMEM, self.whole(*own.shape), self.whole(*own.shape), line, line, self.order()]
            + [self.whole(*p.shape) for p in mixed_kv] + [self.lanes(PARAM_ROWS)],
            [(self.whole(n + HALO, w), self.wide(n + HALO, BF16)), self.pair(), (self.lanes(4 * MODES), self.shape(4 * MODES))]
            + [(self.lanes(self.steps), self.shape(self.steps))]
            + [(self.lanes(n + HALO), self.shape(n + HALO))] + [(self.lanes(n), self.shape(n))] * 3 + [states] * 4
            + [(ends, self.shape(2 * MODES)), (ends, self.shape(2 * MODES, BF16))],
            [pltpu.VMEM((2 * self.channels, w), BF16)],
            10**10,
        )(core, keeps, own, sib, gain, shift, order, *mixed_kv, params)

    def near(self, normed, prod, mixed_qo, order, params, kern):
        n, w = 2 * self.rows, self.width
        big = self.lanes(n)
        return self.call(
            "ssm_near",
            functools.partial(near_kernel, self.steps, len(mixed_qo)),
            [self.whole(*normed.shape), big] + [self.whole(*p.shape) for p in mixed_qo]
            + [self.order(), self.lanes(PARAM_ROWS), self.lanes(self.steps)],
            [self.pair(), (big, self.shape(n)), (big, self.shape(n))],
            [pltpu.VMEM((2 * self.channels, w), BF16)],
            6 * 10**9,
            False,
        )(normed, prod, *mixed_qo, order, params, kern)

    def conv(self, keeps, masks, near, query, er, ei, ends, recv, wqo, tables):
        n, ms, w = 2 * self.rows, 2 * MODES * SEGS, self.width
        big, states, last = self.lanes(n), self.lanes(ms), self.lanes(2 * MODES)
        return self.call(
            "ssm_conv",
            functools.partial(conv_kernel, self.steps, len(recv)),
            [SMEM, SMEM, big, big, states, states] + [last] * (1 + len(recv)) + [self.units(1), self.lanes(4 * MODES)],
            [(big, self.shape(n)), (big, self.shape(n, BF16))] + [(states, self.shape(ms))] * 2
            + [(self.whole(n, w), self.wide(n, BF16))],
            [pltpu.VMEM((ms, LANES), F32)] * 2 + [pltpu.VMEM((n, w), F32)],
            10**10,
        )(keeps, masks, near, query, er, ei, ends, *recv, wqo, tables)

    def after(
        self, core, keeps, residual, grad_own, grad_sib, cot_own, cot_sib, gain, order, wqo, normed, query, conv, core_low,
        tables,
    ):
        n, ms, w = 2 * self.rows, 2 * MODES * SEGS, self.width
        big, states, last = self.lanes(n), self.lanes(ms), self.lanes(2 * MODES)
        full, half = self.whole(n, w), self.whole(n // 2, w)
        return self.call(
            "ssm_after",
            functools.partial(after_kernel, self.steps),
            [SMEM, SMEM, full, full, full, half, half, self.whole(1, w), self.order(), self.units(1), self.whole(*normed.shape)]
            + [big] * 3 + [self.lanes(4 * MODES)],
            [(full, self.wide(n, F32)), (big, self.shape(n)), (big, self.shape(n, BF16))]
            + [(states, self.shape(ms))] * 4 + [(last, self.shape(2 * MODES)), (last, self.shape(2 * MODES, BF16))]
            + [(self.whole(4, w), self.wide(4, F32))] + self.parts(),
            [pltpu.VMEM((n, w), BF16), pltpu.VMEM((n, LANES), F32), pltpu.VMEM((2 * self.channels, w), BF16)],
            10**10,
        )(
            core, keeps, residual, grad_own, grad_sib, cot_own, cot_sib, gain, order, wqo, normed, query, conv, core_low,
            tables,
        )

    def near_back(self, g, prod, params, kern):
        big = self.lanes(2 * self.rows)
        tall = self.steps + SEGS
        return self.call(
            "ssm_near_back",
            functools.partial(near_back_kernel, self.steps),
            [big, big, self.lanes(PARAM_ROWS), self.lanes(self.steps)],
            [(big, self.shape(2 * self.rows)), (self.lanes(tall), self.shape(tall))],
            [],
            8 * 10**9,
            False,
        )(g, prod, params, kern)

    def grads(
        self, base, count, core, keeps, masks, near, lags, q, state, d, ends, recv, params, tables, key, value, shifted,
        grad_query, normed, wkv, wqo, order, before,
    ):
        n, ms, w = 2 * self.rows, 2 * MODES * SEGS, self.width
        lanes = lambda rows: pl.BlockSpec((rows, LANES), lambda l: (0, l + base))
        units = lambda part: pl.BlockSpec((LANES, w), lambda l: (l + base + part * self.channels // LANES, 0))
        big, states, ends_at = lanes(n), lanes(ms), lanes(2 * MODES)
        normed_at = [(self.whole(r, w), self.wide(r, F32)) for r in (self.rows, self.rows + HALO)]
        params_at = (lanes_from(PARAM_ROWS), jax.ShapeDtypeStruct((PARAM_ROWS, count * LANES), F32))
        last = before is not None
        return self.call(
            "ssm_grads_last" if last else "ssm_grads",
            functools.partial(grads_kernel, self.steps, len(recv), base, last),
            [SMEM, SMEM, SMEM, big, lanes(lags.shape[0])] + [states] * 8 + [ends_at] * (1 + len(recv))
            + [lanes(PARAM_ROWS), lanes(4 * MODES), lanes(n + HALO), big, big, big, self.whole(*normed.shape)]
            + [units(0), units(1), units(0)] + [self.order(), normed_at[0][0], normed_at[1][0], self.pair()[0]] * last,
            [*normed_at, params_at] + (self.parts() if last else [self.pair()]),
            [pltpu.VMEM((ms, LANES), F32)] * 2
            + [pltpu.VMEM((n, LANES), F32), pltpu.VMEM((n + HALO, 3 * LANES), BF16), pltpu.VMEM((3 * LANES, w), BF16)]
            + [pltpu.VMEM((2 * self.channels, w), BF16)] * last,
            10**9,
            True,
            count,
        )(
            core, keeps, masks, near, lags, *q, *state, *d, ends, *recv, params, tables, key, value, shifted, grad_query,
            normed, wkv, wkv, wqo, *([order, *before] if last else []),
        )


def lanes_from(rows):
    return pl.BlockSpec((rows, LANES), lambda l: (0, l))


def tail_kernel(steps, shard, core, keep, send, own, sib, sums, params_most, params_rest, bias, tail, rows_of):
    rows = steps * SEGS
    me, me_chip = core[0], core[1]
    total = [jnp.zeros((1, keep.shape[1]), F32)] * 2

    def more(total, grad, x):
        xhat, _ = normalize(x)
        return [t + jnp.sum(v, axis=0, keepdims=True) for t, v in zip(total, (grad * xhat, grad))]

    for r in range(0, rows, LN_TILE):
        at = pl.ds(r, LN_TILE)
        total = more(total, keep[at, :], own[at, :].astype(F32))
        total = more(total, send[at, :], sib[at, :].astype(F32))
    edge = pl.ds(rows, HALO)
    total = more(total, send[edge, :], chunk_of(own, sib, me, 1, edge))
    features = jnp.concatenate([*total, sums[...]], axis=0).astype(BF16)
    params = jnp.concatenate([params_most[...], params_rest[...]], axis=1).astype(BF16)
    chips, deep = tail.shape[0], tail.shape[1]
    rows_of[...] = jnp.zeros_like(rows_of)

    def columns(x, first):
        width = x.shape[1]
        i = lax.broadcasted_iota(jnp.int32, (width, LANES), 0)
        j = lax.broadcasted_iota(jnp.int32, (width, LANES), 1)
        pick = jnp.where(jnp.logical_and(i == first + j, j < shard), 1.0, 0.0).astype(BF16)
        return dot_nn(x, pick)

    for k in range(chips):
        z = lax.rem(me_chip - k + chips, chips)
        rows_of[pl.ds(0, PARAM_ROWS), :] = columns(params, z * shard)
        rows_of[pl.ds(PARAM_ROWS, 6), :] = columns(features, (2 * z + me) * shard)
        rows_of[pl.ds(PARAM_ROWS + 6, 2), :] = columns(features, (2 * z + 1 - me) * shard)[0:2]
        rows_of[pl.ds(PARAM_ROWS + 8, bias.shape[1]), :] = bias[k]
        for i in range(tail.shape[2] // LANES):
            tail[k, :, pl.ds(i * LANES, LANES)] = rows_of[pl.ds(i * deep, deep), :].astype(BF16)


def tail_of(core, keep, send, own, sib, sums, params_most, params_rest, bias, shard):
    width = keep.shape[1]
    across = width // LANES
    used = PARAM_ROWS + 8 + bias.shape[1]
    deep = -(-used // (across * 16)) * 16
    vmem = pl.BlockSpec(memory_space=pltpu.VMEM)
    return pl.pallas_call(
        functools.partial(tail_kernel, keep.shape[0] // SEGS, shard),
        in_specs=[SMEM] + [vmem] * 8,
        out_shape=jax.ShapeDtypeStruct((bias.shape[0], deep, width), BF16),
        scratch_shapes=[pltpu.VMEM((across * deep, LANES), F32)],
        compiler_params=pltpu.CompilerParams(vmem_limit_bytes=VMEM_LIMIT),
        cost_estimate=pl.CostEstimate(flops=10**6, bytes_accessed=10**4, transcendentals=0),
        name="tail_of",
    )(core, keep, send, own, sib, sums, params_most, params_rest, bias)


def finish_kernel(steps, core, keep, from_sib, edge, own, grad_residual, gain, out, total):
    rows = steps * SEGS
    total[...] = keep[...] + from_sib[pl.ds(0, rows), :]
    for b in range(1, TAPS):
        total[pl.ds((steps - b) * SEGS + SEGS - 1, 1), :] += edge[pl.ds(HALO - b, 1), :]
    first = pl.multiple_of(core[0] * rows, rows)
    for r in range(0, rows, LN_TILE):
        at = pl.ds(r, LN_TILE)
        xhat, scale = normalize(own[at, :].astype(F32))
        res = grad_residual[pl.ds(first + r, LN_TILE), :]
        out[at, :] = (res + normalize_back(total[at, :], gain[...], xhat, scale)).astype(BF16)


def finish(core, keep, from_sib, edge, own, grad_residual, gain):
    rows, width = keep.shape
    vmem = pl.BlockSpec(memory_space=pltpu.VMEM)
    return pl.pallas_call(
        functools.partial(finish_kernel, rows // SEGS),
        in_specs=[SMEM] + [vmem] * 6,
        out_shape=jax.ShapeDtypeStruct((rows, width), BF16),
        scratch_shapes=[pltpu.VMEM((rows, width), F32)],
        compiler_params=pltpu.CompilerParams(vmem_limit_bytes=VMEM_LIMIT),
        cost_estimate=pl.CostEstimate(flops=10**6, bytes_accessed=10**4, transcendentals=0),
        name="finish",
    )(core, keep, from_sib, edge, own, grad_residual, gain)


def feed_forward_kernel(reads, writes, first, n_arrays, n_outs, core, bias, lines, *refs):
    n_state = 6 if first else 5
    state, arrays, refs = refs[:n_state], refs[n_state : n_state + n_arrays], refs[n_state + n_arrays :]
    n_kept = 6 if first else 3
    kept, grad_bias, outs, refs = refs[:n_kept], refs[n_kept], refs[n_kept + 1 : n_kept + 1 + n_outs], refs[n_kept + 1 + n_outs :]
    held, refs = refs[:n_state], refs[n_state:]
    branch, grad_x, refs = refs[:2], refs[2], refs[3:]
    if first:
        own, sib, mixed_own, mixed_sib, c_own, c_sib = held
        residual, xs, cs, refs = *refs[:3], refs[3:]
    else:
        *branch_in, grad_in, xs, cs = held
    acts, backs, weights, grads, state_sems, read_sems, kept_sems, write_sems = refs
    me = core[0]
    half = xs.shape[0] // 2
    n_sets, units = bias.shape
    tiles = 2 * half // TILE

    def place(buffer, s, which, row, n):
        return buffer.at[which, pl.ds(s * units + row, n), :]

    def taken(i):
        return pltpu.make_async_copy(state[i], held[i], state_sems.at[i])

    def incoming(s, i):
        array, at, which, row, n = reads[s][i]
        return pltpu.make_async_copy(
            arrays[array].at[pl.ds(at, n), :], place(weights, s, which, row, n), read_sems.at[s, i]
        )

    def outgoing(s, i):
        array, slot, at, which, row, n = writes[s][i]
        return pltpu.make_async_copy(
            place(grads, s, which, row, n), outs[array].at[slot, pl.ds(at, n), :], write_sems.at[s, i]
        )

    def leaving(what, r, to=0):
        at = pl.ds(r * TILE, TILE)
        if what == 0:
            rows = pl.ds(r * TILE % half, TILE)
            return pltpu.make_async_copy(branch[r * TILE // half].at[rows, :], kept[to].at[rows, :], kept_sems.at[0, r])
        if what == 1:
            return pltpu.make_async_copy(grad_x.at[at, :], kept[2].at[at, :], kept_sems.at[1, r])
        return pltpu.make_async_copy((residual, xs, cs)[r], kept[3 + r], kept_sems.at[2, r])

    for i in range(n_state):
        taken(i).start()
    for s in range(n_sets):
        for i in range(len(reads[s])):
            incoming(s, i).start()
    for i in range(n_state):
        taken(i).wait()
    for c in range(2 if first else 0):
        for r in range(0, half, LN_TILE):
            at, part = pl.ds(c * half + r, LN_TILE), pl.ds(r, LN_TILE)
            v = chunk_of(own, sib, me, c, part) + mixed_own[at, :].astype(F32) + mixed_sib[at, :].astype(F32)
            v = v + lines[pl.ds(0, 1), :]
            residual[at, :] = v
            xhat, _ = normalize(v)
            xs[at, :] = (xhat * lines[pl.ds(1, 1), :] + lines[pl.ds(2, 1), :]).astype(BF16)
            cs[at, :] = chunk_of(c_own, c_sib, me, c, part).astype(BF16)
    for i in range(3 if first else 0):
        leaving(2, i).start()
    for s in range(n_sets):
        for i in range(len(reads[s])):
            incoming(s, i).wait()
    total = [jnp.zeros((1, units), F32)] * n_sets
    for r in range(0, 2 * half, TILE):
        at = pl.ds(r, TILE)
        c, place_of = r // half, pl.ds(r % half, TILE)
        for s in range(n_sets):
            mine = pl.ds(s * units, units)
            v = dot_nt(xs[at, :], weights[0, mine, :]) + bias[pl.ds(s, 1), :]
            square = v * v
            th = jnp.tanh(v * (0.79788456 + 0.79788456 * 0.044715 * square))
            half_up = 0.5 + 0.5 * th
            slope = half_up + v * (0.5 - 0.5 * th * th) * (0.79788456 + 0.79788456 * 3.0 * 0.044715 * square)
            back = dot_nt(cs[at, :], weights[1, mine, :]) * slope
            acts[at, mine] = (v * half_up).astype(BF16)
            low = back.astype(BF16)
            backs[at, mine] = low
            total[s] = total[s] + jnp.sum(low.astype(F32), axis=0, keepdims=True)
        out = dot_nn(acts[at, :], weights[1])
        grad = dot_nn(backs[at, :], weights[0])
        grad_x[at, :] = (grad if first else grad_in[at, :] + grad).astype(grad_x.dtype)
        leaving(1, r // TILE).start()
        if not first:
            out = out + jnp.where(me == c, branch_in[0][place_of, :], branch_in[1][place_of, :])
        branch[c][place_of, :] = out

        @pl.when(me == c)
        def _():
            leaving(0, r // TILE, 0).start()

        @pl.when(me != c)
        def _():
            leaving(0, r // TILE, 1).start()

    for s in range(n_sets):
        mine = pl.ds(s * units, units)
        grad_bias[pl.ds(s, 1), :] = total[s]
        for which, (left, right) in enumerate(((backs, xs), (acts, cs))):
            grads[which, mine, :] = dot_tn(left[:, mine], right[...]).astype(BF16)
            for i in range(len(writes[s])):
                if writes[s][i][3] == which:
                    outgoing(s, i).start()
    for r in range(tiles):
        leaving(0, r).wait()
        leaving(1, r).wait()
    for i in range(3 if first else 0):
        leaving(2, i).wait()
    for s in range(n_sets):
        for i in range(len(writes[s])):
            outgoing(s, i).wait()


def feed_forward(core, bias, lines, state, arrays, reads, out_shapes, writes, final):
    first = len(state) > 5
    width = state[2].shape[1]
    rows = state[4].shape[0] * 2 if first else state[2].shape[0]
    n_sets, units = bias.shape
    full, low = ((rows, width), F32), ((rows, width), BF16)
    part = ((rows // 2, width), F32)
    kept = [part, part, low if final else full] + [full, low, low] * first
    vmem, hbm = pl.BlockSpec(memory_space=pltpu.VMEM), pl.BlockSpec(memory_space=pl.ANY)
    shapes = [jax.ShapeDtypeStruct(*x) for x in kept]
    buffers = [pltpu.VMEM(x.shape, x.dtype) for x in state]
    buffers += [pltpu.VMEM(*x) for x in kept]
    out = pl.pallas_call(
        functools.partial(feed_forward_kernel, reads, writes, first, len(arrays), len(out_shapes)),
        in_specs=[SMEM, vmem, vmem] + [hbm] * (len(state) + len(arrays)),
        out_specs=[hbm] * len(kept) + [vmem] + [hbm] * len(out_shapes),
        out_shape=shapes + [jax.ShapeDtypeStruct(bias.shape, F32)]
        + [jax.ShapeDtypeStruct((n, rows_of, width), BF16) for n, rows_of in out_shapes],
        scratch_shapes=buffers
        + [pltpu.VMEM((rows, n_sets * units), BF16)] * 2 + [pltpu.VMEM((2, n_sets * units, width), BF16)] * 2
        + [
            pltpu.SemaphoreType.DMA((len(state),)),
            pltpu.SemaphoreType.DMA((n_sets, max(map(len, reads)))),
            pltpu.SemaphoreType.DMA((3, max(rows // TILE, 3))),
            pltpu.SemaphoreType.DMA((n_sets, max(map(len, writes)))),
        ],
        compiler_params=pltpu.CompilerParams(vmem_limit_bytes=VMEM_LIMIT),
        cost_estimate=pl.CostEstimate(flops=10**6, bytes_accessed=10**4, transcendentals=0),
        name="feed_forward" if first else "feed_forward_more",
    )(core, bias, lines, *state, *arrays)
    return out[: len(kept) + 1], out[len(kept) + 1 :]


def local(
    groups, chips,
    hidden_in, mix_gain, mix_shift, w_query, bias_query, w_key, bias_key, w_value, bias_value, shift_taps,
    log_step, log_decay, frequency, out_real, out_imag, skip_gain, w_out, bias_out, mlp_gain, mlp_shift,
    w_up, bias_up, w_down, bias_down, cotangent, seq_blocks,
):
    rows, width = hidden_in.shape
    shard, shard_units = w_query.shape[1], w_up.shape[1]
    chans, channels = 2 * chips, chips * shard
    cut, unit_cut = shard // groups, shard_units // groups
    steps = rows // SEGS
    me_group, me_chan = lax.axis_index("group"), lax.axis_index("chan")
    me_chip, me_core = me_chan // 2, me_chan % 2
    same_core = [[2 * z + k for z in range(chips)] for k in range(2)]
    square = groups == 4

    def swap_z(x):
        return lax.all_to_all(x, "chan", 0, 0, axis_index_groups=same_core, tiled=True)

    def group_swap(x, bits):
        return lax.ppermute(x, "group", [(i, i ^ bits) for i in range(groups)])

    def sibling(x):
        return lax.ppermute(x, "chan", [(i, i ^ 1) for i in range(chans)])

    def chip_shift(x, by):
        pairs = [(i, i + 2 * by) for i in range(chans) if 0 <= i + 2 * by < chans]
        return lax.ppermute(x, "chan", pairs)

    def chip_turn(x, by):
        return lax.ppermute(x, "chan", [(i, (i + 2 * by) % chans) for i in range(chans)])

    def gather_z(x):
        return jnp.concatenate([x] + [chip_turn(x, by) for by in range(1, chips)])

    def gather_group(x):
        return [x] + [group_swap(x, r) for r in range(1, groups)]

    def add(*xs):
        return sum(x.astype(F32) for x in xs).astype(BF16)

    def fold_z(parts):
        return add(parts[0], *(chip_turn(p, -by) for by, p in enumerate(parts) if by))

    def fold_group(parts):
        return add(parts[0], *(group_swap(p, r) for r, p in enumerate(parts) if r))

    def pieces(x, count):
        n = x.shape[0] // count
        return [x[i * n : (i + 1) * n] for i in range(count)]

    def by_index(parts):
        out = []
        for g in range(groups):
            x = parts[0]
            for r in range(1, groups):
                x = jnp.where(me_group == g ^ r, parts[r], x)
            out.append(x)
        return jnp.stack(out)

    def first_round(a):
        return (group_swap(a, 1), group_swap(a, 2)) if square else tuple(gather_group(a)[1:])

    def second_round(one):
        n = one[0].shape[0] // 2
        return (group_swap(one[1][:n], 1), group_swap(one[0][n:], 2)) if square else ()

    def fold_first(send_a, send_b):
        return [group_swap(x, 1) for x in send_a], [group_swap(x, 2) for x in send_b]

    def fold_second(one, ay, bx):
        return group_swap(add(ay, one[0][1]), 2), group_swap(add(bx, one[1][1]), 1)

    def fold_end(one, two, a0, b0):
        return add(a0, one[0][0], two[0]), add(b0, one[1][0], two[1])

    def fence(*xs):
        return lax.optimization_barrier(xs)

    def share(x):
        return lax.dynamic_index_in_dim(x.reshape(groups, -1, width), me_group, 0, keepdims=False)

    def to_steps(x):
        return x.reshape(SEGS, steps, width).transpose(1, 0, 2).reshape(rows, width)

    def to_rows(x):
        return x.reshape(steps, SEGS, width).transpose(1, 0, 2).reshape(rows, width)

    first = seq_blocks[0, 0]
    second = first + seq_blocks[0, 1]

    def keep(block):
        starts = (block == 0) | (block == first) | (block == second)
        return jnp.where(starts, 0.0, 1.0).astype(F32)

    blocks = 4 * me_chip + jnp.arange(4)
    keeps = keep(blocks).reshape(2, 2)

    def two_shares(a, b):
        return jnp.concatenate([share(a), share(b)])

    turns = (me_chip - jnp.arange(chips)) % chips
    flips = me_group ^ jnp.arange(groups)
    place = flips[None, None, :, None] * chips + turns[None, :, None, None]
    place = (place * 2 + jnp.arange(2)[:, None, None, None]) * cut + jnp.arange(cut)
    order = (place.reshape(-1, 1) == jnp.arange(2 * channels)).astype(BF16)
    z_turn = (turns[:, None] == jnp.arange(chips)).astype(F32)
    g_flip = (flips[:, None] == jnp.arange(groups)).astype(F32)
    exact = lax.Precision.HIGHEST

    core = jnp.stack([me_core, me_chip])
    line = lambda x: x.reshape(1, width)
    kv_z = gather_z(two_shares(w_key.T, w_value.T))
    edge = lax.ppermute(hidden_in[rows - HALO :], "chan", [(2 * z + 1, 2 * z + 3) for z in range(chips - 1)])
    own = jnp.concatenate([to_steps(hidden_in), edge])
    kv_z, own, w_query, w_out, w_up, w_down, cotangent, log_decay, frequency, out_real, out_imag = fence(
        kv_z, own, w_query, w_out, w_up, w_down, cotangent, log_decay, frequency, out_real, out_imag
    )

    mixed_kv = gather_group(kv_z)
    small = jnp.concatenate(
        [
            log_decay.T, frequency.T, out_real.T, out_imag.T, shift_taps.T,
            jnp.stack([log_step, skip_gain, bias_query, bias_key, bias_value]),
            bias_up.reshape(shard_units // shard, shard),
        ]
    )
    small = swap_z(jnp.broadcast_to(small, (chips,) + small.shape))
    sib = sibling(own)
    qo_z = gather_z(two_shares(w_query.T, w_out))
    params = jnp.moveaxis(small[:, :PARAM_ROWS], 0, 1).reshape(PARAM_ROWS, channels)
    units_bias = small[:, PARAM_ROWS:].reshape(chips, groups, unit_cut)
    units_bias = jnp.einsum("rg,zgu->rzu", g_flip, units_bias, precision=exact).reshape(groups, -1)
    ff_z = two_shares(w_up.T, w_down)
    ff_z = jnp.broadcast_to(ff_z, (chips,) + ff_z.shape)
    mixed_kv, sib, qo_z, params, units_bias, order, keeps, ff_z, cotangent = fence(
        mixed_kv, sib, qo_z, params, units_bias, order, keeps, ff_z, cotangent
    )

    ff_z = swap_z(ff_z)
    mixed_qo = gather_group(qo_z)
    mixer = Mixer(rows, channels, width, groups)
    normed, wkv, tables, kern, key, value, prod, shifted, er, ei, dr, di, ends, chip = mixer.before(
        core, keeps, own, sib, line(mix_gain), line(mix_shift), order, mixed_kv, params
    )
    chip, ends, cotangent, mixed_qo, first, second = fence(chip, ends, cotangent, mixed_qo, first, second)

    recv = [chip_shift(chip, by) for by in range(1, chips)]
    wqo, query, near = mixer.near(normed, prod, mixed_qo, order, params, kern)
    cot = to_steps(cotangent)
    around = me_chip + jnp.stack([-jnp.arange(chips), jnp.arange(chips)])
    masks = jnp.prod(keep(4 * around[..., None] + jnp.arange(4)), axis=-1)
    recv, near, ff_z, cot = fence(recv, near, ff_z, cot)

    if not square:
        ff_z = jnp.moveaxis(ff_z.reshape(chips, 2, unit_cut, width), 1, 0)
    ff_z = ff_z.reshape(-1, width)
    ff_one = first_round(ff_z)
    cot_sib = sibling(cot)
    conv, core_low, state_r, state_i, mixed = mixer.conv(
        keeps, masks, near, query, er, ei, ends, recv, wqo, tables
    )
    mixed, cot_sib, ff_one = fence(mixed, cot_sib, ff_one)

    mixed_sib = sibling(mixed)
    ff_two = second_round(ff_one)
    (mixed_sib,) = fence(mixed_sib)

    units = chips * unit_cut
    if square:
        arrays = [ff_z, *ff_one]
        near_half = chips // 2

        def rows_of(z, which):
            return (z % near_half * 2 + which) * unit_cut

        every = [(z, which) for z in range(chips) for which in range(2)]
        reads = [
            [(s, (z * 2 + w) * unit_cut, w, z * unit_cut, unit_cut) for z, w in every] for s in range(3)
        ] + [[(z // near_half, rows_of(z, w), w, z * unit_cut, unit_cut) for z, w in every]]
        to = ((0, 3), (2, 4), (1, 5), (0, 1))
        slots = ((0, 0),) * 4
        writes = [
            [
                (to[s][z // near_half], slots[s][z // near_half], rows_of(z, w), w, z * unit_cut, unit_cut)
                for z, w in every
            ]
            for s in range(4)
        ]
        out_shapes = [(1, units)] * 2 + [(1, units)] + [(1, units)] * 2 + [(1, units)]
    else:
        arrays = [ff_z, *ff_one]
        reads = [[(s, w * units, w, 0, units) for w in range(2)] for s in range(groups)]
        writes = [[(s, 0, w * units, w, 0, units) for w in range(2)] for s in range(groups)]
        out_shapes = [(1, 2 * units)] * groups
    lines = jnp.stack([bias_out, mlp_gain, mlp_shift])
    state = (own, sib, mixed, mixed_sib, cot, cot_sib)
    n_first = 3 if square else groups
    (*branch, grad_two, residual, xs, cs, grad_units_bias), grad_ff = feed_forward(
        core, units_bias[:n_first], lines, state, arrays[:n_first], reads[:n_first], out_shapes, writes[:n_first], not square
    )
    if square:
        branch, grad_two, xs, cs, ff_two = fence(branch, grad_two, xs, cs, ff_two)
        (*branch, grad_two, more_bias), grad_diagonal = feed_forward(
            core, units_bias[3:], lines, (*branch, grad_two, xs, cs), ff_two, reads[3:], [(1, units)] * 2, writes[3:], True
        )
        grad_units_bias = jnp.concatenate([grad_units_bias, more_bias])

    branch_own = branch[0]
    grad_two_sib, branch_sib = sibling(grad_two), sibling(branch[1])
    if square:
        fold_one = fold_first((grad_ff[2][0], grad_diagonal[0][0]), (grad_ff[5][0], grad_diagonal[1][0]))
    else:
        fold_one = ()
    after = mixer.after(
        core, keeps, residual, grad_two, grad_two_sib, cot, cot_sib, line(mlp_gain), order, wqo, normed, query, conv,
        core_low, tables,
    )
    grad_residual, g, grad_query, *qsums, ends, chip, sums = after[:10]
    grad_qo = after[10:]
    chip, grad_qo, branch_own, branch_sib, ends, g = fence(chip, grad_qo, branch_own, branch_sib, ends, g)

    recv = [chip_shift(chip, -by) for by in range(1, chips)]
    near, lags = mixer.near_back(g, prod, params, kern)
    recv, near, lags, fold_one, grad_qo = fence(recv, near, lags, fold_one, grad_qo)

    bias_rows = grad_units_bias.reshape(groups, chips, unit_cut)
    bias_rows = jnp.einsum("kz,rg,rzu->kgu", z_turn, g_flip, bias_rows, precision=exact)
    bias_rows = jnp.pad(bias_rows.reshape(chips, -1, shard), ((0, 0), (0, 0), (0, LANES - shard)))
    used = PARAM_ROWS + 8 + bias_rows.shape[1]

    fold_two = fold_second(fold_one, grad_ff[1][0], grad_ff[4][0]) if square else ()
    blocks = channels // LANES
    grads_of = lambda base, count, before: mixer.grads(
        base, count, core, keeps, masks, near, lags, qsums, (state_r, state_i), (dr, di), ends, recv, params, tables, key,
        value, shifted, grad_query, normed, wkv, wqo, order, before,
    )
    grad_keep, grad_send, params_most, grad_w = grads_of(0, 1, None)
    fold_two, grad_keep, grad_w = fence(fold_two, grad_keep, grad_w)

    if square:
        ff = jnp.concatenate(fold_end(fold_one, fold_two, grad_ff[0][0], grad_ff[3][0]))
    else:
        ff = fold_group([x[0] for x in grad_ff]).reshape(2, chips, unit_cut, width)
        ff = jnp.moveaxis(ff, 1, 0)
    ff = ff.reshape(chips, 2 * unit_cut, width)
    ff = [lax.dynamic_index_in_dim(ff, (me_chip + k) % chips, 0, keepdims=False) for k in range(chips)]
    ff_odd = [chip_turn(ff[k], k) for k in range(1, chips, 2)]
    grad_keep, grad_send, params_rest, *grad_kv = grads_of(1, blocks - 1, (grad_keep, grad_send, grad_w))
    grad_kv, grad_keep, grad_send, params_rest, ff, ff_odd, grad_qo = fence(
        grad_kv, grad_keep, grad_send, params_rest, ff, ff_odd, grad_qo
    )

    kv = fold_group(grad_kv)
    ff = add(ff[0], *ff_odd, *(chip_turn(ff[k], k) for k in range(2, chips, 2)))
    from_sib = sibling(grad_send)
    from_sib, params_rest, bias_rows, grad_qo = fence(from_sib, params_rest, bias_rows, grad_qo)
    tail = tail_of(core, grad_keep, grad_send, own, sib, sums, params_most, params_rest, bias_rows, shard)
    edge = grad_send[rows:] + from_sib[rows:]
    edge = lax.ppermute(edge, "chan", [(2 * z + 3, 2 * z + 1) for z in range(chips - 1)])
    kv, tail, ff, from_sib, edge = fence(kv, tail, ff, from_sib, edge)

    qo = fold_group(grad_qo)
    kv = fold_z([jnp.concatenate(p) for p in zip(pieces(kv, chips), tail)])
    ff = gather_group(ff)
    mine = lax.dynamic_slice_in_dim(residual, me_core * rows, rows, axis=0)
    output = to_rows((mine + branch_own + branch_sib + bias_down).astype(BF16))
    grad_input = to_rows(finish(core, grad_keep, from_sib, edge, own, grad_residual, line(mix_gain)))
    qo = fold_z(pieces(qo, chips))
    kv, qo, output, grad_input, ff = fence(kv, qo, output, grad_input, ff)

    kv = gather_group(kv)
    qo = gather_group(qo)
    grad_wf = by_index(ff).reshape(groups, 2, unit_cut, width)
    grad_wf = jnp.moveaxis(grad_wf, 1, 0).reshape(2, shard_units, width).astype(F32)

    def halves(parts):
        x = by_index(parts).reshape(groups, 2, cut, width)
        return jnp.moveaxis(x, 1, 0).reshape(2, shard, width).astype(F32)

    (grad_wk, grad_wv), (grad_wq, grad_wo) = halves([x[: 2 * cut] for x in kv]), halves(qo)
    tail = sum(x[2 * cut :].astype(F32) for x in kv)
    tail = tail.reshape(-1, width // LANES, LANES).transpose(1, 0, 2).reshape(-1, LANES)[:used, :shard]
    modes = [tail[i * MODES : (i + 1) * MODES].T for i in range(4)]
    biases = tail[BIAS_ROW:PARAM_ROWS]
    feat_part = tail[PARAM_ROWS : PARAM_ROWS + 6]
    first_two = feat_part[:2] + sibling(tail[PARAM_ROWS + 6 : PARAM_ROWS + 8])
    sum_bias_up = tail[PARAM_ROWS + 8 :].reshape(shard_units)
    return (
        output,
        grad_input,
        first_two[0],
        first_two[1],
        grad_wq.T,
        biases[0],
        grad_wk.T,
        biases[1],
        grad_wv.T,
        biases[2],
        tail[TAP_ROW : TAP_ROW + TAPS].T,
        tail[STEP_ROW],
        modes[0],
        modes[1],
        modes[2],
        modes[3],
        tail[SKIP_ROW],
        grad_wo,
        feat_part[2],
        feat_part[3],
        feat_part[4],
        grad_wf[0].T,
        sum_bias_up,
        grad_wf[1],
        feat_part[5],
    )


def solution(mesh):
    rows = P(("group", "chan"), None)
    columns, channels, vector, copied = P(None, "chan"), P("chan", None), P("chan"), P()
    return jax.shard_map(
        functools.partial(local, mesh.shape["group"], mesh.shape["chan"] // 2),
        mesh=mesh,
        in_specs=(
            rows, copied, copied, columns, vector, columns, vector, columns, vector, channels,
            vector, channels, channels, channels, channels, vector, channels, copied, copied, copied,
            columns, vector, channels, copied, rows, P("group", None),
        ),
        out_specs=(
            rows, rows, vector, vector, columns, vector, columns, vector, columns, vector,
            channels, vector, channels, channels, channels, channels, vector, channels, vector, vector,
            vector, columns, vector, channels, vector,
        ),
        check_vma=False,
    )
```
